32 devices in a mesh: dp: 16 (over z, x, core), ctx: 2 (over y).
Axes of the slice: x: 2, y: 2, z: 4, core: 2. Of those that a mesh axis runs over, the one named last changes fastest.
Arguments:
- query_vecs: bfloat16 [16, 256, 1024], P('dp', 'ctx'), may hold values from -12 to 12, as said below
- key_vecs: bfloat16 [16, 256, 1024], P('dp', 'ctx'), may hold values from -12 to 12
- value_vecs: bfloat16 [16, 256, 1024], P('dp', 'ctx'), may hold values from -6 to 6
- residual: bfloat16 [16, 256, 2048], P('dp', 'ctx'), may hold values from -45 to 45
- w_out: bfloat16 [1024, 2048], P('dp'), may hold values from -0.75 to 0.75
- norm_gain: float32 [2048], replicated, may hold values from 0.25 to 1.75
- w_gate_up: bfloat16 [16, 2, 2048, 1408], P('dp', None, None, 'ctx'), may hold values from -0.125 to 0.125
- w_down: bfloat16 [16, 1408, 2048], P('dp', 'ctx'), may hold values from -0.15625 to 0.15625
- expert_ids: int32 [16, 256, 6], P('dp', 'ctx'), may hold values from 0 to 15, as said below
- route_gates: float32 [16, 256, 6], P('dp', 'ctx'), may hold values from 0.1 to 0.9
- capacity: int32 [16, 2, 2], P('dp', 'ctx'), may hold values from 12 to 24, as said below
- expert_owner: int32 [16], replicated, may hold values from 0 to 15, each once
Outputs:
- attn_proj: bfloat16 [16, 256, 2048], P('dp', 'ctx')
- expert_sum: bfloat16 [16, 256, 2048], P('dp', 'ctx')
The draws below stay inside these ranges and needn't reach their ends.
Inputs may be any that keep to these rules, and one draw needn't show every extreme that they name: `query_vecs`: q and k are drawn together. `expert_ids`: each position names 6 different experts; in each aligned block of 128 positions, experts 0 to 1 are each named by at least 24 positions. In each block some expert has capacity 24. `expert_owner`: each index of dp holds one expert.
All inputs are finite; a program needn't handle non-finite values.
Results may differ from the reference program's by a relative error of at most 0.019.
Values may be sent and summed in bfloat16 or wider, within the bound.
No kernel may reach another device: no remote copies, remote signals or barrier semaphores. Data moves between devices by JAX's collectives and lax.ppermute only.
A program may use at most 128 MiB of HBM per device.

```python
import jax
import jax.numpy as jnp
from jax import lax

D = 2048
HEADS = 8
HD = 128
FF = 1408
PICKS_PER_TOKEN = 6
PASS_SPECIALISTS = 2
TOK_DEV = 128
SPECIALIST_TOTAL = 16
CAP = 24
TOKEN_SPAN = 256
TEXT_COUNT = 16


def attention_pair(key):
    base = jax.random.fold_in(key, 4101)
    query_seed, key_seed = jax.random.split(base, 2)
    shape = (TEXT_COUNT, TOKEN_SPAN, HEADS, HD)
    queries = 1.3 * jnp.clip(jax.random.normal(query_seed, shape, jnp.float32), -5.0, 5.0)
    keys_out = jnp.clip(jax.random.normal(key_seed, shape, jnp.float32), -5.0, 5.0)
    return (queries.reshape(TEXT_COUNT, TOKEN_SPAN, HEADS * HD), keys_out.reshape(TEXT_COUNT, TOKEN_SPAN, HEADS * HD))


def draw_query_vecs(key, part):
    return attention_pair(key)[0].astype(jnp.bfloat16)


def draw_key_vecs(key, part):
    return attention_pair(key)[1].astype(jnp.bfloat16)


def draw_residual(key, part):
    base = jax.random.fold_in(key, 5303)
    noise_seed, row_seed, column_seed = jax.random.split(base, 3)
    shape = (TEXT_COUNT, TOKEN_SPAN, D)
    row_scale = jnp.exp(jax.random.uniform(row_seed, (TEXT_COUNT, TOKEN_SPAN, 1), jnp.float32, jnp.log(0.3), jnp.log(3.0)))
    column_scale = jnp.exp(jax.random.uniform(column_seed, (1, 1, D), jnp.float32, jnp.log(0.3), jnp.log(3.0)))
    values = jnp.clip(jax.random.normal(noise_seed, shape, jnp.float32), -5.0, 5.0) * row_scale * column_scale
    return values.astype(jnp.bfloat16)


def draw_expert_ids(key, part):
    base = jax.random.fold_in(key, 7207)
    score_seed, coin_seed, order_seed = jax.random.split(base, 3)
    gating_logits = jax.random.randint(score_seed, (TEXT_COUNT, TOKEN_SPAN, SPECIALIST_TOTAL), 0, 2 ** 20) * SPECIALIST_TOTAL + jnp.arange(SPECIALIST_TOTAL, dtype=jnp.int32)
    coins = jax.random.randint(coin_seed, (TEXT_COUNT, TOKEN_SPAN, PASS_SPECIALISTS), 0, 2)
    blocks = TEXT_COUNT * TOKEN_SPAN // TOK_DEV
    order = jax.random.randint(order_seed, (blocks, PASS_SPECIALISTS, TOK_DEV), 0, 2 ** 16) * TOK_DEV + jnp.arange(TOK_DEV, dtype=jnp.int32)
    places = jnp.argsort(jnp.argsort(order, axis=-1), axis=-1)
    forced = jnp.transpose(places < CAP, (0, 2, 1)).reshape(TEXT_COUNT, TOKEN_SPAN, PASS_SPECIALISTS)
    popular_specialists = (forced | (coins == 1)).astype(jnp.int32)
    added_preference = jnp.concatenate([popular_specialists * 2 ** 30, jnp.zeros((TEXT_COUNT, TOKEN_SPAN, SPECIALIST_TOTAL - PASS_SPECIALISTS), jnp.int32)], axis=-1)
    ignored_specialists, selected_specialists = lax.top_k(gating_logits + added_preference, PICKS_PER_TOKEN)
    return selected_specialists.astype(jnp.int32)


def draw_capacity(key, part):
    block_count = TOKEN_SPAN // TOK_DEV
    values = jax.random.randint(jax.random.fold_in(key, 9001), (TEXT_COUNT, block_count, PASS_SPECIALISTS), CAP // 2, CAP + 1)
    fullest = jax.random.randint(jax.random.fold_in(key, 9002), (TEXT_COUNT, block_count, 1), 0, PASS_SPECIALISTS)
    return jnp.where(jnp.arange(PASS_SPECIALISTS)[None, None, :] == fullest, CAP, values).astype(jnp.int32)


def block_levels(key, extent, cuts, least, high):
    loudness = 1.0
    for dim, blocks in cuts:
        steps = jax.random.uniform(jax.random.fold_in(jax.random.fold_in(key, 6), dim), (blocks,), jnp.float32, least / len(cuts), high / len(cuts))
        loudness = loudness * jnp.repeat(jnp.exp(steps), extent[dim] // blocks).reshape((-1,) + (1,) * (len(extent) - 1 - dim))
    return loudness


def centred(own_key, shape, width, limit, cuts=(), held_as=jnp.bfloat16):
    loudness = block_levels(own_key, shape, cuts, -0.22, 0.18) if cuts else 1.0
    result = jax.random.normal(own_key, shape, jnp.float32) * width * loudness
    return jnp.minimum(jnp.maximum(result, -limit), limit).astype(held_as)


def setup_inputs(seed: int = 0) -> dict:
    keys = jax.random.split(jax.random.key(seed), 13)
    query_vecs = draw_query_vecs(jax.random.fold_in(keys[12], 71), 0)
    key_vecs = draw_key_vecs(jax.random.fold_in(keys[12], 71), 0)
    value_vecs = centred(keys[2], (TEXT_COUNT, TOKEN_SPAN, HEADS * HD), 1.0, 6.0, ((0, 16), (1, 2)))
    residual = draw_residual(jax.random.fold_in(keys[12], 71), 0)
    w_out = centred(keys[4], (HEADS * HD, D), (HEADS * HD // 16) ** -0.5, 0.75, ((0, 16),))
    norm_gain = jnp.clip(1.0 + 0.15 * jax.random.normal(keys[5], (D,), jnp.float32), 0.25, 1.75)
    w_gate_up = centred(keys[6], (SPECIALIST_TOTAL, 2, D, FF), D ** -0.5, 0.125, ((0, 16), (3, 2)))
    w_down = centred(keys[7], (SPECIALIST_TOTAL, FF, D), FF ** -0.5, 0.15625, ((0, 16), (1, 2)))
    expert_ids = draw_expert_ids(jax.random.fold_in(keys[12], 71), 0)
    route_gates = jnp.clip(0.1 + 0.79999997 * jax.random.uniform(keys[9], (TEXT_COUNT, TOKEN_SPAN, PICKS_PER_TOKEN), jnp.float32) ** block_levels(keys[9], (TEXT_COUNT, TOKEN_SPAN, PICKS_PER_TOKEN), ((0, 16), (1, 2)), -0.2, 0.2), 0.1, 0.9)
    capacity = draw_capacity(jax.random.fold_in(keys[12], 71), 0)
    expert_owner = jax.random.permutation(keys[11], SPECIALIST_TOTAL).astype(jnp.int32)
    return dict(query_vecs=query_vecs, key_vecs=key_vecs, value_vecs=value_vecs, residual=residual, w_out=w_out, norm_gain=norm_gain, w_gate_up=w_gate_up, w_down=w_down, expert_ids=expert_ids, route_gates=route_gates, capacity=capacity, expert_owner=expert_owner)


EPSILON = 1e-06

def route_slots(expert_ids, route_gates, capacity, expert):
    matches = expert_ids == expert
    routed = jnp.any(matches, axis=1)
    gate_value = lax.optimization_barrier(jnp.sum(jnp.where(matches, route_gates, 0.0), axis=1))
    slot_rank = (jnp.cumsum(routed.astype(jnp.int32)) - 1).astype(jnp.int32)
    kept_mask = routed & (slot_rank < capacity[expert])
    return (slot_rank, kept_mask, gate_value)

def sequence_attention(tensors):
    query_part = tensors[0].astype(jnp.float32).reshape(TOKEN_SPAN, HEADS, HD)
    key_part = tensors[1].astype(jnp.float32).reshape(TOKEN_SPAN, HEADS, HD)
    value_part = tensors[2].astype(jnp.float32).reshape(TOKEN_SPAN, HEADS, HD)
    gating_logits = jnp.einsum('qhd,khd->hqk', query_part, key_part, precision=lax.Precision.HIGHEST) * HD ** (-0.5)
    position = jnp.arange(TOKEN_SPAN)
    visible = position[None, :] <= position[:, None]
    gating_logits = jnp.where(visible[None], gating_logits, -jnp.inf)
    row_top = lax.optimization_barrier(jnp.max(gating_logits, axis=-1, keepdims=True))
    weights = jnp.exp(gating_logits - row_top)
    row_total = lax.optimization_barrier(jnp.sum(weights, axis=-1))
    rounded = lax.optimization_barrier(weights.astype(jnp.bfloat16)).astype(jnp.float32)
    mixed = jnp.einsum('hqk,khd->qhd', rounded, value_part, precision=lax.Precision.HIGHEST)
    mixed = mixed / jnp.transpose(row_total)[:, :, None]
    return mixed.reshape(TOKEN_SPAN, HEADS * HD).astype(jnp.bfloat16)

def reference(query_vecs, key_vecs, value_vecs, residual, w_out, norm_gain, w_gate_up, w_down, expert_ids, route_gates, capacity, expert_owner):
    attended = lax.map(sequence_attention, (query_vecs, key_vecs, value_vecs))
    attn_proj = jnp.dot(attended.reshape(TEXT_COUNT * TOKEN_SPAN, HEADS * HD), w_out, preferred_element_type=jnp.float32).astype(jnp.bfloat16)
    combined = residual.reshape(TEXT_COUNT * TOKEN_SPAN, D).astype(jnp.float32) + attn_proj.astype(jnp.float32)
    normed = (combined * lax.rsqrt(lax.optimization_barrier(jnp.mean(combined * combined, axis=-1, keepdims=True)) + EPSILON) * norm_gain).astype(jnp.bfloat16)
    blocks = TEXT_COUNT * TOKEN_SPAN // TOK_DEV
    experts_in = [(w_gate_up[expert_owner[expert]], w_down[expert_owner[expert]]) for expert in range(PASS_SPECIALISTS)]
    slot_ids = jnp.arange(CAP)

    def block_output(tensors):
        normed_block, ids_block, gates_block, block_caps = tensors
        summed = jnp.zeros((TOK_DEV, D), jnp.float32)
        for expert in range(PASS_SPECIALISTS):
            slot_rank, kept_mask, gate_value = route_slots(ids_block, gates_block, block_caps, expert)
            select = ((slot_rank[None, :] == slot_ids[:, None]) & kept_mask[None, :]).astype(jnp.bfloat16)
            selected_specialists = jnp.dot(select, normed_block, preferred_element_type=jnp.float32).astype(jnp.bfloat16)
            gate_up, down_part = experts_in[expert]
            gate_proj = jnp.dot(selected_specialists, gate_up[0], preferred_element_type=jnp.float32)
            up_proj = jnp.dot(selected_specialists, gate_up[1], preferred_element_type=jnp.float32)
            hidden = (jax.nn.silu(gate_proj) * up_proj).astype(jnp.bfloat16)
            produced = jnp.dot(hidden, down_part, preferred_element_type=jnp.float32)
            picked = jnp.take(produced, jnp.clip(slot_rank, 0, CAP - 1), axis=0)
            summed = summed + jnp.where(kept_mask, gate_value, 0.0)[:, None] * picked
        return summed.astype(jnp.bfloat16)
    expert_sum = lax.map(block_output, (normed.reshape(blocks, TOK_DEV, D), expert_ids.reshape(blocks, TOK_DEV, PICKS_PER_TOKEN), route_gates.reshape(blocks, TOK_DEV, PICKS_PER_TOKEN), capacity.reshape(blocks, PASS_SPECIALISTS)))
    return (attn_proj.reshape(TEXT_COUNT, TOKEN_SPAN, D), expert_sum.reshape(TEXT_COUNT, TOKEN_SPAN, D))
```

```python
import jax
import jax.numpy as jnp
from jax import lax
from jax.sharding import PartitionSpec as P

HEADS = 8
HD = 128
PASS_SPECIALISTS = 2
CAP = 24


EPSILON = 1e-06
LOWEST = -1e30


def broadcast(array, axis, root):
    mine = lax.axis_index(axis) == root
    return lax.psum(jnp.where(mine, array, jnp.zeros_like(array)), axis)


def hop(array, axis, size, bit):
    return lax.ppermute(array, axis, [(i, i ^ bit) for i in range(size)])


def route_slots(expert_ids, route_gates, capacity, expert):
    matches = expert_ids == expert
    routed = jnp.any(matches, axis=1)
    gate_value = jnp.sum(jnp.where(matches, route_gates, 0.0), axis=1)
    slot_rank = jnp.cumsum(routed.astype(jnp.int32)) - 1
    kept_mask = routed & (slot_rank < capacity[expert])
    return (slot_rank, kept_mask, gate_value)


def attend(queries, key_block, value_block, visible):
    width = key_block.shape[0]
    token_count = queries.shape[0]
    query_heads = queries.reshape(token_count, HEADS, HD)
    key_heads = key_block.reshape(width, HEADS, HD)
    value_heads = value_block.reshape(width, HEADS, HD)
    gating_logits = jnp.einsum(
        "qhd,khd->qhk", query_heads, key_heads, preferred_element_type=jnp.float32
    ) * HD ** (-0.5)
    gating_logits = jnp.where(visible[:, None, :], gating_logits, -jnp.inf)
    row_top = jnp.max(gating_logits, axis=-1)
    weights = jnp.exp(gating_logits - row_top[:, :, None])
    denominator = jnp.sum(weights, axis=-1)
    weighted = jnp.einsum(
        "qhk,khd->qhd",
        weights.astype(jnp.bfloat16),
        value_heads,
        preferred_element_type=jnp.float32,
    )
    attended = (weighted / denominator[:, :, None]).astype(jnp.bfloat16)
    return attended.reshape(token_count, HEADS * HD)


def feed_forward(rows, gate_up, down_part):
    gate_proj = jnp.dot(rows, gate_up[0], preferred_element_type=jnp.float32)
    up_proj = jnp.dot(rows, gate_up[1], preferred_element_type=jnp.float32)
    hidden = (jax.nn.silu(gate_proj) * up_proj).astype(jnp.bfloat16)
    return jnp.dot(hidden, down_part, preferred_element_type=jnp.float32).astype(jnp.bfloat16)


def normalise(attn_proj, residual, norm_gain):
    combined = residual.astype(jnp.float32) + attn_proj.astype(jnp.float32)
    return (
        combined
        * lax.rsqrt(jnp.mean(combined * combined, axis=-1, keepdims=True) + EPSILON)
        * norm_gain
    ).astype(jnp.bfloat16)


def pick_rows(routing, normed):
    slot_ids = jnp.arange(CAP)
    select = [
        (slot_rank[None, :] == slot_ids[:, None]) & kept_mask[None, :]
        for slot_rank, kept_mask, _ in routing
    ]
    select = jnp.concatenate(select, axis=0).astype(jnp.bfloat16)
    chosen = jnp.dot(select, normed, preferred_element_type=jnp.float32).astype(jnp.bfloat16)
    return chosen.reshape(PASS_SPECIALISTS, CAP, normed.shape[1])


def combine_rows(routing, produced):
    slot_ids = jnp.arange(CAP)
    summed = 0.0
    for expert in range(PASS_SPECIALISTS):
        slot_rank, kept_mask, gate_value = routing[expert]
        place = ((slot_rank[:, None] == slot_ids[None, :]) & kept_mask[:, None]).astype(
            jnp.bfloat16
        )
        picked = jnp.dot(place, produced[expert], preferred_element_type=jnp.float32)
        summed = summed + gate_value[:, None] * picked
    return summed.astype(jnp.bfloat16)


def body_move_weights(
    query_vecs,
    key_vecs,
    value_vecs,
    residual,
    w_out,
    norm_gain,
    w_gate_up,
    w_down,
    expert_ids,
    route_gates,
    capacity,
    expert_owner,
):
    token_count = query_vecs.shape[1]
    weights_in = []
    for expert in range(PASS_SPECIALISTS):
        weights_in.append(
            (
                broadcast(w_gate_up[0], "dp", expert_owner[expert]),
                broadcast(w_down[0], "dp", expert_owner[expert]),
            )
        )
    keys = lax.all_gather(key_vecs[0], "ctx", axis=0, tiled=True)
    values = lax.all_gather(value_vecs[0], "ctx", axis=0, tiled=True)
    first_row = lax.axis_index("ctx") * token_count
    query_pos = first_row + jnp.arange(token_count)
    visible = jnp.arange(keys.shape[0])[None, :] <= query_pos[:, None]
    attended = attend(query_vecs[0], keys, values, visible)
    projected = jnp.dot(
        attended,
        lax.all_gather(w_out, "dp", axis=0, tiled=True),
        preferred_element_type=jnp.float32,
    )
    attn_proj = projected.astype(jnp.bfloat16)
    normed = normalise(attn_proj, residual[0], norm_gain)
    routing = [
        route_slots(expert_ids[0], route_gates[0], capacity[0, 0], expert)
        for expert in range(PASS_SPECIALISTS)
    ]
    chosen = pick_rows(routing, normed)
    routed_rows = lax.all_gather(jnp.swapaxes(chosen, 0, 1), "ctx", axis=0, tiled=True)
    outputs = [
        feed_forward(routed_rows[:, expert], *weights_in[expert])
        for expert in range(PASS_SPECIALISTS)
    ]
    expert_out = lax.psum_scatter(
        jnp.stack(outputs, axis=1), "ctx", scatter_dimension=0, tiled=True
    )
    expert_sum = combine_rows(routing, [expert_out[:, e] for e in range(PASS_SPECIALISTS)])
    return (attn_proj[None], expert_sum[None])


def gather_rows(unit, bits, dp_size):
    for bit in bits[:-1]:
        unit = jnp.concatenate([unit, hop(unit, "dp", dp_size, bit)], axis=0)
    half = unit.shape[-1] // 2
    left, right = unit[..., :half], unit[..., half:]
    left = jnp.stack([left, hop(left, "dp", dp_size, bits[-1])])
    right = jnp.stack([right, hop(right, "ctx", 2, 1)])
    left = jnp.stack([left, hop(left, "ctx", 2, 1)])
    right = jnp.stack([right, hop(right, "dp", dp_size, bits[-1])], axis=1)
    return jnp.concatenate([left, right], axis=-1)


def scatter_rows(rows, bits, dp_size, offset):
    half = rows.shape[-1] // 2
    left, right = rows[..., :half], rows[..., half:]

    def add(kept, came):
        return (kept.astype(jnp.float32) + came.astype(jnp.float32)).astype(jnp.bfloat16)

    near = (offset & bits[-1]) == 0
    left = add(left[0], hop(left[1], "ctx", 2, 1))
    right = jnp.where(near, right[:, 0], hop(right[:, 1], "dp", dp_size, bits[-1]))
    left = jnp.where(near, left[0], hop(left[1], "dp", dp_size, bits[-1]))
    right = add(right[0], hop(right[1], "ctx", 2, 1))
    unit = jnp.concatenate([left, right], axis=-1)
    for bit in reversed(bits[:-1]):
        kept, sent = jnp.split(unit, 2, axis=0)
        unit = jnp.where((offset & bit) == 0, kept, hop(sent, "dp", dp_size, bit))
    return unit


def body_move_rows(
    query_vecs,
    key_vecs,
    value_vecs,
    residual,
    w_out,
    norm_gain,
    w_gate_up,
    w_down,
    expert_ids,
    route_gates,
    capacity,
    expert_owner,
):
    token_count = query_vecs.shape[1]
    width = residual.shape[2]
    dp_size = lax.axis_size("dp")
    me = lax.axis_index("dp")
    core = me & 1
    ctx = lax.axis_index("ctx")

    keys_before = lax.ppermute(key_vecs[0], "ctx", [(0, 1)])
    values_before = lax.ppermute(value_vecs[0], "ctx", [(0, 1)])
    groups = [list(range(c, dp_size, 2)) for c in range(2)]
    out_near = lax.all_gather(w_out, "dp", axis=0, tiled=True, axis_index_groups=groups)
    out_far = hop(out_near, "dp", dp_size, 1)
    gate_up_far = hop(w_gate_up[0], "dp", dp_size, 1)
    down_far = hop(w_down[0], "dp", dp_size, 1)

    row = jnp.arange(token_count)
    own_visible = row[None, :] <= row[:, None]
    before_visible = jnp.broadcast_to(ctx == 1, own_visible.shape)
    attended = attend(
        query_vecs[0],
        jnp.concatenate([keys_before, key_vecs[0]], axis=0),
        jnp.concatenate([values_before, value_vecs[0]], axis=0),
        jnp.concatenate([before_visible, own_visible], axis=1),
    )
    by_core = attended.reshape(token_count, dp_size // 2, 2, w_out.shape[0])
    even = by_core[:, :, 0].reshape(token_count, -1)
    odd = by_core[:, :, 1].reshape(token_count, -1)
    projected = jnp.dot(
        jnp.where(core == 0, even, odd), out_near, preferred_element_type=jnp.float32
    ) + jnp.dot(jnp.where(core == 0, odd, even), out_far, preferred_element_type=jnp.float32)
    attn_proj = projected.astype(jnp.bfloat16)
    normed = normalise(attn_proj, residual[0], norm_gain)
    routing = [
        route_slots(expert_ids[0], route_gates[0], capacity[0, 0], expert)
        for expert in range(PASS_SPECIALISTS)
    ]
    chosen = pick_rows(routing, normed)

    bits = [1 << k for k in reversed(range(1, dp_size.bit_length() - 1))]
    owners = expert_owner[:PASS_SPECIALISTS]
    differ = owners[0] ^ owners[1]
    branch = len(bits)
    for k in reversed(range(len(bits))):
        branch = jnp.where((differ & bits[k]) != 0, k, branch)
    split_bit = jnp.asarray(bits + [0])[branch]
    local = jnp.where(((me ^ owners[0]) & split_bit) == 0, 0, 1)
    local_owner = owners[local]
    own_weights = (local_owner & 1) == core
    gate_up_local, down_local = lax.optimization_barrier(
        (
            jnp.where(own_weights, w_gate_up[0], gate_up_far),
            jnp.where(own_weights, w_down[0], down_far),
        )
    )
    offset = me ^ local_owner

    def apart(bit):
        rest = [b for b in bits if b != bit]

        def run(chosen):
            kept = jnp.where(local == 0, chosen[0], chosen[1])
            sent = jnp.where(local == 0, chosen[1], chosen[0])
            unit = jnp.stack([kept, hop(sent, "dp", dp_size, bit)])
            rows = gather_rows(unit, rest, dp_size)
            made = feed_forward(rows.reshape(-1, width), gate_up_local, down_local)
            unit = scatter_rows(made.reshape(rows.shape), rest, dp_size, offset)
            near, far = unit[0], hop(unit[1], "dp", dp_size, bit)
            return jnp.stack(
                [jnp.where(local == 0, near, far), jnp.where(local == 0, far, near)]
            )

        return run

    def together(chosen):
        rows = gather_rows(chosen[None], bits, dp_size)
        gate_up_next = jnp.where(own_weights, gate_up_far, w_gate_up[0])
        down_next = jnp.where(own_weights, down_far, w_down[0])
        shape = rows[..., 0, :, :].shape
        made = jnp.stack(
            [
                feed_forward(
                    rows[..., 0, :, :].reshape(-1, width), gate_up_local, down_local
                ).reshape(shape),
                feed_forward(
                    rows[..., 1, :, :].reshape(-1, width), gate_up_next, down_next
                ).reshape(shape),
            ],
            axis=-3,
        )
        return scatter_rows(made, bits, dp_size, offset)[0]

    produced = lax.switch(branch, [apart(bit) for bit in bits] + [together], chosen)
    expert_sum = combine_rows(routing, produced)
    return (attn_proj[None], expert_sum[None])


def solution(mesh):
    placed = (
        P("dp", "ctx", None),
        P("dp", "ctx", None),
        P("dp", "ctx", None),
        P("dp", "ctx", None),
        P("dp", None),
        P(),
        P("dp", None, None, "ctx"),
        P("dp", "ctx", None),
        P("dp", "ctx", None),
        P("dp", "ctx", None),
        P("dp", "ctx", None),
        P(),
    )
    dp_size, ctx_size = mesh.shape["dp"], mesh.shape["ctx"]
    small = ctx_size == 2 and 4 <= dp_size <= 16 and dp_size & (dp_size - 1) == 0
    return jax.shard_map(
        body_move_rows if small else body_move_weights,
        mesh=mesh,
        in_specs=placed,
        out_specs=(P("dp", "ctx", None), P("dp", "ctx", None)),
        check_vma=False,
    )
```

```python
import jax
import jax.numpy as jnp
from jax import lax
from jax.experimental import pallas as pl
from jax.experimental.pallas import tpu as pltpu
from jax.sharding import PartitionSpec as P

HEADS = 8
HD = 128
PASS_SPECIALISTS = 2
CAP = 24


EPSILON = 1e-06
LOWEST = -1e30


def broadcast(array, axis, root):
    mine = lax.axis_index(axis) == root
    return lax.psum(jnp.where(mine, array, jnp.zeros_like(array)), axis)


def hop(array, axis, size, bit):
    return lax.ppermute(array, axis, [(i, i ^ bit) for i in range(size)])


def route_slots(expert_ids, route_gates, capacity, expert):
    matches = expert_ids == expert
    routed = jnp.any(matches, axis=1)
    gate_value = jnp.sum(jnp.where(matches, route_gates, 0.0), axis=1)
    slot_rank = jnp.cumsum(routed.astype(jnp.int32)) - 1
    kept_mask = routed & (slot_rank < capacity[expert])
    return (slot_rank, kept_mask, gate_value)


def attend(queries, key_block, value_block, visible):
    width = key_block.shape[0]
    token_count = queries.shape[0]
    query_heads = queries.reshape(token_count, HEADS, HD)
    key_heads = key_block.reshape(width, HEADS, HD)
    value_heads = value_block.reshape(width, HEADS, HD)
    gating_logits = jnp.einsum(
        "qhd,khd->qhk", query_heads, key_heads, preferred_element_type=jnp.float32
    ) * HD ** (-0.5)
    gating_logits = jnp.where(visible[:, None, :], gating_logits, -jnp.inf)
    row_top = jnp.max(gating_logits, axis=-1)
    weights = jnp.exp(gating_logits - row_top[:, :, None])
    denominator = jnp.sum(weights, axis=-1)
    weighted = jnp.einsum(
        "qhk,khd->qhd",
        weights.astype(jnp.bfloat16),
        value_heads,
        preferred_element_type=jnp.float32,
    )
    attended = (weighted / denominator[:, :, None]).astype(jnp.bfloat16)
    return attended.reshape(token_count, HEADS * HD)


def feed_forward(rows, gate_up, down_part):
    gate_proj = jnp.dot(rows, gate_up[0], preferred_element_type=jnp.float32)
    up_proj = jnp.dot(rows, gate_up[1], preferred_element_type=jnp.float32)
    hidden = (jax.nn.silu(gate_proj) * up_proj).astype(jnp.bfloat16)
    return jnp.dot(hidden, down_part, preferred_element_type=jnp.float32).astype(jnp.bfloat16)


def normalise(attn_proj, residual, norm_gain):
    combined = residual.astype(jnp.float32) + attn_proj.astype(jnp.float32)
    return (
        combined
        * lax.rsqrt(jnp.mean(combined * combined, axis=-1, keepdims=True) + EPSILON)
        * norm_gain
    ).astype(jnp.bfloat16)


def pick_rows(routing, normed):
    slot_ids = jnp.arange(CAP)
    select = [
        (slot_rank[None, :] == slot_ids[:, None]) & kept_mask[None, :]
        for slot_rank, kept_mask, _ in routing
    ]
    select = jnp.concatenate(select, axis=0).astype(jnp.bfloat16)
    chosen = jnp.dot(select, normed, preferred_element_type=jnp.float32).astype(jnp.bfloat16)
    return chosen.reshape(PASS_SPECIALISTS, CAP, normed.shape[1])


def combine_rows(routing, produced):
    slot_ids = jnp.arange(CAP)
    summed = 0.0
    for expert in range(PASS_SPECIALISTS):
        slot_rank, kept_mask, gate_value = routing[expert]
        place = ((slot_rank[:, None] == slot_ids[None, :]) & kept_mask[:, None]).astype(
            jnp.bfloat16
        )
        picked = jnp.dot(place, produced[expert], preferred_element_type=jnp.float32)
        summed = summed + gate_value[:, None] * picked
    return summed.astype(jnp.bfloat16)


def body_move_weights(
    query_vecs,
    key_vecs,
    value_vecs,
    residual,
    w_out,
    norm_gain,
    w_gate_up,
    w_down,
    expert_ids,
    route_gates,
    capacity,
    expert_owner,
):
    token_count = query_vecs.shape[1]
    weights_in = []
    for expert in range(PASS_SPECIALISTS):
        weights_in.append(
            (
                broadcast(w_gate_up[0], "dp", expert_owner[expert]),
                broadcast(w_down[0], "dp", expert_owner[expert]),
            )
        )
    keys = lax.all_gather(key_vecs[0], "ctx", axis=0, tiled=True)
    values = lax.all_gather(value_vecs[0], "ctx", axis=0, tiled=True)
    first_row = lax.axis_index("ctx") * token_count
    query_pos = first_row + jnp.arange(token_count)
    visible = jnp.arange(keys.shape[0])[None, :] <= query_pos[:, None]
    attended = attend(query_vecs[0], keys, values, visible)
    projected = jnp.dot(
        attended,
        lax.all_gather(w_out, "dp", axis=0, tiled=True),
        preferred_element_type=jnp.float32,
    )
    attn_proj = projected.astype(jnp.bfloat16)
    normed = normalise(attn_proj, residual[0], norm_gain)
    routing = [
        route_slots(expert_ids[0], route_gates[0], capacity[0, 0], expert)
        for expert in range(PASS_SPECIALISTS)
    ]
    chosen = pick_rows(routing, normed)
    routed_rows = lax.all_gather(jnp.swapaxes(chosen, 0, 1), "ctx", axis=0, tiled=True)
    outputs = [
        feed_forward(routed_rows[:, expert], *weights_in[expert])
        for expert in range(PASS_SPECIALISTS)
    ]
    expert_out = lax.psum_scatter(
        jnp.stack(outputs, axis=1), "ctx", scatter_dimension=0, tiled=True
    )
    expert_sum = combine_rows(routing, [expert_out[:, e] for e in range(PASS_SPECIALISTS)])
    return (attn_proj[None], expert_sum[None])


def attend_kernel(info, query, key, value, key_before, value_before, ids, gates, attended, place, gate_values):
    token_count = query.shape[0]
    row = lax.broadcasted_iota(jnp.int32, (token_count, token_count), 0)
    col = lax.broadcasted_iota(jnp.int32, (token_count, token_count), 1)
    own_visible = col <= row
    before_visible = jnp.broadcast_to(info[0], (token_count, token_count)) == 1
    contract_last = (((1,), (1,)), ((), ()))
    for head in range(HEADS):
        span = slice(head * HD, (head + 1) * HD)
        heads = query[:, span]
        own = lax.dot_general(
            heads, key[:, span], contract_last, preferred_element_type=jnp.float32
        )
        before = lax.dot_general(
            heads, key_before[:, span], contract_last, preferred_element_type=jnp.float32
        )
        own = jnp.where(own_visible, own * HD ** (-0.5), -jnp.inf)
        before = jnp.where(before_visible, before * HD ** (-0.5), -jnp.inf)
        top = jnp.maximum(
            jnp.max(own, axis=1, keepdims=True), jnp.max(before, axis=1, keepdims=True)
        )
        own = jnp.exp(own - top)
        before = jnp.exp(before - top)
        total = jnp.sum(own, axis=1, keepdims=True) + jnp.sum(before, axis=1, keepdims=True)
        mixed = jnp.dot(
            own.astype(jnp.bfloat16), value[:, span], preferred_element_type=jnp.float32
        ) + jnp.dot(
            before.astype(jnp.bfloat16), value_before[:, span], preferred_element_type=jnp.float32
        )
        mixed = mixed / total
        swapped = pltpu.roll(mixed, HD // 2, 1)
        mixed = jnp.where(jnp.broadcast_to(info[2], mixed.shape) == 0, mixed, swapped)
        attended[head ^ info[1]] = mixed.astype(jnp.bfloat16)

    slots = PASS_SPECIALISTS * CAP
    lane = lax.broadcasted_iota(jnp.int32, (token_count, slots), 1)
    routed = jnp.zeros((token_count, slots), jnp.float32)
    limit = jnp.zeros((token_count, slots), jnp.int32)
    for expert in range(PASS_SPECIALISTS):
        matches = ids[...] == expert
        named = jnp.max(matches.astype(jnp.float32), axis=1, keepdims=True)
        gate_values[:, expert : expert + 1] = jnp.sum(
            jnp.where(matches, gates[...], 0.0), axis=1, keepdims=True
        )
        mine = (lane >= expert * CAP) & (lane < (expert + 1) * CAP)
        routed = jnp.where(mine, named, routed)
        limit = jnp.where(mine, info[3 + expert], limit)
    earlier = (col < row).astype(jnp.bfloat16)
    rank = jnp.dot(
        earlier, routed.astype(jnp.bfloat16), preferred_element_type=jnp.float32
    ).astype(jnp.int32)
    slot = jnp.where(lane >= CAP, lane - CAP, lane)
    place[...] = ((routed > 0.0) & (rank == slot) & (rank < limit)).astype(jnp.bfloat16)


def project_kernel(*refs):
    attended, residual, gain, place = refs[:4]
    near = refs[4 : 4 + HEADS]
    far = refs[4 + HEADS : 4 + 2 * HEADS]
    attn_proj, chosen, combined = refs[4 + 2 * HEADS :]
    token_count, width = residual.shape
    tile = 512
    squares = jnp.zeros((token_count, 1), jnp.float32)
    for start in range(0, width, tile):
        span = slice(start, start + tile)
        total = jnp.zeros((token_count, tile), jnp.float32)
        for pair in range(0, HEADS, 2):
            left = jnp.concatenate([attended[pair], attended[pair + 1]], axis=1)
            right = jnp.concatenate(
                [near[pair][:, span], far[pair][:, span]]
                + [near[pair + 1][:, span], far[pair + 1][:, span]],
                axis=0,
            )
            total = total + jnp.dot(left, right, preferred_element_type=jnp.float32)
        rounded = total.astype(jnp.bfloat16)
        attn_proj[:, span] = rounded
        added = residual[:, span].astype(jnp.float32) + rounded.astype(jnp.float32)
        combined[:, span] = added
        squares = squares + jnp.sum(added * added, axis=1, keepdims=True)
    scale = lax.rsqrt(squares / width + EPSILON)
    for start in range(0, width, tile):
        span = slice(start, start + tile)
        normed = (combined[:, span] * scale * gain[:, span]).astype(jnp.bfloat16)
        chosen[:, span] = lax.dot_general(
            place[...], normed, (((0,), (0,)), ((), ())), preferred_element_type=jnp.float32
        ).astype(jnp.bfloat16)


def expert_kernel(other, rows, gate_up_near, gate_up_far, down_near, down_far, made, gate_up, down, hidden, sems):
    units = down.shape[0]
    starts = list(range(0, units, 256))

    def copies(gate_up_from, down_from):
        out = []
        for k, start in enumerate(starts):
            size = min(256, units - start)
            span = pl.ds(start, size)
            for part in range(2):
                out.append(
                    pltpu.make_async_copy(
                        gate_up_from.at[part, span], gate_up.at[part, span], sems.at[2 * k + part]
                    )
                )
        out.append(pltpu.make_async_copy(down_from, down, sems.at[2 * len(starts)]))
        return out

    @pl.when(other[0] == 0)
    def _():
        for copy in copies(gate_up_near, down_near):
            copy.start()

    @pl.when(other[0] != 0)
    def _():
        for copy in copies(gate_up_far, down_far):
            copy.start()

    arrived = copies(gate_up_near, down_near)
    contract_last = (((1,), (1,)), ((), ()))
    for k, start in enumerate(starts):
        size = min(256, units - start)
        span = slice(start, start + size)
        arrived[2 * k].wait()
        gate_proj = lax.dot_general(
            rows[...], gate_up[0, span], contract_last, preferred_element_type=jnp.float32
        )
        arrived[2 * k + 1].wait()
        up_proj = lax.dot_general(
            rows[...], gate_up[1, span], contract_last, preferred_element_type=jnp.float32
        )
        hidden[:, span] = (gate_proj / (1.0 + jnp.exp(-gate_proj)) * up_proj).astype(jnp.bfloat16)
    arrived[-1].wait()
    width = made.shape[1]
    for start in range(0, width, 512):
        span = slice(start, start + 512)
        made[:, span] = jnp.dot(
            hidden[...], down[:, span], preferred_element_type=jnp.float32
        ).astype(jnp.bfloat16)


def gather_rows(unit, bits, dp_size):
    for bit in bits[:-1]:
        unit = jnp.concatenate([unit, hop(unit, "dp", dp_size, bit)], axis=0)
    half = unit.shape[1] // 2
    left, right = unit[:, :half], unit[:, half:]
    left = jnp.stack([left, hop(left, "dp", dp_size, bits[-1])])
    right = jnp.stack([right, hop(right, "ctx", 2, 1)])
    left = jnp.stack([left, hop(left, "ctx", 2, 1)])
    right = jnp.stack([right, hop(right, "dp", dp_size, bits[-1])], axis=1)
    rows = jnp.concatenate([left, right], axis=-1)
    return rows.reshape(-1, rows.shape[-1])


def scatter_rows(rows, bits, dp_size, offset):
    half = rows.shape[1] // 2
    rows = rows.reshape(2, 2, -1, rows.shape[1])
    left, right = rows[..., :half], rows[..., half:]

    def add(kept, came):
        return (kept.astype(jnp.float32) + came.astype(jnp.float32)).astype(jnp.bfloat16)

    near = (offset & bits[-1]) == 0
    left = add(left[0], hop(left[1], "ctx", 2, 1))
    right = jnp.where(near, right[:, 0], hop(right[:, 1], "dp", dp_size, bits[-1]))
    left = jnp.where(near, left[0], hop(left[1], "dp", dp_size, bits[-1]))
    right = add(right[0], hop(right[1], "ctx", 2, 1))
    unit = jnp.concatenate([left, right], axis=-1)
    for bit in reversed(bits[:-1]):
        kept, sent = jnp.split(unit, 2, axis=0)
        unit = jnp.where((offset & bit) == 0, kept, hop(sent, "dp", dp_size, bit))
    return unit


def vmem(count):
    return [pl.BlockSpec(memory_space=pltpu.VMEM)] * count


def body_move_rows(
    query_vecs,
    key_vecs,
    value_vecs,
    residual,
    w_out,
    norm_gain,
    w_gate_up,
    w_down,
    expert_ids,
    route_gates,
    capacity,
    expert_owner,
):
    token_count = query_vecs.shape[1]
    width = residual.shape[2]
    dp_size = lax.axis_size("dp")
    me = lax.axis_index("dp")
    core = me & 1
    ctx = lax.axis_index("ctx")
    bits = [1 << k for k in reversed(range(1, dp_size.bit_length() - 1))]

    key_before = lax.ppermute(key_vecs[0], "ctx", [(0, 1)])
    value_before = lax.ppermute(value_vecs[0], "ctx", [(0, 1)])
    z_far, z_near, x_bit = bits
    half = width // 2
    near = [None] * HEADS
    near[0] = w_out
    near[z_near >> 1] = hop(w_out, "dp", dp_size, z_near)
    near[z_far >> 1] = hop(w_out, "dp", dp_size, z_far)
    near[x_bit >> 1] = hop(w_out, "dp", dp_size, x_bit)
    near[(z_near | x_bit) >> 1] = hop(near[z_near >> 1], "dp", dp_size, x_bit)
    near[(z_far | x_bit) >> 1] = hop(near[z_far >> 1], "dp", dp_size, x_bit)
    z_both = jnp.concatenate(
        [
            hop(near[z_far >> 1][:, :half], "dp", dp_size, z_near),
            hop(near[z_near >> 1][:, half:], "dp", dp_size, z_far),
        ],
        axis=1,
    )
    near[(z_far | z_near) >> 1] = z_both
    near[(z_far | z_near | x_bit) >> 1] = hop(z_both, "dp", dp_size, x_bit)
    far = [None] * HEADS
    for group in ([0, z_near >> 1, z_far >> 1, x_bit >> 1], [(z_near | x_bit) >> 1, (z_far | x_bit) >> 1], [(z_far | z_near) >> 1, (z_far | z_near | x_bit) >> 1]):
        came = hop(jnp.stack([near[j] for j in group]), "dp", dp_size, 1)
        for k, j in enumerate(group):
            far[j] = came[k]
    gate_up_near = jnp.swapaxes(w_gate_up[0], 1, 2)
    gate_up_far = hop(gate_up_near, "dp", dp_size, 1)
    down_far = hop(w_down[0], "dp", dp_size, 1)

    info = jnp.stack([ctx, me >> 1, core, capacity[0, 0, 0], capacity[0, 0, 1]]).astype(jnp.int32)
    slots = PASS_SPECIALISTS * CAP
    attended, place, gate_values = pl.pallas_call(
        attend_kernel,
        out_shape=(
            jax.ShapeDtypeStruct((HEADS, token_count, HD), jnp.bfloat16),
            jax.ShapeDtypeStruct((token_count, slots), jnp.bfloat16),
            jax.ShapeDtypeStruct((token_count, PASS_SPECIALISTS), jnp.float32),
        ),
        in_specs=[pl.BlockSpec(memory_space=pltpu.SMEM)] + vmem(7),
        out_specs=tuple(vmem(3)),
        cost_estimate=pl.CostEstimate(
            flops=4 * HEADS * HD * 2 * token_count * token_count,
            bytes_accessed=6 * 2 * token_count * HEADS * HD,
            transcendentals=2 * HEADS * token_count * token_count,
        ),
        compiler_params=pltpu.CompilerParams(vmem_limit_bytes=16 * 2**20),
    )(
        info,
        query_vecs[0],
        key_vecs[0],
        value_vecs[0],
        key_before,
        value_before,
        expert_ids[0],
        route_gates[0],
    )
    attn_proj, chosen = pl.pallas_call(
        project_kernel,
        out_shape=(
            jax.ShapeDtypeStruct((token_count, width), jnp.bfloat16),
            jax.ShapeDtypeStruct((slots, width), jnp.bfloat16),
        ),
        in_specs=vmem(4 + 2 * HEADS),
        out_specs=tuple(vmem(2)),
        scratch_shapes=[pltpu.VMEM((token_count, width), jnp.float32)],
        cost_estimate=pl.CostEstimate(
            flops=2 * token_count * HEADS * HD * width,
            bytes_accessed=2 * HEADS * HD * width,
            transcendentals=0,
        ),
        compiler_params=pltpu.CompilerParams(vmem_limit_bytes=24 * 2**20),
    )(attended, residual[0], norm_gain[None], place, *near, *far)

    owners = expert_owner[:PASS_SPECIALISTS]
    differ = owners[0] ^ owners[1]
    branch = 0
    split_bit = 0
    for k in reversed(range(len(bits))):
        parted = (differ & bits[k]) != 0
        branch = jnp.where(parted, k, branch)
        split_bit = jnp.where(parted, bits[k], split_bit)
    same = split_bit == 0
    side = jnp.where(((me ^ owners[0]) & split_bit) == 0, 0, 1)
    units = w_down.shape[1]
    row_count = dp_size * CAP

    def dispatch(bit):
        rest = [b for b in bits if b != bit]

        def run(kept, sent):
            unit = jnp.concatenate([kept, hop(sent, "dp", dp_size, bit)], axis=0)
            return gather_rows(unit, rest, dp_size)

        return run

    def give_back(bit):
        rest = [b for b in bits if b != bit]

        def run(made, offset):
            unit = scatter_rows(made, rest, dp_size, offset)
            return unit[:CAP], hop(unit[CAP:], "dp", dp_size, bit)

        return run

    def one_pass(step, produced):
        local = jnp.where(same, step, side)
        sent_expert = jnp.where(same, step, 1 - side)
        owner = jnp.where(local == 0, owners[0], owners[1])
        offset = me ^ owner
        kept = jnp.where(local == 0, chosen[:CAP], chosen[CAP:])
        sent = jnp.where(sent_expert == 0, chosen[:CAP], chosen[CAP:])
        rows = lax.switch(branch, [dispatch(bit) for bit in bits], kept, sent)
        made = pl.pallas_call(
            expert_kernel,
            out_shape=jax.ShapeDtypeStruct((row_count, width), jnp.bfloat16),
            in_specs=[pl.BlockSpec(memory_space=pltpu.SMEM)]
            + vmem(1)
            + [pl.BlockSpec(memory_space=pl.ANY)] * 4,
            out_specs=vmem(1)[0],
            scratch_shapes=[
                pltpu.VMEM((2, units, width), jnp.bfloat16),
                pltpu.VMEM((units, width), jnp.bfloat16),
                pltpu.VMEM((row_count, units), jnp.bfloat16),
                pltpu.SemaphoreType.DMA((2 * -(-units // 256) + 1,)),
            ],
            cost_estimate=pl.CostEstimate(
                flops=6 * row_count * units * width,
                bytes_accessed=6 * units * width,
                transcendentals=row_count * units,
            ),
            compiler_params=pltpu.CompilerParams(vmem_limit_bytes=40 * 2**20),
        )((offset & 1)[None], rows, gate_up_near, gate_up_far, w_down[0], down_far)
        own, other = lax.switch(branch, [give_back(bit) for bit in bits], made, offset)
        served = jnp.where((offset & bits[0]) == 0, own, other)
        first = jnp.where(same, served, jnp.where(local == 0, own, other))
        second = jnp.where(same, served, jnp.where(local == 0, other, own))
        return (
            jnp.where(same & (step != 0), produced[0], first),
            jnp.where(same & (step != 1), produced[1], second),
        )

    nothing = jnp.zeros((CAP, width), jnp.bfloat16)
    produced = lax.fori_loop(0, jnp.where(same, 2, 1), one_pass, (nothing, nothing))
    summed = 0.0
    for expert in range(PASS_SPECIALISTS):
        picked = jnp.dot(
            place[:, expert * CAP : (expert + 1) * CAP],
            produced[expert],
            preferred_element_type=jnp.float32,
        )
        summed = summed + gate_values[:, expert : expert + 1] * picked
    expert_sum = summed.astype(jnp.bfloat16)
    return (attn_proj[None], expert_sum[None])


def solution(mesh):
    placed = (
        P("dp", "ctx", None),
        P("dp", "ctx", None),
        P("dp", "ctx", None),
        P("dp", "ctx", None),
        P("dp", None),
        P(),
        P("dp", None, None, "ctx"),
        P("dp", "ctx", None),
        P("dp", "ctx", None),
        P("dp", "ctx", None),
        P("dp", "ctx", None),
        P(),
    )
    dp_size, ctx_size = mesh.shape["dp"], mesh.shape["ctx"]
    small = ctx_size == 2 and dp_size == 2 * HEADS
    return jax.shard_map(
        body_move_rows if small else body_move_weights,
        mesh=mesh,
        in_specs=placed,
        out_specs=(P("dp", "ctx", None), P("dp", "ctx", None)),
        check_vma=False,
    )
```

```python
import jax
import jax.numpy as jnp
from jax import lax
from jax.experimental import pallas as pl
from jax.experimental.pallas import tpu as pltpu
from jax.sharding import PartitionSpec as P

HEADS = 8
HD = 128
PASS_SPECIALISTS = 2
CAP = 24


EPSILON = 1e-06
LOWEST = -1e30


def broadcast(array, axis, root):
    mine = lax.axis_index(axis) == root
    return lax.psum(jnp.where(mine, array, jnp.zeros_like(array)), axis)


def hop(array, axis, size, bit):
    return lax.ppermute(array, axis, [(i, i ^ bit) for i in range(size)])


def route_slots(expert_ids, route_gates, capacity, expert):
    matches = expert_ids == expert
    routed = jnp.any(matches, axis=1)
    gate_value = jnp.sum(jnp.where(matches, route_gates, 0.0), axis=1)
    slot_rank = jnp.cumsum(routed.astype(jnp.int32)) - 1
    kept_mask = routed & (slot_rank < capacity[expert])
    return (slot_rank, kept_mask, gate_value)


def attend(queries, key_block, value_block, visible):
    width = key_block.shape[0]
    token_count = queries.shape[0]
    query_heads = queries.reshape(token_count, HEADS, HD)
    key_heads = key_block.reshape(width, HEADS, HD)
    value_heads = value_block.reshape(width, HEADS, HD)
    gating_logits = jnp.einsum(
        "qhd,khd->qhk", query_heads, key_heads, preferred_element_type=jnp.float32
    ) * HD ** (-0.5)
    gating_logits = jnp.where(visible[:, None, :], gating_logits, -jnp.inf)
    row_top = jnp.max(gating_logits, axis=-1)
    weights = jnp.exp(gating_logits - row_top[:, :, None])
    denominator = jnp.sum(weights, axis=-1)
    weighted = jnp.einsum(
        "qhk,khd->qhd",
        weights.astype(jnp.bfloat16),
        value_heads,
        preferred_element_type=jnp.float32,
    )
    attended = (weighted / denominator[:, :, None]).astype(jnp.bfloat16)
    return attended.reshape(token_count, HEADS * HD)


def feed_forward(rows, gate_up, down_part):
    gate_proj = jnp.dot(rows, gate_up[0], preferred_element_type=jnp.float32)
    up_proj = jnp.dot(rows, gate_up[1], preferred_element_type=jnp.float32)
    hidden = (jax.nn.silu(gate_proj) * up_proj).astype(jnp.bfloat16)
    return jnp.dot(hidden, down_part, preferred_element_type=jnp.float32).astype(jnp.bfloat16)


def normalise(attn_proj, residual, norm_gain):
    combined = residual.astype(jnp.float32) + attn_proj.astype(jnp.float32)
    return (
        combined
        * lax.rsqrt(jnp.mean(combined * combined, axis=-1, keepdims=True) + EPSILON)
        * norm_gain
    ).astype(jnp.bfloat16)


def pick_rows(routing, normed):
    slot_ids = jnp.arange(CAP)
    select = [
        (slot_rank[None, :] == slot_ids[:, None]) & kept_mask[None, :]
        for slot_rank, kept_mask, _ in routing
    ]
    select = jnp.concatenate(select, axis=0).astype(jnp.bfloat16)
    chosen = jnp.dot(select, normed, preferred_element_type=jnp.float32).astype(jnp.bfloat16)
    return chosen.reshape(PASS_SPECIALISTS, CAP, normed.shape[1])


def combine_rows(routing, produced):
    slot_ids = jnp.arange(CAP)
    summed = 0.0
    for expert in range(PASS_SPECIALISTS):
        slot_rank, kept_mask, gate_value = routing[expert]
        place = ((slot_rank[:, None] == slot_ids[None, :]) & kept_mask[:, None]).astype(
            jnp.bfloat16
        )
        picked = jnp.dot(place, produced[expert], preferred_element_type=jnp.float32)
        summed = summed + gate_value[:, None] * picked
    return summed.astype(jnp.bfloat16)


def body_move_weights(
    query_vecs,
    key_vecs,
    value_vecs,
    residual,
    w_out,
    norm_gain,
    w_gate_up,
    w_down,
    expert_ids,
    route_gates,
    capacity,
    expert_owner,
):
    token_count = query_vecs.shape[1]
    weights_in = []
    for expert in range(PASS_SPECIALISTS):
        weights_in.append(
            (
                broadcast(w_gate_up[0], "dp", expert_owner[expert]),
                broadcast(w_down[0], "dp", expert_owner[expert]),
            )
        )
    keys = lax.all_gather(key_vecs[0], "ctx", axis=0, tiled=True)
    values = lax.all_gather(value_vecs[0], "ctx", axis=0, tiled=True)
    first_row = lax.axis_index("ctx") * token_count
    query_pos = first_row + jnp.arange(token_count)
    visible = jnp.arange(keys.shape[0])[None, :] <= query_pos[:, None]
    attended = attend(query_vecs[0], keys, values, visible)
    projected = jnp.dot(
        attended,
        lax.all_gather(w_out, "dp", axis=0, tiled=True),
        preferred_element_type=jnp.float32,
    )
    attn_proj = projected.astype(jnp.bfloat16)
    normed = normalise(attn_proj, residual[0], norm_gain)
    routing = [
        route_slots(expert_ids[0], route_gates[0], capacity[0, 0], expert)
        for expert in range(PASS_SPECIALISTS)
    ]
    chosen = pick_rows(routing, normed)
    routed_rows = lax.all_gather(jnp.swapaxes(chosen, 0, 1), "ctx", axis=0, tiled=True)
    outputs = [
        feed_forward(routed_rows[:, expert], *weights_in[expert])
        for expert in range(PASS_SPECIALISTS)
    ]
    expert_out = lax.psum_scatter(
        jnp.stack(outputs, axis=1), "ctx", scatter_dimension=0, tiled=True
    )
    expert_sum = combine_rows(routing, [expert_out[:, e] for e in range(PASS_SPECIALISTS)])
    return (attn_proj[None], expert_sum[None])


def attend_kernel(info, query, key, value, before_both, ids, gates, attended, place, gate_values):
    token_count = query.shape[0]
    row = lax.broadcasted_iota(jnp.int32, (token_count, token_count), 0)
    col = lax.broadcasted_iota(jnp.int32, (token_count, token_count), 1)
    own_visible = col <= row
    before_visible = jnp.broadcast_to(info[0], (token_count, token_count)) == 1
    contract_last = (((1,), (1,)), ((), ()))
    for head in range(HEADS):
        span = slice(head * HD, (head + 1) * HD)
        heads = query[:, span]
        own = lax.dot_general(
            heads, key[:, span], contract_last, preferred_element_type=jnp.float32
        )
        before = lax.dot_general(
            heads, before_both[0, :, span], contract_last, preferred_element_type=jnp.float32
        )
        own = jnp.where(own_visible, own * HD ** (-0.5), -jnp.inf)
        before = jnp.where(before_visible, before * HD ** (-0.5), -jnp.inf)
        top = jnp.maximum(
            jnp.max(own, axis=1, keepdims=True), jnp.max(before, axis=1, keepdims=True)
        )
        own = jnp.exp(own - top)
        before = jnp.exp(before - top)
        total = jnp.sum(own, axis=1, keepdims=True) + jnp.sum(before, axis=1, keepdims=True)
        mixed = jnp.dot(
            own.astype(jnp.bfloat16), value[:, span], preferred_element_type=jnp.float32
        ) + jnp.dot(
            before.astype(jnp.bfloat16), before_both[1, :, span], preferred_element_type=jnp.float32
        )
        mixed = mixed / total
        swapped = pltpu.roll(mixed, HD // 2, 1)
        mixed = jnp.where(jnp.broadcast_to(info[2], mixed.shape) == 0, mixed, swapped)
        attended[head ^ info[1]] = mixed.astype(jnp.bfloat16)

    slots = PASS_SPECIALISTS * CAP
    lane = lax.broadcasted_iota(jnp.int32, (token_count, slots), 1)
    routed = jnp.zeros((token_count, slots), jnp.float32)
    limit = jnp.zeros((token_count, slots), jnp.int32)
    for expert in range(PASS_SPECIALISTS):
        matches = ids[...] == expert
        named = jnp.max(matches.astype(jnp.float32), axis=1, keepdims=True)
        gate_values[:, expert : expert + 1] = jnp.sum(
            jnp.where(matches, gates[...], 0.0), axis=1, keepdims=True
        )
        mine = (lane >= expert * CAP) & (lane < (expert + 1) * CAP)
        routed = jnp.where(mine, named, routed)
        limit = jnp.where(mine, info[3 + expert], limit)
    earlier = (col < row).astype(jnp.bfloat16)
    rank = jnp.dot(
        earlier, routed.astype(jnp.bfloat16), preferred_element_type=jnp.float32
    ).astype(jnp.int32)
    slot = jnp.where(lane >= CAP, lane - CAP, lane)
    place[...] = ((routed > 0.0) & (rank == slot) & (rank < limit)).astype(jnp.bfloat16)


def project_kernel(*refs):
    attended, residual, gain, place = refs[:4]
    near = refs[4 : 4 + HEADS]
    far = refs[4 + HEADS : 4 + 2 * HEADS]
    attn_proj, chosen, combined = refs[4 + 2 * HEADS :]
    token_count, width = residual.shape
    tile = 512
    squares = jnp.zeros((token_count, 1), jnp.float32)
    for start in range(0, width, tile):
        span = slice(start, start + tile)
        total = jnp.zeros((token_count, tile), jnp.float32)
        for pair in range(0, HEADS, 2):
            left = jnp.concatenate([attended[pair], attended[pair + 1]], axis=1)
            right = jnp.concatenate(
                [near[pair][:, span], far[pair][:, span]]
                + [near[pair + 1][:, span], far[pair + 1][:, span]],
                axis=0,
            )
            total = total + jnp.dot(left, right, preferred_element_type=jnp.float32)
        rounded = total.astype(jnp.bfloat16)
        attn_proj[:, span] = rounded
        added = residual[:, span].astype(jnp.float32) + rounded.astype(jnp.float32)
        combined[:, span] = added
        squares = squares + jnp.sum(added * added, axis=1, keepdims=True)
    scale = lax.rsqrt(squares / width + EPSILON)
    for start in range(0, width, tile):
        span = slice(start, start + tile)
        normed = (combined[:, span] * scale * gain[:, span]).astype(jnp.bfloat16)
        chosen[:, span] = lax.dot_general(
            place[...], normed, (((0,), (0,)), ((), ())), preferred_element_type=jnp.float32
        ).astype(jnp.bfloat16)


def expert_kernel(other, rows, gate_up_near, gate_up_far, down_near, down_far, made, gate_up, down, hidden, sems):
    units = down.shape[0]
    starts = list(range(0, units, 256))

    def copies(gate_up_from, down_from):
        out = []
        for k, start in enumerate(starts):
            size = min(256, units - start)
            span = pl.ds(start, size)
            for part in range(2):
                out.append(
                    pltpu.make_async_copy(
                        gate_up_from.at[part, span], gate_up.at[part, span], sems.at[2 * k + part]
                    )
                )
        out.append(pltpu.make_async_copy(down_from, down, sems.at[2 * len(starts)]))
        return out

    @pl.when(other[0] == 0)
    def _():
        for copy in copies(gate_up_near, down_near):
            copy.start()

    @pl.when(other[0] != 0)
    def _():
        for copy in copies(gate_up_far, down_far):
            copy.start()

    arrived = copies(gate_up_near, down_near)
    contract_last = (((1,), (1,)), ((), ()))
    for k, start in enumerate(starts):
        size = min(256, units - start)
        span = slice(start, start + size)
        arrived[2 * k].wait()
        gate_proj = lax.dot_general(
            gate_up[0, span], rows[...], contract_last, preferred_element_type=jnp.float32
        )
        arrived[2 * k + 1].wait()
        up_proj = lax.dot_general(
            gate_up[1, span], rows[...], contract_last, preferred_element_type=jnp.float32
        )
        hidden[span] = (gate_proj / (1.0 + jnp.exp(-gate_proj)) * up_proj).astype(jnp.bfloat16)
    arrived[-1].wait()
    width = made.shape[1]
    contract_first = (((0,), (0,)), ((), ()))
    for start in range(0, width, 512):
        span = slice(start, start + 512)
        made[:, span] = lax.dot_general(
            hidden[...], down[:, span], contract_first, preferred_element_type=jnp.float32
        ).astype(jnp.bfloat16)


def gather_rows(unit, bits, dp_size):
    for bit in bits[:-1]:
        unit = jnp.concatenate([unit, hop(unit, "dp", dp_size, bit)], axis=0)
    half = unit.shape[1] // 2
    left, right = unit[:, :half], unit[:, half:]
    left = jnp.stack([left, hop(left, "dp", dp_size, bits[-1])])
    right = jnp.stack([right, hop(right, "ctx", 2, 1)])
    left = jnp.stack([left, hop(left, "ctx", 2, 1)])
    right = jnp.stack([right, hop(right, "dp", dp_size, bits[-1])], axis=1)
    rows = jnp.concatenate([left, right], axis=-1)
    return rows.reshape(-1, rows.shape[-1])


def scatter_rows(rows, bits, dp_size, offset):
    half = rows.shape[1] // 2
    rows = rows.reshape(2, 2, -1, rows.shape[1])
    left, right = rows[..., :half], rows[..., half:]

    def add(kept, came):
        return (kept.astype(jnp.float32) + came.astype(jnp.float32)).astype(jnp.bfloat16)

    near = (offset & bits[-1]) == 0
    left = add(left[0], hop(left[1], "ctx", 2, 1))
    right = jnp.where(near, right[:, 0], hop(right[:, 1], "dp", dp_size, bits[-1]))
    left = jnp.where(near, left[0], hop(left[1], "dp", dp_size, bits[-1]))
    right = add(right[0], hop(right[1], "ctx", 2, 1))
    unit = jnp.concatenate([left, right], axis=-1)
    for bit in reversed(bits[:-1]):
        kept, sent = jnp.split(unit, 2, axis=0)
        unit = jnp.where((offset & bit) == 0, kept, hop(sent, "dp", dp_size, bit))
    return unit


def vmem(count):
    return [pl.BlockSpec(memory_space=pltpu.VMEM)] * count


def body_move_rows(
    query_vecs,
    key_vecs,
    value_vecs,
    residual,
    w_out,
    norm_gain,
    w_gate_up,
    w_down,
    expert_ids,
    route_gates,
    capacity,
    expert_owner,
):
    token_count = query_vecs.shape[1]
    width = residual.shape[2]
    dp_size = lax.axis_size("dp")
    me = lax.axis_index("dp")
    core = me & 1
    ctx = lax.axis_index("ctx")
    bits = [1 << k for k in reversed(range(1, dp_size.bit_length() - 1))]

    before = lax.ppermute(jnp.stack([key_vecs[0], value_vecs[0]]), "ctx", [(0, 1)])
    z_far, z_near, x_bit = bits
    z_both = z_far | z_near
    near = {0: w_out}
    for bit in (z_near, x_bit, z_far):
        near[bit] = hop(w_out, "dp", dp_size, bit)
    near[z_near], near[x_bit] = lax.optimization_barrier((near[z_near], near[x_bit]))
    near[z_near | x_bit] = hop(near[z_near], "dp", dp_size, x_bit)
    near[z_far], before = lax.optimization_barrier((near[z_far], before))
    near[z_both] = hop(near[z_far], "dp", dp_size, z_near)
    next_sent, near[z_near | x_bit] = lax.optimization_barrier(
        (near[z_far], near[z_near | x_bit])
    )
    near[z_far | x_bit] = hop(next_sent, "dp", dp_size, x_bit)
    near[z_both | x_bit] = hop(near[z_both], "dp", dp_size, x_bit)
    far = {}
    for group in (
        (0, z_near, x_bit, z_far),
        (z_near | x_bit, z_far | x_bit, z_both),
        (z_both | x_bit,),
    ):
        came = hop(jnp.stack([near[j] for j in group]), "dp", dp_size, 1)
        for k, j in enumerate(group):
            far[j] = came[k]
    shares = [near[2 * j] for j in range(HEADS)] + [far[2 * j] for j in range(HEADS)]
    gate_up_near = jnp.swapaxes(w_gate_up[0], 1, 2)

    info = jnp.stack([ctx, me >> 1, core, capacity[0, 0, 0], capacity[0, 0, 1]]).astype(jnp.int32)
    slots = PASS_SPECIALISTS * CAP
    attended, place, gate_values = pl.pallas_call(
        attend_kernel,
        out_shape=(
            jax.ShapeDtypeStruct((HEADS, token_count, HD), jnp.bfloat16),
            jax.ShapeDtypeStruct((token_count, slots), jnp.bfloat16),
            jax.ShapeDtypeStruct((token_count, PASS_SPECIALISTS), jnp.float32),
        ),
        in_specs=[pl.BlockSpec(memory_space=pltpu.SMEM)] + vmem(6),
        out_specs=tuple(vmem(3)),
        cost_estimate=pl.CostEstimate(
            flops=4 * HEADS * HD * 2 * token_count * token_count,
            bytes_accessed=6 * 2 * token_count * HEADS * HD,
            transcendentals=2 * HEADS * token_count * token_count,
        ),
        compiler_params=pltpu.CompilerParams(vmem_limit_bytes=16 * 2**20),
    )(
        info,
        query_vecs[0],
        key_vecs[0],
        value_vecs[0],
        before,
        expert_ids[0],
        route_gates[0],
    )
    attn_proj, chosen = pl.pallas_call(
        project_kernel,
        out_shape=(
            jax.ShapeDtypeStruct((token_count, width), jnp.bfloat16),
            jax.ShapeDtypeStruct((slots, width), jnp.bfloat16),
        ),
        in_specs=vmem(4 + 2 * HEADS),
        out_specs=tuple(vmem(2)),
        scratch_shapes=[pltpu.VMEM((token_count, width), jnp.float32)],
        cost_estimate=pl.CostEstimate(
            flops=2 * token_count * HEADS * HD * width,
            bytes_accessed=2 * HEADS * HD * width,
            transcendentals=0,
        ),
        compiler_params=pltpu.CompilerParams(vmem_limit_bytes=24 * 2**20),
    )(attended, residual[0], norm_gain[None], place, *shares)

    owners = expert_owner[:PASS_SPECIALISTS]
    differ = owners[0] ^ owners[1]
    branch = 0
    split_bit = 0
    for k in reversed(range(len(bits))):
        parted = (differ & bits[k]) != 0
        branch = jnp.where(parted, k, branch)
        split_bit = jnp.where(parted, bits[k], split_bit)
    same = split_bit == 0
    side = jnp.where(((me ^ owners[0]) & split_bit) == 0, 0, 1)
    units = w_down.shape[1]
    row_count = dp_size * CAP

    def dispatch(bit):
        rest = [b for b in bits if b != bit]

        def run(kept, sent):
            gate_up_far = hop(gate_up_near, "dp", dp_size, 1)
            down_far = hop(w_down[0], "dp", dp_size, 1)
            unit = jnp.concatenate([kept, hop(sent, "dp", dp_size, bit)], axis=0)
            return gather_rows(unit, rest, dp_size), gate_up_far, down_far

        return run

    def give_back(bit):
        rest = [b for b in bits if b != bit]

        def run(made, offset):
            unit = scatter_rows(made, rest, dp_size, offset)
            return unit[:CAP], hop(unit[CAP:], "dp", dp_size, bit)

        return run

    def one_pass(step, produced):
        local = jnp.where(same, step, side)
        sent_expert = jnp.where(same, step, 1 - side)
        owner = jnp.where(local == 0, owners[0], owners[1])
        offset = me ^ owner
        kept = jnp.where(local == 0, chosen[:CAP], chosen[CAP:])
        sent = jnp.where(sent_expert == 0, chosen[:CAP], chosen[CAP:])
        rows, gate_up_far, down_far = lax.switch(
            branch, [dispatch(bit) for bit in bits], kept, sent
        )
        made = pl.pallas_call(
            expert_kernel,
            out_shape=jax.ShapeDtypeStruct((row_count, width), jnp.bfloat16),
            in_specs=[pl.BlockSpec(memory_space=pltpu.SMEM)]
            + vmem(1)
            + [pl.BlockSpec(memory_space=pl.ANY)] * 4,
            out_specs=vmem(1)[0],
            scratch_shapes=[
                pltpu.VMEM((2, units, width), jnp.bfloat16),
                pltpu.VMEM((units, width), jnp.bfloat16),
                pltpu.VMEM((units, row_count), jnp.bfloat16),
                pltpu.SemaphoreType.DMA((2 * -(-units // 256) + 1,)),
            ],
            cost_estimate=pl.CostEstimate(
                flops=6 * row_count * units * width,
                bytes_accessed=6 * units * width,
                transcendentals=row_count * units,
            ),
            compiler_params=pltpu.CompilerParams(vmem_limit_bytes=52 * 2**20),
        )((offset & 1)[None], rows, gate_up_near, gate_up_far, w_down[0], down_far)
        own, other = lax.switch(branch, [give_back(bit) for bit in bits], made, offset)
        served = jnp.where((offset & bits[0]) == 0, own, other)
        first = jnp.where(same, served, jnp.where(local == 0, own, other))
        second = jnp.where(same, served, jnp.where(local == 0, other, own))
        return (
            jnp.where(same & (step != 0), produced[0], first),
            jnp.where(same & (step != 1), produced[1], second),
        )

    nothing = jnp.zeros((CAP, width), jnp.bfloat16)
    produced = lax.fori_loop(0, jnp.where(same, 2, 1), one_pass, (nothing, nothing))
    summed = 0.0
    for expert in range(PASS_SPECIALISTS):
        picked = jnp.dot(
            place[:, expert * CAP : (expert + 1) * CAP],
            produced[expert],
            preferred_element_type=jnp.float32,
        )
        summed = summed + gate_values[:, expert : expert + 1] * picked
    expert_sum = summed.astype(jnp.bfloat16)
    return (attn_proj[None], expert_sum[None])


def solution(mesh):
    placed = (
        P("dp", "ctx", None),
        P("dp", "ctx", None),
        P("dp", "ctx", None),
        P("dp", "ctx", None),
        P("dp", None),
        P(),
        P("dp", None, None, "ctx"),
        P("dp", "ctx", None),
        P("dp", "ctx", None),
        P("dp", "ctx", None),
        P("dp", "ctx", None),
        P(),
    )
    dp_size, ctx_size = mesh.shape["dp"], mesh.shape["ctx"]
    small = ctx_size == 2 and dp_size == 2 * HEADS
    return jax.shard_map(
        body_move_rows if small else body_move_weights,
        mesh=mesh,
        in_specs=placed,
        out_specs=(P("dp", "ctx", None), P("dp", "ctx", None)),
        check_vma=False,
    )
```

```python
import functools

import jax
import jax.numpy as jnp
from jax import lax
from jax.experimental import pallas as pl
from jax.experimental.pallas import tpu as pltpu
from jax.sharding import PartitionSpec as P

HEADS = 8
HD = 128
PASS_SPECIALISTS = 2
CAP = 24


EPSILON = 1e-06
LOWEST = -1e30


def broadcast(array, axis, root):
    mine = lax.axis_index(axis) == root
    return lax.psum(jnp.where(mine, array, jnp.zeros_like(array)), axis)


def hop(array, axis, size, bit):
    return lax.ppermute(array, axis, [(i, i ^ bit) for i in range(size)])


def route_slots(expert_ids, route_gates, capacity, expert):
    matches = expert_ids == expert
    routed = jnp.any(matches, axis=1)
    gate_value = jnp.sum(jnp.where(matches, route_gates, 0.0), axis=1)
    slot_rank = jnp.cumsum(routed.astype(jnp.int32)) - 1
    kept_mask = routed & (slot_rank < capacity[expert])
    return (slot_rank, kept_mask, gate_value)


def attend(queries, key_block, value_block, visible):
    width = key_block.shape[0]
    token_count = queries.shape[0]
    query_heads = queries.reshape(token_count, HEADS, HD)
    key_heads = key_block.reshape(width, HEADS, HD)
    value_heads = value_block.reshape(width, HEADS, HD)
    gating_logits = jnp.einsum(
        "qhd,khd->qhk", query_heads, key_heads, preferred_element_type=jnp.float32
    ) * HD ** (-0.5)
    gating_logits = jnp.where(visible[:, None, :], gating_logits, -jnp.inf)
    row_top = jnp.max(gating_logits, axis=-1)
    weights = jnp.exp(gating_logits - row_top[:, :, None])
    denominator = jnp.sum(weights, axis=-1)
    weighted = jnp.einsum(
        "qhk,khd->qhd",
        weights.astype(jnp.bfloat16),
        value_heads,
        preferred_element_type=jnp.float32,
    )
    attended = (weighted / denominator[:, :, None]).astype(jnp.bfloat16)
    return attended.reshape(token_count, HEADS * HD)


def feed_forward(rows, gate_up, down_part):
    gate_proj = jnp.dot(rows, gate_up[0], preferred_element_type=jnp.float32)
    up_proj = jnp.dot(rows, gate_up[1], preferred_element_type=jnp.float32)
    hidden = (jax.nn.silu(gate_proj) * up_proj).astype(jnp.bfloat16)
    return jnp.dot(hidden, down_part, preferred_element_type=jnp.float32).astype(jnp.bfloat16)


def normalise(attn_proj, residual, norm_gain):
    combined = residual.astype(jnp.float32) + attn_proj.astype(jnp.float32)
    return (
        combined
        * lax.rsqrt(jnp.mean(combined * combined, axis=-1, keepdims=True) + EPSILON)
        * norm_gain
    ).astype(jnp.bfloat16)


def pick_rows(routing, normed):
    slot_ids = jnp.arange(CAP)
    select = [
        (slot_rank[None, :] == slot_ids[:, None]) & kept_mask[None, :]
        for slot_rank, kept_mask, _ in routing
    ]
    select = jnp.concatenate(select, axis=0).astype(jnp.bfloat16)
    chosen = jnp.dot(select, normed, preferred_element_type=jnp.float32).astype(jnp.bfloat16)
    return chosen.reshape(PASS_SPECIALISTS, CAP, normed.shape[1])


def combine_rows(routing, produced):
    slot_ids = jnp.arange(CAP)
    summed = 0.0
    for expert in range(PASS_SPECIALISTS):
        slot_rank, kept_mask, gate_value = routing[expert]
        place = ((slot_rank[:, None] == slot_ids[None, :]) & kept_mask[:, None]).astype(
            jnp.bfloat16
        )
        picked = jnp.dot(place, produced[expert], preferred_element_type=jnp.float32)
        summed = summed + gate_value[:, None] * picked
    return summed.astype(jnp.bfloat16)


def body_move_weights(
    query_vecs,
    key_vecs,
    value_vecs,
    residual,
    w_out,
    norm_gain,
    w_gate_up,
    w_down,
    expert_ids,
    route_gates,
    capacity,
    expert_owner,
):
    token_count = query_vecs.shape[1]
    weights_in = []
    for expert in range(PASS_SPECIALISTS):
        weights_in.append(
            (
                broadcast(w_gate_up[0], "dp", expert_owner[expert]),
                broadcast(w_down[0], "dp", expert_owner[expert]),
            )
        )
    keys = lax.all_gather(key_vecs[0], "ctx", axis=0, tiled=True)
    values = lax.all_gather(value_vecs[0], "ctx", axis=0, tiled=True)
    first_row = lax.axis_index("ctx") * token_count
    query_pos = first_row + jnp.arange(token_count)
    visible = jnp.arange(keys.shape[0])[None, :] <= query_pos[:, None]
    attended = attend(query_vecs[0], keys, values, visible)
    projected = jnp.dot(
        attended,
        lax.all_gather(w_out, "dp", axis=0, tiled=True),
        preferred_element_type=jnp.float32,
    )
    attn_proj = projected.astype(jnp.bfloat16)
    normed = normalise(attn_proj, residual[0], norm_gain)
    routing = [
        route_slots(expert_ids[0], route_gates[0], capacity[0, 0], expert)
        for expert in range(PASS_SPECIALISTS)
    ]
    chosen = pick_rows(routing, normed)
    routed_rows = lax.all_gather(jnp.swapaxes(chosen, 0, 1), "ctx", axis=0, tiled=True)
    outputs = [
        feed_forward(routed_rows[:, expert], *weights_in[expert])
        for expert in range(PASS_SPECIALISTS)
    ]
    expert_out = lax.psum_scatter(
        jnp.stack(outputs, axis=1), "ctx", scatter_dimension=0, tiled=True
    )
    expert_sum = combine_rows(routing, [expert_out[:, e] for e in range(PASS_SPECIALISTS)])
    return (attn_proj[None], expert_sum[None])


def attend_kernel(info, query, key, value, before_both, ids, gates, attended, place, gate_values):
    token_count = query.shape[0]
    row = lax.broadcasted_iota(jnp.int32, (token_count, token_count), 0)
    col = lax.broadcasted_iota(jnp.int32, (token_count, token_count), 1)
    own_visible = col <= row
    before_visible = jnp.broadcast_to(info[0], (token_count, token_count)) == 1
    contract_last = (((1,), (1,)), ((), ()))
    for head in range(HEADS):
        span = slice(head * HD, (head + 1) * HD)
        heads = query[:, span]
        own = lax.dot_general(
            heads, key[:, span], contract_last, preferred_element_type=jnp.float32
        )
        before = lax.dot_general(
            heads, before_both[0, :, span], contract_last, preferred_element_type=jnp.float32
        )
        own = jnp.where(own_visible, own * HD ** (-0.5), -jnp.inf)
        before = jnp.where(before_visible, before * HD ** (-0.5), -jnp.inf)
        top = jnp.maximum(
            jnp.max(own, axis=1, keepdims=True), jnp.max(before, axis=1, keepdims=True)
        )
        own = jnp.exp(own - top)
        before = jnp.exp(before - top)
        total = jnp.sum(own, axis=1, keepdims=True) + jnp.sum(before, axis=1, keepdims=True)
        mixed = jnp.dot(
            own.astype(jnp.bfloat16), value[:, span], preferred_element_type=jnp.float32
        ) + jnp.dot(
            before.astype(jnp.bfloat16), before_both[1, :, span], preferred_element_type=jnp.float32
        )
        mixed = mixed / total
        swapped = pltpu.roll(mixed, HD // 2, 1)
        mixed = jnp.where(jnp.broadcast_to(info[2], mixed.shape) == 0, mixed, swapped)
        attended[head ^ info[1]] = mixed.astype(jnp.bfloat16)

    slots = PASS_SPECIALISTS * CAP
    lane = lax.broadcasted_iota(jnp.int32, (token_count, slots), 1)
    routed = jnp.zeros((token_count, slots), jnp.float32)
    limit = jnp.zeros((token_count, slots), jnp.int32)
    for expert in range(PASS_SPECIALISTS):
        matches = ids[...] == expert
        named = jnp.max(matches.astype(jnp.float32), axis=1, keepdims=True)
        gate_values[:, expert : expert + 1] = jnp.sum(
            jnp.where(matches, gates[...], 0.0), axis=1, keepdims=True
        )
        mine = (lane >= expert * CAP) & (lane < (expert + 1) * CAP)
        routed = jnp.where(mine, named, routed)
        limit = jnp.where(mine, info[3 + expert], limit)
    earlier = (col < row).astype(jnp.bfloat16)
    rank = jnp.dot(
        earlier, routed.astype(jnp.bfloat16), preferred_element_type=jnp.float32
    ).astype(jnp.int32)
    slot = jnp.where(lane >= CAP, lane - CAP, lane)
    place[...] = ((routed > 0.0) & (rank == slot) & (rank < limit)).astype(jnp.bfloat16)


def project_kernel(far_place, *refs):
    attended, residual, gain, place = refs[:4]
    near = refs[4 : 4 + HEADS]
    groups = refs[4 + HEADS : -3]
    far = [groups[group].at[k] for group, k in far_place]
    attn_proj, chosen, combined = refs[-3:]
    token_count, width = residual.shape
    tile = 512
    squares = jnp.zeros((token_count, 1), jnp.float32)
    for start in range(0, width, tile):
        span = slice(start, start + tile)
        total = jnp.zeros((token_count, tile), jnp.float32)
        for pair in range(0, HEADS, 2):
            left = jnp.concatenate([attended[pair], attended[pair + 1]], axis=1)
            right = jnp.concatenate(
                [near[pair][:, span], far[pair][:, span]]
                + [near[pair + 1][:, span], far[pair + 1][:, span]],
                axis=0,
            )
            total = total + jnp.dot(left, right, preferred_element_type=jnp.float32)
        rounded = total.astype(jnp.bfloat16)
        attn_proj[:, span] = rounded
        added = residual[:, span].astype(jnp.float32) + rounded.astype(jnp.float32)
        combined[:, span] = added
        squares = squares + jnp.sum(added * added, axis=1, keepdims=True)
    scale = lax.rsqrt(squares / width + EPSILON)
    for start in range(0, width, tile):
        span = slice(start, start + tile)
        normed = (combined[:, span] * scale * gain[:, span]).astype(jnp.bfloat16)
        chosen[:, span] = lax.dot_general(
            place[...], normed, (((0,), (0,)), ((), ())), preferred_element_type=jnp.float32
        ).astype(jnp.bfloat16)


def expert_kernel(other, rows, gate_up_near, gate_up_far, down_near, down_far, made, gate_up, down, hidden, sems):
    units = down.shape[0]
    starts = list(range(0, units, 256))

    def copies(gate_up_from, down_from):
        out = []
        for k, start in enumerate(starts):
            size = min(256, units - start)
            span = pl.ds(start, size)
            for part in range(2):
                out.append(
                    pltpu.make_async_copy(
                        gate_up_from.at[part, span], gate_up.at[part, span], sems.at[2 * k + part]
                    )
                )
        out.append(pltpu.make_async_copy(down_from, down, sems.at[2 * len(starts)]))
        return out

    @pl.when(other[0] == 0)
    def _():
        for copy in copies(gate_up_near, down_near):
            copy.start()

    @pl.when(other[0] != 0)
    def _():
        for copy in copies(gate_up_far, down_far):
            copy.start()

    arrived = copies(gate_up_near, down_near)
    contract_last = (((1,), (1,)), ((), ()))
    for k, start in enumerate(starts):
        size = min(256, units - start)
        span = slice(start, start + size)
        arrived[2 * k].wait()
        gate_proj = lax.dot_general(
            gate_up[0, span], rows[...], contract_last, preferred_element_type=jnp.float32
        )
        arrived[2 * k + 1].wait()
        up_proj = lax.dot_general(
            gate_up[1, span], rows[...], contract_last, preferred_element_type=jnp.float32
        )
        hidden[span] = (gate_proj / (1.0 + jnp.exp(-gate_proj)) * up_proj).astype(jnp.bfloat16)
    arrived[-1].wait()
    width = made.shape[1]
    contract_first = (((0,), (0,)), ((), ()))
    for start in range(0, width, 512):
        span = slice(start, start + 512)
        made[:, span] = lax.dot_general(
            hidden[...], down[:, span], contract_first, preferred_element_type=jnp.float32
        ).astype(jnp.bfloat16)


def gather_rows(kept, sent, first, bits, dp_size):
    second, last = bits
    unit = jnp.concatenate(
        [
            kept,
            hop(sent, "dp", dp_size, first),
            hop(kept, "dp", dp_size, second),
            hop(sent, "dp", dp_size, first | second),
        ],
        axis=0,
    )
    half = unit.shape[1] // 2
    left, right = unit[:, :half], unit[:, half:]
    left = jnp.stack([left, hop(left, "dp", dp_size, last)])
    right = jnp.stack([right, hop(right, "ctx", 2, 1)])
    left = jnp.stack([left, hop(left, "ctx", 2, 1)])
    right = jnp.stack([right, hop(right, "dp", dp_size, last)], axis=1)
    rows = jnp.concatenate([left, right], axis=-1)
    return rows.reshape(-1, rows.shape[-1])


def scatter_rows(rows, first, bits, dp_size, offset, other_offset):
    second, last = bits
    half = rows.shape[1] // 2
    rows = rows.reshape(2, 2, -1, rows.shape[1])
    left, right = rows[..., :half], rows[..., half:]

    def add(kept, came):
        return (kept.astype(jnp.float32) + came.astype(jnp.float32)).astype(jnp.bfloat16)

    near = (offset & last) == 0
    left = add(left[0], hop(left[1], "ctx", 2, 1))
    right = jnp.where(near, right[:, 0], hop(right[:, 1], "dp", dp_size, last))
    left = jnp.where(near, left[0], hop(left[1], "dp", dp_size, last))
    right = add(right[0], hop(right[1], "ctx", 2, 1))
    unit = jnp.concatenate([left, right], axis=-1)
    here, across, beside, beyond = jnp.split(unit, 4, axis=0)
    across = hop(across, "dp", dp_size, first)
    beside = hop(beside, "dp", dp_size, second)
    beyond = hop(beyond, "dp", dp_size, first | second)
    return (
        jnp.where((offset & second) == 0, here, beside),
        jnp.where((other_offset & second) == 0, across, beyond),
    )


def vmem(count):
    return [pl.BlockSpec(memory_space=pltpu.VMEM)] * count


def body_move_rows(
    query_vecs,
    key_vecs,
    value_vecs,
    residual,
    w_out,
    norm_gain,
    w_gate_up,
    w_down,
    expert_ids,
    route_gates,
    capacity,
    expert_owner,
):
    token_count = query_vecs.shape[1]
    width = residual.shape[2]
    dp_size = lax.axis_size("dp")
    me = lax.axis_index("dp")
    core = me & 1
    ctx = lax.axis_index("ctx")
    bits = [1 << k for k in reversed(range(1, dp_size.bit_length() - 1))]

    info = jnp.stack([ctx, me >> 1, core, capacity[0, 0, 0], capacity[0, 0, 1]]).astype(jnp.int32)
    before = lax.ppermute(jnp.stack([key_vecs[0], value_vecs[0]]), "ctx", [(0, 1)])
    z_far, z_near, x_bit = bits
    z_both = z_far | z_near
    near = {0: w_out}
    for bit in (z_near, x_bit, z_far):
        near[bit] = hop(w_out, "dp", dp_size, bit)
    near[z_near], near[x_bit], info, ids, gates = lax.optimization_barrier(
        (near[z_near], near[x_bit], info, expert_ids[0], route_gates[0])
    )
    near[z_near | x_bit] = hop(near[z_near], "dp", dp_size, x_bit)
    near[z_both] = hop(near[z_far], "dp", dp_size, z_near)
    next_sent, near[z_near | x_bit], before = lax.optimization_barrier(
        (near[z_far], near[z_near | x_bit], before)
    )
    near[z_far | x_bit] = hop(next_sent, "dp", dp_size, x_bit)
    slots = PASS_SPECIALISTS * CAP
    attended, place, gate_values = pl.pallas_call(
        attend_kernel,
        out_shape=(
            jax.ShapeDtypeStruct((HEADS, token_count, HD), jnp.bfloat16),
            jax.ShapeDtypeStruct((token_count, slots), jnp.bfloat16),
            jax.ShapeDtypeStruct((token_count, PASS_SPECIALISTS), jnp.float32),
        ),
        in_specs=[pl.BlockSpec(memory_space=pltpu.SMEM)] + vmem(6),
        out_specs=tuple(vmem(3)),
        cost_estimate=pl.CostEstimate(
            flops=64 * HEADS * HD * 2 * token_count * token_count,
            bytes_accessed=6 * 2 * token_count * HEADS * HD,
            transcendentals=2 * HEADS * token_count * token_count,
        ),
        compiler_params=pltpu.CompilerParams(vmem_limit_bytes=16 * 2**20),
    )(
        info,
        query_vecs[0],
        key_vecs[0],
        value_vecs[0],
        before,
        ids,
        gates,
    )
    near[z_both], near[z_far | x_bit], attended = lax.optimization_barrier(
        (near[z_both], near[z_far | x_bit], attended)
    )
    near[z_both | x_bit] = hop(near[z_both], "dp", dp_size, x_bit)
    far = [
        hop(jnp.stack([near[j] for j in group]), "dp", dp_size, 1)
        for group in (
            (0, z_near, x_bit, z_far),
            (z_near | x_bit, z_far | x_bit, z_both),
            (z_both | x_bit,),
        )
    ]
    far_place = {
        0: (0, 0),
        z_near: (0, 1),
        x_bit: (0, 2),
        z_far: (0, 3),
        z_near | x_bit: (1, 0),
        z_far | x_bit: (1, 1),
        z_both: (1, 2),
        z_both | x_bit: (2, 0),
    }
    far_place = [far_place[2 * j] for j in range(HEADS)]
    shares = [near[2 * j] for j in range(HEADS)] + far
    gate_up_near = jnp.swapaxes(w_gate_up[0], 1, 2)

    attn_proj, chosen = pl.pallas_call(
        functools.partial(project_kernel, far_place),
        out_shape=(
            jax.ShapeDtypeStruct((token_count, width), jnp.bfloat16),
            jax.ShapeDtypeStruct((slots, width), jnp.bfloat16),
        ),
        in_specs=vmem(4 + len(shares)),
        out_specs=tuple(vmem(2)),
        scratch_shapes=[pltpu.VMEM((token_count, width), jnp.float32)],
        cost_estimate=pl.CostEstimate(
            flops=2 * token_count * HEADS * HD * width,
            bytes_accessed=2 * HEADS * HD * width,
            transcendentals=0,
        ),
        compiler_params=pltpu.CompilerParams(vmem_limit_bytes=24 * 2**20),
    )(attended, residual[0], norm_gain[None], place, *shares)

    owners = expert_owner[:PASS_SPECIALISTS]
    differ = owners[0] ^ owners[1]
    branch = 0
    split_bit = 0
    for k in reversed(range(len(bits))):
        parted = (differ & bits[k]) != 0
        branch = jnp.where(parted, k, branch)
        split_bit = jnp.where(parted, bits[k], split_bit)
    same = split_bit == 0
    side = jnp.where(((me ^ owners[0]) & split_bit) == 0, 0, 1)
    units = w_down.shape[1]
    row_count = dp_size * CAP

    def dispatch(bit):
        rest = [b for b in bits if b != bit]

        def run(kept, sent):
            gate_up_far = hop(gate_up_near, "dp", dp_size, 1)
            down_far = hop(w_down[0], "dp", dp_size, 1)
            rows = gather_rows(kept, sent, bit, rest, dp_size)
            return rows, gate_up_far, down_far

        return run

    def give_back(bit):
        rest = [b for b in bits if b != bit]

        def run(made, offset, other_offset):
            return scatter_rows(made, bit, rest, dp_size, offset, other_offset)

        return run

    def one_pass(step, produced):
        local = jnp.where(same, step, side)
        sent_expert = jnp.where(same, step, 1 - side)
        owner = jnp.where(local == 0, owners[0], owners[1])
        offset = me ^ owner
        other_offset = me ^ jnp.where(sent_expert == 0, owners[0], owners[1])
        kept = jnp.where(local == 0, chosen[:CAP], chosen[CAP:])
        sent = jnp.where(sent_expert == 0, chosen[:CAP], chosen[CAP:])
        rows, gate_up_far, down_far = lax.switch(
            branch, [dispatch(bit) for bit in bits], kept, sent
        )
        made = pl.pallas_call(
            expert_kernel,
            out_shape=jax.ShapeDtypeStruct((row_count, width), jnp.bfloat16),
            in_specs=[pl.BlockSpec(memory_space=pltpu.SMEM)]
            + vmem(1)
            + [pl.BlockSpec(memory_space=pl.ANY)] * 4,
            out_specs=vmem(1)[0],
            scratch_shapes=[
                pltpu.VMEM((2, units, width), jnp.bfloat16),
                pltpu.VMEM((units, width), jnp.bfloat16),
                pltpu.VMEM((units, row_count), jnp.bfloat16),
                pltpu.SemaphoreType.DMA((2 * -(-units // 256) + 1,)),
            ],
            cost_estimate=pl.CostEstimate(
                flops=6 * row_count * units * width,
                bytes_accessed=6 * units * width,
                transcendentals=row_count * units,
            ),
            compiler_params=pltpu.CompilerParams(vmem_limit_bytes=30 * 2**20),
        )((offset & 1)[None], rows, gate_up_near, gate_up_far, w_down[0], down_far)
        own, other = lax.switch(branch, [give_back(bit) for bit in bits], made, offset, other_offset)
        served = jnp.where((offset & bits[0]) == 0, own, other)
        first = jnp.where(same, served, jnp.where(local == 0, own, other))
        second = jnp.where(same, served, jnp.where(local == 0, other, own))
        return (
            jnp.where(same & (step != 0), produced[0], first),
            jnp.where(same & (step != 1), produced[1], second),
        )

    nothing = jnp.zeros((CAP, width), jnp.bfloat16)
    produced = lax.fori_loop(0, jnp.where(same, 2, 1), one_pass, (nothing, nothing))
    summed = 0.0
    for expert in range(PASS_SPECIALISTS):
        picked = jnp.dot(
            place[:, expert * CAP : (expert + 1) * CAP],
            produced[expert],
            preferred_element_type=jnp.float32,
        )
        summed = summed + gate_values[:, expert : expert + 1] * picked
    expert_sum = summed.astype(jnp.bfloat16)
    return (attn_proj[None], expert_sum[None])


def solution(mesh):
    placed = (
        P("dp", "ctx", None),
        P("dp", "ctx", None),
        P("dp", "ctx", None),
        P("dp", "ctx", None),
        P("dp", None),
        P(),
        P("dp", None, None, "ctx"),
        P("dp", "ctx", None),
        P("dp", "ctx", None),
        P("dp", "ctx", None),
        P("dp", "ctx", None),
        P(),
    )
    dp_size, ctx_size = mesh.shape["dp"], mesh.shape["ctx"]
    small = ctx_size == 2 and dp_size == 2 * HEADS
    return jax.shard_map(
        body_move_rows if small else body_move_weights,
        mesh=mesh,
        in_specs=placed,
        out_specs=(P("dp", "ctx", None), P("dp", "ctx", None)),
        check_vma=False,
    )
```

```python
import functools

import jax
import jax.numpy as jnp
from jax import lax
from jax.experimental import pallas as pl
from jax.experimental.pallas import tpu as pltpu
from jax.sharding import PartitionSpec as P

HEADS = 8
HD = 128
PASS_SPECIALISTS = 2
CAP = 24


EPSILON = 1e-06
LOWEST = -1e30


def broadcast(array, axis, root):
    mine = lax.axis_index(axis) == root
    return lax.psum(jnp.where(mine, array, jnp.zeros_like(array)), axis)


def hop(array, axis, size, bit):
    return lax.ppermute(array, axis, [(i, i ^ bit) for i in range(size)])


def route_slots(expert_ids, route_gates, capacity, expert):
    matches = expert_ids == expert
    routed = jnp.any(matches, axis=1)
    gate_value = jnp.sum(jnp.where(matches, route_gates, 0.0), axis=1)
    slot_rank = jnp.cumsum(routed.astype(jnp.int32)) - 1
    kept_mask = routed & (slot_rank < capacity[expert])
    return (slot_rank, kept_mask, gate_value)


def attend(queries, key_block, value_block, visible):
    width = key_block.shape[0]
    token_count = queries.shape[0]
    query_heads = queries.reshape(token_count, HEADS, HD)
    key_heads = key_block.reshape(width, HEADS, HD)
    value_heads = value_block.reshape(width, HEADS, HD)
    gating_logits = jnp.einsum(
        "qhd,khd->qhk", query_heads, key_heads, preferred_element_type=jnp.float32
    ) * HD ** (-0.5)
    gating_logits = jnp.where(visible[:, None, :], gating_logits, -jnp.inf)
    row_top = jnp.max(gating_logits, axis=-1)
    weights = jnp.exp(gating_logits - row_top[:, :, None])
    denominator = jnp.sum(weights, axis=-1)
    weighted = jnp.einsum(
        "qhk,khd->qhd",
        weights.astype(jnp.bfloat16),
        value_heads,
        preferred_element_type=jnp.float32,
    )
    attended = (weighted / denominator[:, :, None]).astype(jnp.bfloat16)
    return attended.reshape(token_count, HEADS * HD)


def feed_forward(rows, gate_up, down_part):
    gate_proj = jnp.dot(rows, gate_up[0], preferred_element_type=jnp.float32)
    up_proj = jnp.dot(rows, gate_up[1], preferred_element_type=jnp.float32)
    hidden = (jax.nn.silu(gate_proj) * up_proj).astype(jnp.bfloat16)
    return jnp.dot(hidden, down_part, preferred_element_type=jnp.float32).astype(jnp.bfloat16)


def normalise(attn_proj, residual, norm_gain):
    combined = residual.astype(jnp.float32) + attn_proj.astype(jnp.float32)
    return (
        combined
        * lax.rsqrt(jnp.mean(combined * combined, axis=-1, keepdims=True) + EPSILON)
        * norm_gain
    ).astype(jnp.bfloat16)


def pick_rows(routing, normed):
    slot_ids = jnp.arange(CAP)
    select = [
        (slot_rank[None, :] == slot_ids[:, None]) & kept_mask[None, :]
        for slot_rank, kept_mask, _ in routing
    ]
    select = jnp.concatenate(select, axis=0).astype(jnp.bfloat16)
    chosen = jnp.dot(select, normed, preferred_element_type=jnp.float32).astype(jnp.bfloat16)
    return chosen.reshape(PASS_SPECIALISTS, CAP, normed.shape[1])


def combine_rows(routing, produced):
    slot_ids = jnp.arange(CAP)
    summed = 0.0
    for expert in range(PASS_SPECIALISTS):
        slot_rank, kept_mask, gate_value = routing[expert]
        place = ((slot_rank[:, None] == slot_ids[None, :]) & kept_mask[:, None]).astype(
            jnp.bfloat16
        )
        picked = jnp.dot(place, produced[expert], preferred_element_type=jnp.float32)
        summed = summed + gate_value[:, None] * picked
    return summed.astype(jnp.bfloat16)


def body_move_weights(
    query_vecs,
    key_vecs,
    value_vecs,
    residual,
    w_out,
    norm_gain,
    w_gate_up,
    w_down,
    expert_ids,
    route_gates,
    capacity,
    expert_owner,
):
    token_count = query_vecs.shape[1]
    weights_in = []
    for expert in range(PASS_SPECIALISTS):
        weights_in.append(
            (
                broadcast(w_gate_up[0], "dp", expert_owner[expert]),
                broadcast(w_down[0], "dp", expert_owner[expert]),
            )
        )
    keys = lax.all_gather(key_vecs[0], "ctx", axis=0, tiled=True)
    values = lax.all_gather(value_vecs[0], "ctx", axis=0, tiled=True)
    first_row = lax.axis_index("ctx") * token_count
    query_pos = first_row + jnp.arange(token_count)
    visible = jnp.arange(keys.shape[0])[None, :] <= query_pos[:, None]
    attended = attend(query_vecs[0], keys, values, visible)
    projected = jnp.dot(
        attended,
        lax.all_gather(w_out, "dp", axis=0, tiled=True),
        preferred_element_type=jnp.float32,
    )
    attn_proj = projected.astype(jnp.bfloat16)
    normed = normalise(attn_proj, residual[0], norm_gain)
    routing = [
        route_slots(expert_ids[0], route_gates[0], capacity[0, 0], expert)
        for expert in range(PASS_SPECIALISTS)
    ]
    chosen = pick_rows(routing, normed)
    routed_rows = lax.all_gather(jnp.swapaxes(chosen, 0, 1), "ctx", axis=0, tiled=True)
    outputs = [
        feed_forward(routed_rows[:, expert], *weights_in[expert])
        for expert in range(PASS_SPECIALISTS)
    ]
    expert_out = lax.psum_scatter(
        jnp.stack(outputs, axis=1), "ctx", scatter_dimension=0, tiled=True
    )
    expert_sum = combine_rows(routing, [expert_out[:, e] for e in range(PASS_SPECIALISTS)])
    return (attn_proj[None], expert_sum[None])


def attend_kernel(info, query, key, value, before_both, ids, gates, attended, place, gate_values):
    token_count = query.shape[0]
    row = lax.broadcasted_iota(jnp.int32, (token_count, token_count), 0)
    col = lax.broadcasted_iota(jnp.int32, (token_count, token_count), 1)
    own_visible = col <= row
    before_visible = jnp.broadcast_to(info[0], (token_count, token_count)) == 1
    contract_last = (((1,), (1,)), ((), ()))
    for head in range(HEADS):
        span = slice(head * HD, (head + 1) * HD)
        heads = query[:, span]
        own = lax.dot_general(
            heads, key[:, span], contract_last, preferred_element_type=jnp.float32
        )
        before = lax.dot_general(
            heads, before_both[0, :, span], contract_last, preferred_element_type=jnp.float32
        )
        own = jnp.where(own_visible, own * HD ** (-0.5), -jnp.inf)
        before = jnp.where(before_visible, before * HD ** (-0.5), -jnp.inf)
        top = jnp.maximum(
            jnp.max(own, axis=1, keepdims=True), jnp.max(before, axis=1, keepdims=True)
        )
        own = jnp.exp(own - top)
        before = jnp.exp(before - top)
        total = jnp.sum(own, axis=1, keepdims=True) + jnp.sum(before, axis=1, keepdims=True)
        mixed = jnp.dot(
            own.astype(jnp.bfloat16), value[:, span], preferred_element_type=jnp.float32
        ) + jnp.dot(
            before.astype(jnp.bfloat16), before_both[1, :, span], preferred_element_type=jnp.float32
        )
        mixed = mixed / total
        swapped = pltpu.roll(mixed, HD // 2, 1)
        mixed = jnp.where(jnp.broadcast_to(info[2], mixed.shape) == 0, mixed, swapped)
        attended[head ^ info[1]] = mixed.astype(jnp.bfloat16)

    slot = lax.broadcasted_iota(jnp.int32, (token_count, CAP), 1)
    earlier = (col < row).astype(jnp.bfloat16)
    for k in range(PASS_SPECIALISTS):
        matches = ids[...] == info[3 + 2 * k]
        named = jnp.max(matches.astype(jnp.float32), axis=1, keepdims=True)
        gate_values[:, k : k + 1] = jnp.sum(
            jnp.where(matches, gates[...], 0.0), axis=1, keepdims=True
        )
        routed = jnp.broadcast_to(named, (token_count, CAP))
        rank = jnp.dot(
            earlier, routed.astype(jnp.bfloat16), preferred_element_type=jnp.float32
        ).astype(jnp.int32)
        kept = (routed > 0.0) & (rank == slot) & (rank < info[4 + 2 * k])
        place[k] = kept.astype(jnp.bfloat16)


def project_kernel(far_place, same, attended, residual, gain, place, *refs):
    near = refs[:HEADS]
    groups = refs[HEADS:-5]
    attn_proj, kept, sent, second, combined = refs[-5:]
    far = [groups[group].at[k] for group, k in far_place]
    token_count, width = residual.shape
    tile = 512
    squares = jnp.zeros((token_count, 1), jnp.float32)
    for start in range(0, width, tile):
        span = slice(start, start + tile)
        total = jnp.zeros((token_count, tile), jnp.float32)
        for pair in range(0, HEADS, 2):
            left = jnp.concatenate([attended[pair], attended[pair + 1]], axis=1)
            right = jnp.concatenate(
                [near[pair][:, span], far[pair][:, span]]
                + [near[pair + 1][:, span], far[pair + 1][:, span]],
                axis=0,
            )
            total = total + jnp.dot(left, right, preferred_element_type=jnp.float32)
        rounded = total.astype(jnp.bfloat16)
        attn_proj[:, span] = rounded
        added = residual[:, span].astype(jnp.float32) + rounded.astype(jnp.float32)
        combined[:, span] = added
        squares = squares + jnp.sum(added * added, axis=1, keepdims=True)
    scale = lax.rsqrt(squares / width + EPSILON)
    contract_first = (((0,), (0,)), ((), ()))
    for start in range(0, width, tile):
        span = slice(start, start + tile)
        normed = (combined[:, span] * scale * gain[:, span]).astype(jnp.bfloat16)
        rows = [
            lax.dot_general(place[k], normed, contract_first, preferred_element_type=jnp.float32)
            for k in range(PASS_SPECIALISTS)
        ]
        kept[:, span] = rows[0].astype(jnp.bfloat16)
        second[:, span] = rows[1].astype(jnp.bfloat16)
        use_first = jnp.broadcast_to(same[0], rows[0].shape) != 0
        sent[:, span] = jnp.where(use_first, rows[0], rows[1]).astype(jnp.bfloat16)


def combine_kernel(flags, own, other, last_own, last_other, place, gate_values, out):
    width = own.shape[1]
    for start in range(0, width, 512):
        span = slice(start, start + 512)
        shape = (own.shape[0], 512)
        same = jnp.broadcast_to(flags[0], shape) != 0
        first_here = jnp.broadcast_to(flags[1], shape) != 0
        second_here = jnp.broadcast_to(flags[2], shape) != 0
        near, far = own[:, span].astype(jnp.float32), other[:, span].astype(jnp.float32)
        last = jnp.where(
            first_here,
            last_own[:, span].astype(jnp.float32),
            last_other[:, span].astype(jnp.float32),
        )
        first = jnp.where(same, last, near)
        second = jnp.where(same, jnp.where(second_here, near, far), far)
        total = 0.0
        for k, rows in enumerate((first, second)):
            picked = jnp.dot(
                place[k], rows.astype(jnp.bfloat16), preferred_element_type=jnp.float32
            )
            total = total + gate_values[:, k : k + 1] * picked
        out[:, span] = total.astype(jnp.bfloat16)


def expert_kernel(other, rows, gate_up_near, gate_up_far, down_near, down_far, made, gate_up, down, hidden, sems):
    units = down.shape[0]
    starts = list(range(0, units, 256))

    def copies(gate_up_from, down_from):
        out = []
        for k, start in enumerate(starts):
            size = min(256, units - start)
            span = pl.ds(start, size)
            for part in range(2):
                out.append(
                    pltpu.make_async_copy(
                        gate_up_from.at[part, span], gate_up.at[part, span], sems.at[2 * k + part]
                    )
                )
        out.append(pltpu.make_async_copy(down_from, down, sems.at[2 * len(starts)]))
        return out

    @pl.when(other[0] == 0)
    def _():
        for copy in copies(gate_up_near, down_near):
            copy.start()

    @pl.when(other[0] != 0)
    def _():
        for copy in copies(gate_up_far, down_far):
            copy.start()

    arrived = copies(gate_up_near, down_near)
    contract_last = (((1,), (1,)), ((), ()))
    for k, start in enumerate(starts):
        size = min(256, units - start)
        span = slice(start, start + size)
        arrived[2 * k].wait()
        gate_proj = lax.dot_general(
            gate_up[0, span], rows[...], contract_last, preferred_element_type=jnp.float32
        )
        arrived[2 * k + 1].wait()
        up_proj = lax.dot_general(
            gate_up[1, span], rows[...], contract_last, preferred_element_type=jnp.float32
        )
        hidden[span] = (gate_proj / (1.0 + jnp.exp(-gate_proj)) * up_proj).astype(jnp.bfloat16)
    arrived[-1].wait()
    width = made.shape[1]
    contract_first = (((0,), (0,)), ((), ()))
    for start in range(0, width, 512):
        span = slice(start, start + 512)
        made[:, span] = lax.dot_general(
            hidden[...], down[:, span], contract_first, preferred_element_type=jnp.float32
        ).astype(jnp.bfloat16)


def gather_rows(kept, sent, first, bits, dp_size):
    second, last = bits
    unit = jnp.concatenate(
        [
            kept,
            hop(sent, "dp", dp_size, first),
            hop(kept, "dp", dp_size, second),
            hop(sent, "dp", dp_size, first | second),
        ],
        axis=0,
    )
    half = unit.shape[1] // 2
    left, right = unit[:, :half], unit[:, half:]
    left = jnp.stack([left, hop(left, "dp", dp_size, last)])
    right = jnp.stack([right, hop(right, "ctx", 2, 1)])
    left = jnp.stack([left, hop(left, "ctx", 2, 1)])
    right = jnp.stack([right, hop(right, "dp", dp_size, last)], axis=1)
    rows = jnp.concatenate([left, right], axis=-1)
    return rows.reshape(-1, rows.shape[-1])


def scatter_rows(rows, first, bits, dp_size, offset, other_offset):
    second, last = bits
    half = rows.shape[1] // 2
    rows = rows.reshape(2, 2, -1, rows.shape[1])
    left, right = rows[..., :half], rows[..., half:]

    def add(kept, came):
        return (kept.astype(jnp.float32) + came.astype(jnp.float32)).astype(jnp.bfloat16)

    near = (offset & last) == 0
    left = add(left[0], hop(left[1], "ctx", 2, 1))
    right = jnp.where(near, right[:, 0], hop(right[:, 1], "dp", dp_size, last))
    left = jnp.where(near, left[0], hop(left[1], "dp", dp_size, last))
    right = add(right[0], hop(right[1], "ctx", 2, 1))
    unit = jnp.concatenate([left, right], axis=-1)
    here, across, beside, beyond = lax.optimization_barrier(jnp.split(unit, 4, axis=0))
    across = hop(across, "dp", dp_size, first)
    beside = hop(beside, "dp", dp_size, second)
    beyond = hop(beyond, "dp", dp_size, first | second)
    return (
        jnp.where((offset & second) == 0, here, beside),
        jnp.where((other_offset & second) == 0, across, beyond),
    )


def vmem(count):
    return [pl.BlockSpec(memory_space=pltpu.VMEM)] * count


def body_move_rows(
    query_vecs,
    key_vecs,
    value_vecs,
    residual,
    w_out,
    norm_gain,
    w_gate_up,
    w_down,
    expert_ids,
    route_gates,
    capacity,
    expert_owner,
):
    token_count = query_vecs.shape[1]
    width = residual.shape[2]
    dp_size = lax.axis_size("dp")
    me = lax.axis_index("dp")
    core = me & 1
    ctx = lax.axis_index("ctx")
    bits = [1 << k for k in reversed(range(1, dp_size.bit_length() - 1))]

    owners = expert_owner[:PASS_SPECIALISTS]
    differ = owners[0] ^ owners[1]
    branch = 0
    split_bit = 0
    for k in reversed(range(len(bits))):
        parted = (differ & bits[k]) != 0
        branch = jnp.where(parted, k, branch)
        split_bit = jnp.where(parted, bits[k], split_bit)
    same = split_bit == 0
    swapped = ((me ^ owners[0]) & split_bit) != 0
    offset = me ^ jnp.where(swapped, owners[1], owners[0])
    second_offset = me ^ jnp.where(swapped, owners[0], owners[1])
    other_offset = jnp.where(same, offset, second_offset)
    first_expert = swapped.astype(jnp.int32)
    caps = capacity[0, 0]
    info = jnp.stack(
        [
            ctx,
            me >> 1,
            core,
            first_expert,
            jnp.where(swapped, caps[1], caps[0]),
            1 - first_expert,
            jnp.where(swapped, caps[0], caps[1]),
        ]
    ).astype(jnp.int32)
    flags = jnp.stack(
        [same, (offset & bits[0]) == 0, (second_offset & bits[0]) == 0]
    ).astype(jnp.int32)
    passes = jnp.where(same, 2, 1)
    before = lax.ppermute(jnp.stack([key_vecs[0], value_vecs[0]]), "ctx", [(0, 1)])
    z_far, z_near, x_bit = bits
    z_both = z_far | z_near
    near = {0: w_out}
    for bit in (z_near, x_bit, z_far):
        near[bit] = hop(w_out, "dp", dp_size, bit)
    (
        near[z_near],
        near[x_bit],
        near[z_far],
        info,
        flags,
        passes,
        branch,
        offset,
        second_offset,
        other_offset,
        ids,
        gates,
    ) = lax.optimization_barrier(
        (
            near[z_near],
            near[x_bit],
            near[z_far],
            info,
            flags,
            passes,
            branch,
            offset,
            second_offset,
            other_offset,
            expert_ids[0],
            route_gates[0],
        )
    )
    near[z_near | x_bit] = hop(near[z_near], "dp", dp_size, x_bit)
    near[z_both] = hop(near[z_far], "dp", dp_size, z_near)
    near[z_far | x_bit] = hop(near[z_far], "dp", dp_size, x_bit)
    before, near[z_near | x_bit] = lax.optimization_barrier((before, near[z_near | x_bit]))
    attended, place, gate_values = pl.pallas_call(
        attend_kernel,
        out_shape=(
            jax.ShapeDtypeStruct((HEADS, token_count, HD), jnp.bfloat16),
            jax.ShapeDtypeStruct((PASS_SPECIALISTS, token_count, CAP), jnp.bfloat16),
            jax.ShapeDtypeStruct((token_count, PASS_SPECIALISTS), jnp.float32),
        ),
        in_specs=[pl.BlockSpec(memory_space=pltpu.SMEM)] + vmem(6),
        out_specs=tuple(vmem(3)),
        cost_estimate=pl.CostEstimate(
            flops=64 * HEADS * HD * 2 * token_count * token_count,
            bytes_accessed=6 * 2 * token_count * HEADS * HD,
            transcendentals=2 * HEADS * token_count * token_count,
        ),
        compiler_params=pltpu.CompilerParams(vmem_limit_bytes=8 * 2**20),
    )(
        info,
        query_vecs[0],
        key_vecs[0],
        value_vecs[0],
        before,
        ids,
        gates,
    )
    near[z_both], attended = lax.optimization_barrier((near[z_both], attended))
    near[z_both | x_bit] = hop(near[z_both], "dp", dp_size, x_bit)
    far = [
        hop(jnp.stack([near[j] for j in group]), "dp", dp_size, 1)
        for group in (
            (0, z_near, x_bit, z_far),
            (z_near | x_bit, z_both),
            (z_far | x_bit, z_both | x_bit),
        )
    ]
    far_place = {
        0: (0, 0),
        z_near: (0, 1),
        x_bit: (0, 2),
        z_far: (0, 3),
        z_near | x_bit: (1, 0),
        z_both: (1, 1),
        z_far | x_bit: (2, 0),
        z_both | x_bit: (2, 1),
    }
    far_place = [far_place[2 * j] for j in range(HEADS)]
    shares = [near[2 * j] for j in range(HEADS)] + far
    gate_up_near = jnp.swapaxes(w_gate_up[0], 1, 2)

    some_rows = jax.ShapeDtypeStruct((CAP, width), jnp.bfloat16)
    attn_proj, kept, sent, second = pl.pallas_call(
        functools.partial(project_kernel, far_place),
        out_shape=(
            jax.ShapeDtypeStruct((token_count, width), jnp.bfloat16),
            some_rows,
            some_rows,
            some_rows,
        ),
        in_specs=[pl.BlockSpec(memory_space=pltpu.SMEM)] + vmem(4 + len(shares)),
        out_specs=tuple(vmem(4)),
        scratch_shapes=[pltpu.VMEM((token_count, width), jnp.float32)],
        cost_estimate=pl.CostEstimate(
            flops=2 * token_count * HEADS * HD * width,
            bytes_accessed=2 * HEADS * HD * width,
            transcendentals=0,
        ),
        compiler_params=pltpu.CompilerParams(vmem_limit_bytes=16 * 2**20),
    )(flags, attended, residual[0], norm_gain[None], place, *shares)

    units = w_down.shape[1]
    row_count = dp_size * CAP

    def dispatch(bit):
        rest = [b for b in bits if b != bit]

        def run(kept, sent):
            gate_up_far = hop(gate_up_near, "dp", dp_size, 1)
            down_far = hop(w_down[0], "dp", dp_size, 1)
            rows = gather_rows(kept, sent, bit, rest, dp_size)
            return rows, gate_up_far, down_far

        return run

    def give_back(bit):
        rest = [b for b in bits if b != bit]

        def run(made, offset, other_offset):
            return scatter_rows(made, bit, rest, dp_size, offset, other_offset)

        return run

    def one_pass(_, carried):
        kept, sent, offset, other_offset, last_own, last_other, _, _ = carried
        rows, gate_up_far, down_far = lax.switch(
            branch, [dispatch(bit) for bit in bits], kept, sent
        )
        made = pl.pallas_call(
            expert_kernel,
            out_shape=jax.ShapeDtypeStruct((row_count, width), jnp.bfloat16),
            in_specs=[pl.BlockSpec(memory_space=pltpu.SMEM)]
            + vmem(1)
            + [pl.BlockSpec(memory_space=pl.ANY)] * 4,
            out_specs=vmem(1)[0],
            scratch_shapes=[
                pltpu.VMEM((2, units, width), jnp.bfloat16),
                pltpu.VMEM((units, width), jnp.bfloat16),
                pltpu.VMEM((units, row_count), jnp.bfloat16),
                pltpu.SemaphoreType.DMA((2 * -(-units // 256) + 1,)),
            ],
            cost_estimate=pl.CostEstimate(
                flops=6 * row_count * units * width,
                bytes_accessed=6 * units * width,
                transcendentals=row_count * units,
            ),
            compiler_params=pltpu.CompilerParams(vmem_limit_bytes=22 * 2**20),
        )((offset & 1)[None], rows, gate_up_near, gate_up_far, w_down[0], down_far)
        own, other = lax.switch(
            branch, [give_back(bit) for bit in bits], made, offset, other_offset
        )
        return second, second, second_offset, second_offset, own, other, last_own, last_other

    nothing = jnp.zeros((CAP, width), jnp.bfloat16)
    carried = (kept, sent, offset, other_offset) + (nothing,) * 4
    produced = lax.fori_loop(0, passes, one_pass, carried)[4:]
    expert_sum = pl.pallas_call(
        combine_kernel,
        out_shape=jax.ShapeDtypeStruct((token_count, width), jnp.bfloat16),
        in_specs=[pl.BlockSpec(memory_space=pltpu.SMEM)] + vmem(6),
        out_specs=vmem(1)[0],
        compiler_params=pltpu.CompilerParams(vmem_limit_bytes=8 * 2**20),
    )(flags, *produced, place, gate_values)
    return (attn_proj[None], expert_sum[None])


def solution(mesh):
    placed = (
        P("dp", "ctx", None),
        P("dp", "ctx", None),
        P("dp", "ctx", None),
        P("dp", "ctx", None),
        P("dp", None),
        P(),
        P("dp", None, None, "ctx"),
        P("dp", "ctx", None),
        P("dp", "ctx", None),
        P("dp", "ctx", None),
        P("dp", "ctx", None),
        P(),
    )
    dp_size, ctx_size = mesh.shape["dp"], mesh.shape["ctx"]
    small = ctx_size == 2 and dp_size == 2 * HEADS
    return jax.shard_map(
        body_move_rows if small else body_move_weights,
        mesh=mesh,
        in_specs=placed,
        out_specs=(P("dp", "ctx", None), P("dp", "ctx", None)),
        check_vma=False,
    )
```

```python
import functools

import jax
import jax.numpy as jnp
from jax import lax
from jax.experimental import pallas as pl
from jax.experimental.pallas import tpu as pltpu
from jax.sharding import PartitionSpec as P

HEADS = 8
HD = 128
PASS_SPECIALISTS = 2
CAP = 24


EPSILON = 1e-06
LOWEST = -1e30


def broadcast(array, axis, root):
    mine = lax.axis_index(axis) == root
    return lax.psum(jnp.where(mine, array, jnp.zeros_like(array)), axis)


def hop(array, axis, size, bit):
    return lax.ppermute(array, axis, [(i, i ^ bit) for i in range(size)])


def route_slots(expert_ids, route_gates, capacity, expert):
    matches = expert_ids == expert
    routed = jnp.any(matches, axis=1)
    gate_value = jnp.sum(jnp.where(matches, route_gates, 0.0), axis=1)
    slot_rank = jnp.cumsum(routed.astype(jnp.int32)) - 1
    kept_mask = routed & (slot_rank < capacity[expert])
    return (slot_rank, kept_mask, gate_value)


def attend(queries, key_block, value_block, visible):
    width = key_block.shape[0]
    token_count = queries.shape[0]
    query_heads = queries.reshape(token_count, HEADS, HD)
    key_heads = key_block.reshape(width, HEADS, HD)
    value_heads = value_block.reshape(width, HEADS, HD)
    gating_logits = jnp.einsum(
        "qhd,khd->qhk", query_heads, key_heads, preferred_element_type=jnp.float32
    ) * HD ** (-0.5)
    gating_logits = jnp.where(visible[:, None, :], gating_logits, -jnp.inf)
    row_top = jnp.max(gating_logits, axis=-1)
    weights = jnp.exp(gating_logits - row_top[:, :, None])
    denominator = jnp.sum(weights, axis=-1)
    weighted = jnp.einsum(
        "qhk,khd->qhd",
        weights.astype(jnp.bfloat16),
        value_heads,
        preferred_element_type=jnp.float32,
    )
    attended = (weighted / denominator[:, :, None]).astype(jnp.bfloat16)
    return attended.reshape(token_count, HEADS * HD)


def feed_forward(rows, gate_up, down_part):
    gate_proj = jnp.dot(rows, gate_up[0], preferred_element_type=jnp.float32)
    up_proj = jnp.dot(rows, gate_up[1], preferred_element_type=jnp.float32)
    hidden = (jax.nn.silu(gate_proj) * up_proj).astype(jnp.bfloat16)
    return jnp.dot(hidden, down_part, preferred_element_type=jnp.float32).astype(jnp.bfloat16)


def normalise(attn_proj, residual, norm_gain):
    combined = residual.astype(jnp.float32) + attn_proj.astype(jnp.float32)
    return (
        combined
        * lax.rsqrt(jnp.mean(combined * combined, axis=-1, keepdims=True) + EPSILON)
        * norm_gain
    ).astype(jnp.bfloat16)


def pick_rows(routing, normed):
    slot_ids = jnp.arange(CAP)
    select = [
        (slot_rank[None, :] == slot_ids[:, None]) & kept_mask[None, :]
        for slot_rank, kept_mask, _ in routing
    ]
    select = jnp.concatenate(select, axis=0).astype(jnp.bfloat16)
    chosen = jnp.dot(select, normed, preferred_element_type=jnp.float32).astype(jnp.bfloat16)
    return chosen.reshape(PASS_SPECIALISTS, CAP, normed.shape[1])


def combine_rows(routing, produced):
    slot_ids = jnp.arange(CAP)
    summed = 0.0
    for expert in range(PASS_SPECIALISTS):
        slot_rank, kept_mask, gate_value = routing[expert]
        place = ((slot_rank[:, None] == slot_ids[None, :]) & kept_mask[:, None]).astype(
            jnp.bfloat16
        )
        picked = jnp.dot(place, produced[expert], preferred_element_type=jnp.float32)
        summed = summed + gate_value[:, None] * picked
    return summed.astype(jnp.bfloat16)


def body_move_weights(
    query_vecs,
    key_vecs,
    value_vecs,
    residual,
    w_out,
    norm_gain,
    w_gate_up,
    w_down,
    expert_ids,
    route_gates,
    capacity,
    expert_owner,
):
    token_count = query_vecs.shape[1]
    weights_in = []
    for expert in range(PASS_SPECIALISTS):
        weights_in.append(
            (
                broadcast(w_gate_up[0], "dp", expert_owner[expert]),
                broadcast(w_down[0], "dp", expert_owner[expert]),
            )
        )
    keys = lax.all_gather(key_vecs[0], "ctx", axis=0, tiled=True)
    values = lax.all_gather(value_vecs[0], "ctx", axis=0, tiled=True)
    first_row = lax.axis_index("ctx") * token_count
    query_pos = first_row + jnp.arange(token_count)
    visible = jnp.arange(keys.shape[0])[None, :] <= query_pos[:, None]
    attended = attend(query_vecs[0], keys, values, visible)
    projected = jnp.dot(
        attended,
        lax.all_gather(w_out, "dp", axis=0, tiled=True),
        preferred_element_type=jnp.float32,
    )
    attn_proj = projected.astype(jnp.bfloat16)
    normed = normalise(attn_proj, residual[0], norm_gain)
    routing = [
        route_slots(expert_ids[0], route_gates[0], capacity[0, 0], expert)
        for expert in range(PASS_SPECIALISTS)
    ]
    chosen = pick_rows(routing, normed)
    routed_rows = lax.all_gather(jnp.swapaxes(chosen, 0, 1), "ctx", axis=0, tiled=True)
    outputs = [
        feed_forward(routed_rows[:, expert], *weights_in[expert])
        for expert in range(PASS_SPECIALISTS)
    ]
    expert_out = lax.psum_scatter(
        jnp.stack(outputs, axis=1), "ctx", scatter_dimension=0, tiled=True
    )
    expert_sum = combine_rows(routing, [expert_out[:, e] for e in range(PASS_SPECIALISTS)])
    return (attn_proj[None], expert_sum[None])


CTX, CHIP, CORE, FIRST, FIRST_CAP, SECOND, SECOND_CAP, SAME = range(8)
FIRST_HERE, SECOND_HERE, PASSES, BRANCH, PASS_INFO = range(8, 13)
USE_FAR, NEAR_LAST, NEAR_SECOND, OTHER_NEAR, PASS_COUNT = range(5)


def work_out_places(bits, owners, caps, info):
    me = lax.axis_index("dp")
    differ = owners[0] ^ owners[1]
    branch = 0
    split_bit = 0
    rest = [bits[1], bits[2]]
    for k in reversed(range(len(bits))):
        parted = (differ & bits[k]) != 0
        branch = jnp.where(parted, k, branch)
        split_bit = jnp.where(parted, bits[k], split_bit)
        others = [bit for bit in bits if bit != bits[k]]
        rest = [jnp.where(parted, others[i], rest[i]) for i in range(2)]
    same = split_bit == 0
    swapped = ((me ^ owners[0]) & split_bit) != 0
    first_offset = me ^ jnp.where(swapped, owners[1], owners[0])
    second_offset = me ^ jnp.where(swapped, owners[0], owners[1])

    def put(place, value):
        info[place] = value.astype(jnp.int32)

    put(CTX, lax.axis_index("ctx"))
    put(CHIP, me >> 1)
    put(CORE, me & 1)
    put(FIRST, jnp.where(swapped, 1, 0))
    put(FIRST_CAP, jnp.where(swapped, caps[0, 0, 1], caps[0, 0, 0]))
    put(SECOND, jnp.where(swapped, 0, 1))
    put(SECOND_CAP, jnp.where(swapped, caps[0, 0, 0], caps[0, 0, 1]))
    put(SAME, jnp.where(same, 1, 0))
    put(FIRST_HERE, jnp.where((first_offset & bits[0]) == 0, 1, 0))
    put(SECOND_HERE, jnp.where((second_offset & bits[0]) == 0, 1, 0))
    put(PASSES, jnp.where(same, 2, 1))
    put(BRANCH, branch)
    pairs = (
        (first_offset, jnp.where(same, first_offset, second_offset)),
        (second_offset, second_offset),
    )
    for k, (offset, other_offset) in enumerate(pairs):
        base = PASS_INFO + k * PASS_COUNT
        put(base + USE_FAR, offset & 1)
        put(base + NEAR_LAST, jnp.where((offset & rest[1]) == 0, 1, 0))
        put(base + NEAR_SECOND, jnp.where((offset & rest[0]) == 0, 1, 0))
        put(base + OTHER_NEAR, jnp.where((other_offset & rest[0]) == 0, 1, 0))


def attend_kernel(bits, owners, caps, query, key, value, before_both, ids, gates, *outs):
    attended, select, gate_values, info = outs
    work_out_places(bits, owners, caps, info)
    token_count = query.shape[0]
    row = lax.broadcasted_iota(jnp.int32, (token_count, token_count), 0)
    col = lax.broadcasted_iota(jnp.int32, (token_count, token_count), 1)
    own_visible = col <= row
    before_visible = jnp.broadcast_to(info[CTX], (token_count, token_count)) == 1
    contract_last = (((1,), (1,)), ((), ()))
    for head in range(HEADS):
        span = slice(head * HD, (head + 1) * HD)
        heads = query[:, span]
        own = lax.dot_general(
            heads, key[:, span], contract_last, preferred_element_type=jnp.float32
        )
        before = lax.dot_general(
            heads, before_both[0, :, span], contract_last, preferred_element_type=jnp.float32
        )
        own = jnp.where(own_visible, own * HD ** (-0.5), -jnp.inf)
        before = jnp.where(before_visible, before * HD ** (-0.5), -jnp.inf)
        top = jnp.maximum(
            jnp.max(own, axis=1, keepdims=True), jnp.max(before, axis=1, keepdims=True)
        )
        own = jnp.exp(own - top)
        before = jnp.exp(before - top)
        total = jnp.sum(own, axis=1, keepdims=True) + jnp.sum(before, axis=1, keepdims=True)
        mixed = jnp.dot(
            own.astype(jnp.bfloat16), value[:, span], preferred_element_type=jnp.float32
        ) + jnp.dot(
            before.astype(jnp.bfloat16), before_both[1, :, span], preferred_element_type=jnp.float32
        )
        mixed = mixed / total
        swapped = pltpu.roll(mixed, HD // 2, 1)
        mixed = jnp.where(jnp.broadcast_to(info[CORE], mixed.shape) == 0, mixed, swapped)
        attended[head ^ info[CHIP]] = mixed.astype(jnp.bfloat16)

    slot = lax.broadcasted_iota(jnp.int32, (CAP, token_count), 0)
    earlier = (row < col).astype(jnp.bfloat16)
    for k in range(PASS_SPECIALISTS):
        matches = ids[...] == info[FIRST + 2 * k]
        named = jnp.max(matches.astype(jnp.float32), axis=0, keepdims=True)
        gate_row = jnp.sum(jnp.where(matches, gates[...], 0.0), axis=0, keepdims=True)
        gate_values[:, k : k + 1] = jnp.sum(
            jnp.where(row == col, jnp.broadcast_to(gate_row, row.shape), 0.0),
            axis=1,
            keepdims=True,
        )
        routed = jnp.broadcast_to(named, (CAP, token_count))
        rank = jnp.dot(
            routed.astype(jnp.bfloat16), earlier, preferred_element_type=jnp.float32
        ).astype(jnp.int32)
        kept = (routed > 0.0) & (rank == slot) & (rank < info[FIRST_CAP + 2 * k])
        select[k] = kept.astype(jnp.bfloat16)


def project_kernel(info, attended, residual, gain, select, *refs):
    near = refs[:HEADS]
    far = refs[HEADS : 2 * HEADS]
    attn_proj, kept, sent, second, _, _, combined = refs[-7:]
    token_count, width = residual.shape
    tile = 512
    squares = jnp.zeros((token_count, 1), jnp.float32)
    for start in range(0, width, tile):
        span = slice(start, start + tile)
        total = jnp.zeros((token_count, tile), jnp.float32)
        for pair in range(0, HEADS, 2):
            left = jnp.concatenate([attended[pair], attended[pair + 1]], axis=1)
            right = jnp.concatenate(
                [near[pair][:, span], far[pair][:, span]]
                + [near[pair + 1][:, span], far[pair + 1][:, span]],
                axis=0,
            )
            total = total + jnp.dot(left, right, preferred_element_type=jnp.float32)
        rounded = total.astype(jnp.bfloat16)
        attn_proj[:, span] = rounded
        added = residual[:, span].astype(jnp.float32) + rounded.astype(jnp.float32)
        combined[:, span] = added
        squares = squares + jnp.sum(added * added, axis=1, keepdims=True)
    scale = lax.rsqrt(squares / width + EPSILON)
    for start in range(0, width, tile):
        span = slice(start, start + tile)
        normed = (combined[:, span] * scale * gain[:, span]).astype(jnp.bfloat16)
        rows = [
            jnp.dot(select[k], normed, preferred_element_type=jnp.float32)
            for k in range(PASS_SPECIALISTS)
        ]
        kept[:, span] = rows[0].astype(jnp.bfloat16)
        second[:, span] = rows[1].astype(jnp.bfloat16)
        use_first = jnp.broadcast_to(info[SAME], rows[0].shape) != 0
        sent[:, span] = jnp.where(use_first, rows[0], rows[1]).astype(jnp.bfloat16)


def combine_kernel(info, step, own, other, last, second, select, gate_values, *outs):
    out, next_last, next_kept, next_sent = outs
    same = info[SAME] != 0
    contract_first = (((0,), (0,)), ((), ()))

    def add_up(first_rows, second_rows):
        total = 0.0
        for k, rows in enumerate((first_rows, second_rows)):
            picked = lax.dot_general(
                select[k], rows, contract_first, preferred_element_type=jnp.float32
            )
            total = total + gate_values[:, k : k + 1] * picked
        return total.astype(jnp.bfloat16)

    @pl.when(jnp.logical_not(same))
    def _():
        for start in range(0, own.shape[1], 512):
            span = slice(start, start + 512)
            out[:, span] = add_up(own[:, span], other[:, span])

    @pl.when(same)
    def _():
        here = jnp.where(step[0] == 0, info[FIRST_HERE], info[SECOND_HERE])
        for start in range(0, own.shape[1], 512):
            span = slice(start, start + 512)
            use_own = jnp.broadcast_to(here, (own.shape[0], 512)) != 0
            served = jnp.where(
                use_own, own[:, span].astype(jnp.float32), other[:, span].astype(jnp.float32)
            ).astype(jnp.bfloat16)
            out[:, span] = add_up(last[:, span], served)
            next_last[:, span] = served
            next_kept[:, span] = second[:, span]
            next_sent[:, span] = second[:, span]


def expert_kernel(info, step, rows, gate_up_near, gate_up_far, down_near, down_far, made, gate_up, down, hidden, sems):
    units = down.shape[0]
    starts = list(range(0, units, 256))

    def copies(gate_up_from, down_from):
        out = []
        for k, start in enumerate(starts):
            size = min(256, units - start)
            span = pl.ds(start, size)
            for part in range(2):
                out.append(
                    pltpu.make_async_copy(
                        gate_up_from.at[part, span], gate_up.at[part, span], sems.at[2 * k + part]
                    )
                )
        out.append(pltpu.make_async_copy(down_from, down, sems.at[2 * len(starts)]))
        return out

    use_far = info[PASS_INFO + USE_FAR + PASS_COUNT * step[0]]

    @pl.when(use_far == 0)
    def _():
        for copy in copies(gate_up_near, down_near):
            copy.start()

    @pl.when(use_far != 0)
    def _():
        for copy in copies(gate_up_far, down_far):
            copy.start()

    arrived = copies(gate_up_near, down_near)
    contract_last = (((1,), (1,)), ((), ()))
    for k, start in enumerate(starts):
        size = min(256, units - start)
        span = slice(start, start + size)
        arrived[2 * k].wait()
        gate_proj = lax.dot_general(
            gate_up[0, span], rows[...], contract_last, preferred_element_type=jnp.float32
        )
        arrived[2 * k + 1].wait()
        up_proj = lax.dot_general(
            gate_up[1, span], rows[...], contract_last, preferred_element_type=jnp.float32
        )
        hidden[span] = (gate_proj / (1.0 + jnp.exp(-gate_proj)) * up_proj).astype(jnp.bfloat16)
    arrived[-1].wait()
    width = made.shape[1]
    contract_first = (((0,), (0,)), ((), ()))
    for start in range(0, width, 512):
        span = slice(start, start + 512)
        made[:, span] = lax.dot_general(
            hidden[...], down[:, span], contract_first, preferred_element_type=jnp.float32
        ).astype(jnp.bfloat16)


def gather_rows(kept, sent, first, bits, dp_size):
    second, last = bits
    unit = jnp.concatenate(
        [
            kept,
            hop(sent, "dp", dp_size, first),
            hop(kept, "dp", dp_size, second),
            hop(sent, "dp", dp_size, first | second),
        ],
        axis=0,
    )
    half = unit.shape[1] // 2
    left, right = unit[:, :half], unit[:, half:]
    left = jnp.stack([left, hop(left, "dp", dp_size, last)])
    right = jnp.stack([right, hop(right, "ctx", 2, 1)])
    left = jnp.stack([left, hop(left, "ctx", 2, 1)])
    right = jnp.stack([right, hop(right, "dp", dp_size, last)], axis=1)
    rows = jnp.concatenate([left, right], axis=-1)
    return rows.reshape(-1, rows.shape[-1])


def scatter_rows(rows, first, bits, dp_size, near_last, near_second, other_near):
    second, last = bits
    half = rows.shape[1] // 2
    rows = rows.reshape(2, 2, -1, rows.shape[1])
    left, right = rows[..., :half], rows[..., half:]

    def add(kept, came):
        return (kept.astype(jnp.float32) + came.astype(jnp.float32)).astype(jnp.bfloat16)

    left = add(left[0], hop(left[1], "ctx", 2, 1))
    right = jnp.where(near_last, right[:, 0], hop(right[:, 1], "dp", dp_size, last))
    left = jnp.where(near_last, left[0], hop(left[1], "dp", dp_size, last))
    right = add(right[0], hop(right[1], "ctx", 2, 1))
    unit = jnp.concatenate([left, right], axis=-1)
    here, across, beside, beyond = lax.optimization_barrier(jnp.split(unit, 4, axis=0))
    across = hop(across, "dp", dp_size, first)
    beside = hop(beside, "dp", dp_size, second)
    beyond = hop(beyond, "dp", dp_size, first | second)
    return (
        jnp.where(near_second, here, beside),
        jnp.where(other_near, across, beyond),
    )


def smem(count):
    return [pl.BlockSpec(memory_space=pltpu.SMEM)] * count


def vmem(count):
    return [pl.BlockSpec(memory_space=pltpu.VMEM)] * count


def body_move_rows(
    query_vecs,
    key_vecs,
    value_vecs,
    residual,
    w_out,
    norm_gain,
    w_gate_up,
    w_down,
    expert_ids,
    route_gates,
    capacity,
    expert_owner,
):
    token_count = query_vecs.shape[1]
    width = residual.shape[2]
    dp_size = lax.axis_size("dp")
    bits = [1 << k for k in reversed(range(1, dp_size.bit_length() - 1))]

    before = lax.ppermute(jnp.stack([key_vecs[0], value_vecs[0]]), "ctx", [(0, 1)])
    z_far, z_near, x_bit = bits
    z_both = z_far | z_near
    near = {0: w_out}
    for bit in (z_near, x_bit, z_far):
        near[bit] = hop(w_out, "dp", dp_size, bit)
    near[z_near], near[x_bit], near[z_far] = lax.optimization_barrier(
        (near[z_near], near[x_bit], near[z_far])
    )
    near[z_near | x_bit] = hop(near[z_near], "dp", dp_size, x_bit)
    near[z_both] = hop(near[z_far], "dp", dp_size, z_near)
    near[z_far | x_bit] = hop(near[z_far], "dp", dp_size, x_bit)
    before, near[z_near | x_bit] = lax.optimization_barrier((before, near[z_near | x_bit]))
    attended, select, gate_values, info = pl.pallas_call(
        functools.partial(attend_kernel, bits),
        out_shape=(
            jax.ShapeDtypeStruct((HEADS, token_count, HD), jnp.bfloat16),
            jax.ShapeDtypeStruct((PASS_SPECIALISTS, CAP, token_count), jnp.bfloat16),
            jax.ShapeDtypeStruct((token_count, PASS_SPECIALISTS), jnp.float32),
            jax.ShapeDtypeStruct((PASS_INFO + 2 * PASS_COUNT,), jnp.int32),
        ),
        in_specs=smem(2) + vmem(6),
        out_specs=tuple(vmem(3) + smem(1)),
        cost_estimate=pl.CostEstimate(
            flops=64 * HEADS * HD * 2 * token_count * token_count,
            bytes_accessed=6 * 2 * token_count * HEADS * HD,
            transcendentals=2 * HEADS * token_count * token_count,
        ),
        compiler_params=pltpu.CompilerParams(vmem_limit_bytes=8 * 2**20),
    )(
        expert_owner,
        capacity,
        query_vecs[0],
        key_vecs[0],
        value_vecs[0],
        before,
        jnp.transpose(expert_ids[0]),
        jnp.transpose(route_gates[0]),
    )
    near[z_both], attended = lax.optimization_barrier((near[z_both], attended))
    near[z_both | x_bit] = hop(near[z_both], "dp", dp_size, x_bit)
    far = [hop(near[2 * j], "dp", dp_size, 1) for j in range(HEADS)]
    shares = [near[2 * j] for j in range(HEADS)] + far
    gate_up_near = jnp.swapaxes(w_gate_up[0], 1, 2)

    some_rows = jax.ShapeDtypeStruct((CAP, width), jnp.bfloat16)
    all_rows = jax.ShapeDtypeStruct((token_count, width), jnp.bfloat16)
    attn_proj, kept, sent, second, last, expert_sum = pl.pallas_call(
        project_kernel,
        out_shape=(all_rows, some_rows, some_rows, some_rows, some_rows, all_rows),
        in_specs=smem(1) + vmem(4 + len(shares)),
        out_specs=tuple(vmem(4) + [pl.BlockSpec(memory_space=pl.ANY)] * 2),
        scratch_shapes=[pltpu.VMEM((token_count, width), jnp.float32)],
        cost_estimate=pl.CostEstimate(
            flops=2 * token_count * HEADS * HD * width,
            bytes_accessed=2 * HEADS * HD * width,
            transcendentals=0,
        ),
        compiler_params=pltpu.CompilerParams(vmem_limit_bytes=16 * 2**20),
    )(info, attended, residual[0], norm_gain[None], select, *shares)

    units = w_down.shape[1]
    row_count = dp_size * CAP

    def dispatch(bit):
        rest = [b for b in bits if b != bit]

        def run(kept, sent):
            gate_up_far = hop(gate_up_near, "dp", dp_size, 1)
            down_far = hop(w_down[0], "dp", dp_size, 1)
            rows = gather_rows(kept, sent, bit, rest, dp_size)
            return rows, gate_up_far, down_far

        return run

    def give_back(bit):
        rest = [b for b in bits if b != bit]

        def run(made, info, step):
            places = [
                jnp.where(step == 0, info[PASS_INFO + k], info[PASS_INFO + PASS_COUNT + k]) != 0
                for k in (NEAR_LAST, NEAR_SECOND, OTHER_NEAR)
            ]
            return scatter_rows(made, bit, rest, dp_size, *places)

        return run

    branch = info[BRANCH]

    def one_pass(step, carried):
        kept, sent, last, _ = carried
        rows, gate_up_far, down_far = lax.switch(
            branch, [dispatch(bit) for bit in bits], kept, sent
        )
        made = pl.pallas_call(
            expert_kernel,
            out_shape=jax.ShapeDtypeStruct((row_count, width), jnp.bfloat16),
            in_specs=smem(2) + vmem(1) + [pl.BlockSpec(memory_space=pltpu.HBM)] * 4,
            out_specs=vmem(1)[0],
            scratch_shapes=[
                pltpu.VMEM((2, units, width), jnp.bfloat16),
                pltpu.VMEM((units, width), jnp.bfloat16),
                pltpu.VMEM((units, row_count), jnp.bfloat16),
                pltpu.SemaphoreType.DMA((2 * -(-units // 256) + 1,)),
            ],
            cost_estimate=pl.CostEstimate(
                flops=6 * row_count * units * width,
                bytes_accessed=6 * units * width,
                transcendentals=row_count * units,
            ),
            compiler_params=pltpu.CompilerParams(vmem_limit_bytes=22 * 2**20),
        )(info, step[None], rows, gate_up_near, gate_up_far, w_down[0], down_far)
        own, other = lax.switch(branch, [give_back(bit) for bit in bits], made, info, step)
        expert_sum, last, kept, sent = pl.pallas_call(
            combine_kernel,
            out_shape=(all_rows, some_rows, some_rows, some_rows),
            in_specs=smem(2) + vmem(6),
            out_specs=tuple(vmem(4)),
            compiler_params=pltpu.CompilerParams(vmem_limit_bytes=8 * 2**20),
        )(info, step[None], own, other, last, second, select, gate_values)
        return kept, sent, last, expert_sum

    carried = (kept, sent, last, expert_sum)
    expert_sum = lax.fori_loop(0, info[PASSES], one_pass, carried)[3]
    return (attn_proj[None], expert_sum[None])


def solution(mesh):
    placed = (
        P("dp", "ctx", None),
        P("dp", "ctx", None),
        P("dp", "ctx", None),
        P("dp", "ctx", None),
        P("dp", None),
        P(),
        P("dp", None, None, "ctx"),
        P("dp", "ctx", None),
        P("dp", "ctx", None),
        P("dp", "ctx", None),
        P("dp", "ctx", None),
        P(),
    )
    dp_size, ctx_size = mesh.shape["dp"], mesh.shape["ctx"]
    small = ctx_size == 2 and dp_size == 2 * HEADS
    return jax.shard_map(
        body_move_rows if small else body_move_weights,
        mesh=mesh,
        in_specs=placed,
        out_specs=(P("dp", "ctx", None), P("dp", "ctx", None)),
        check_vma=False,
    )
```

```python
import functools

import jax
import jax.numpy as jnp
from jax import lax
from jax.experimental import pallas as pl
from jax.experimental.pallas import tpu as pltpu
from jax.sharding import PartitionSpec as P

HEADS = 8
HD = 128
PASS_SPECIALISTS = 2
CAP = 24


EPSILON = 1e-06
LOWEST = -1e30


def broadcast(array, axis, root):
    mine = lax.axis_index(axis) == root
    return lax.psum(jnp.where(mine, array, jnp.zeros_like(array)), axis)


def hop(array, axis, size, bit):
    return lax.ppermute(array, axis, [(i, i ^ bit) for i in range(size)])


def route_slots(expert_ids, route_gates, capacity, expert):
    matches = expert_ids == expert
    routed = jnp.any(matches, axis=1)
    gate_value = jnp.sum(jnp.where(matches, route_gates, 0.0), axis=1)
    slot_rank = jnp.cumsum(routed.astype(jnp.int32)) - 1
    kept_mask = routed & (slot_rank < capacity[expert])
    return (slot_rank, kept_mask, gate_value)


def attend(queries, key_block, value_block, visible):
    width = key_block.shape[0]
    token_count = queries.shape[0]
    query_heads = queries.reshape(token_count, HEADS, HD)
    key_heads = key_block.reshape(width, HEADS, HD)
    value_heads = value_block.reshape(width, HEADS, HD)
    gating_logits = jnp.einsum(
        "qhd,khd->qhk", query_heads, key_heads, preferred_element_type=jnp.float32
    ) * HD ** (-0.5)
    gating_logits = jnp.where(visible[:, None, :], gating_logits, -jnp.inf)
    row_top = jnp.max(gating_logits, axis=-1)
    weights = jnp.exp(gating_logits - row_top[:, :, None])
    denominator = jnp.sum(weights, axis=-1)
    weighted = jnp.einsum(
        "qhk,khd->qhd",
        weights.astype(jnp.bfloat16),
        value_heads,
        preferred_element_type=jnp.float32,
    )
    attended = (weighted / denominator[:, :, None]).astype(jnp.bfloat16)
    return attended.reshape(token_count, HEADS * HD)


def feed_forward(rows, gate_up, down_part):
    gate_proj = jnp.dot(rows, gate_up[0], preferred_element_type=jnp.float32)
    up_proj = jnp.dot(rows, gate_up[1], preferred_element_type=jnp.float32)
    hidden = (jax.nn.silu(gate_proj) * up_proj).astype(jnp.bfloat16)
    return jnp.dot(hidden, down_part, preferred_element_type=jnp.float32).astype(jnp.bfloat16)


def normalise(attn_proj, residual, norm_gain):
    combined = residual.astype(jnp.float32) + attn_proj.astype(jnp.float32)
    return (
        combined
        * lax.rsqrt(jnp.mean(combined * combined, axis=-1, keepdims=True) + EPSILON)
        * norm_gain
    ).astype(jnp.bfloat16)


def pick_rows(routing, normed):
    slot_ids = jnp.arange(CAP)
    select = [
        (slot_rank[None, :] == slot_ids[:, None]) & kept_mask[None, :]
        for slot_rank, kept_mask, _ in routing
    ]
    select = jnp.concatenate(select, axis=0).astype(jnp.bfloat16)
    chosen = jnp.dot(select, normed, preferred_element_type=jnp.float32).astype(jnp.bfloat16)
    return chosen.reshape(PASS_SPECIALISTS, CAP, normed.shape[1])


def combine_rows(routing, produced):
    slot_ids = jnp.arange(CAP)
    summed = 0.0
    for expert in range(PASS_SPECIALISTS):
        slot_rank, kept_mask, gate_value = routing[expert]
        place = ((slot_rank[:, None] == slot_ids[None, :]) & kept_mask[:, None]).astype(
            jnp.bfloat16
        )
        picked = jnp.dot(place, produced[expert], preferred_element_type=jnp.float32)
        summed = summed + gate_value[:, None] * picked
    return summed.astype(jnp.bfloat16)


def body_move_weights(
    query_vecs,
    key_vecs,
    value_vecs,
    residual,
    w_out,
    norm_gain,
    w_gate_up,
    w_down,
    expert_ids,
    route_gates,
    capacity,
    expert_owner,
):
    token_count = query_vecs.shape[1]
    weights_in = []
    for expert in range(PASS_SPECIALISTS):
        weights_in.append(
            (
                broadcast(w_gate_up[0], "dp", expert_owner[expert]),
                broadcast(w_down[0], "dp", expert_owner[expert]),
            )
        )
    keys = lax.all_gather(key_vecs[0], "ctx", axis=0, tiled=True)
    values = lax.all_gather(value_vecs[0], "ctx", axis=0, tiled=True)
    first_row = lax.axis_index("ctx") * token_count
    query_pos = first_row + jnp.arange(token_count)
    visible = jnp.arange(keys.shape[0])[None, :] <= query_pos[:, None]
    attended = attend(query_vecs[0], keys, values, visible)
    projected = jnp.dot(
        attended,
        lax.all_gather(w_out, "dp", axis=0, tiled=True),
        preferred_element_type=jnp.float32,
    )
    attn_proj = projected.astype(jnp.bfloat16)
    normed = normalise(attn_proj, residual[0], norm_gain)
    routing = [
        route_slots(expert_ids[0], route_gates[0], capacity[0, 0], expert)
        for expert in range(PASS_SPECIALISTS)
    ]
    chosen = pick_rows(routing, normed)
    routed_rows = lax.all_gather(jnp.swapaxes(chosen, 0, 1), "ctx", axis=0, tiled=True)
    outputs = [
        feed_forward(routed_rows[:, expert], *weights_in[expert])
        for expert in range(PASS_SPECIALISTS)
    ]
    expert_out = lax.psum_scatter(
        jnp.stack(outputs, axis=1), "ctx", scatter_dimension=0, tiled=True
    )
    expert_sum = combine_rows(routing, [expert_out[:, e] for e in range(PASS_SPECIALISTS)])
    return (attn_proj[None], expert_sum[None])


CTX, CHIP, CORE, FIRST, FIRST_CAP, SECOND, SECOND_CAP, SAME = range(8)
FIRST_HERE, SECOND_HERE, PASSES, BRANCH, PASS_INFO = range(8, 13)
USE_FAR, NEAR_LAST, NEAR_SECOND, OTHER_NEAR, PASS_COUNT = range(5)


def work_out_places(bits, owners, caps, info):
    me = lax.axis_index("dp")
    differ = owners[0] ^ owners[1]
    branch = 0
    split_bit = 0
    rest = [bits[1], bits[2]]
    for k in reversed(range(len(bits))):
        parted = (differ & bits[k]) != 0
        branch = jnp.where(parted, k, branch)
        split_bit = jnp.where(parted, bits[k], split_bit)
        others = [bit for bit in bits if bit != bits[k]]
        rest = [jnp.where(parted, others[i], rest[i]) for i in range(2)]
    same = split_bit == 0
    swapped = ((me ^ owners[0]) & split_bit) != 0
    first_offset = me ^ jnp.where(swapped, owners[1], owners[0])
    second_offset = me ^ jnp.where(swapped, owners[0], owners[1])

    def put(place, value):
        info[place] = value.astype(jnp.int32)

    put(CTX, lax.axis_index("ctx"))
    put(CHIP, me >> 1)
    put(CORE, me & 1)
    put(FIRST, jnp.where(swapped, 1, 0))
    put(FIRST_CAP, jnp.where(swapped, caps[0, 0, 1], caps[0, 0, 0]))
    put(SECOND, jnp.where(swapped, 0, 1))
    put(SECOND_CAP, jnp.where(swapped, caps[0, 0, 0], caps[0, 0, 1]))
    put(SAME, jnp.where(same, 1, 0))
    put(FIRST_HERE, jnp.where((first_offset & bits[0]) == 0, 1, 0))
    put(SECOND_HERE, jnp.where((second_offset & bits[0]) == 0, 1, 0))
    put(PASSES, jnp.where(same, 2, 1))
    put(BRANCH, branch)
    pairs = (
        (first_offset, jnp.where(same, first_offset, second_offset)),
        (second_offset, second_offset),
    )
    for k, (offset, other_offset) in enumerate(pairs):
        base = PASS_INFO + k * PASS_COUNT
        put(base + USE_FAR, offset & 1)
        put(base + NEAR_LAST, jnp.where((offset & rest[1]) == 0, 1, 0))
        put(base + NEAR_SECOND, jnp.where((offset & rest[0]) == 0, 1, 0))
        put(base + OTHER_NEAR, jnp.where((other_offset & rest[0]) == 0, 1, 0))


def attend_kernel(bits, owners, caps, query, own_both, before_both, ids, gates, *outs):
    attended, select, gate_values, info = outs
    work_out_places(bits, owners, caps, info)
    token_count = query.shape[0]
    row = lax.broadcasted_iota(jnp.int32, (token_count, token_count), 0)
    col = lax.broadcasted_iota(jnp.int32, (token_count, token_count), 1)
    own_visible = col <= row
    before_visible = jnp.broadcast_to(info[CTX], (token_count, token_count)) == 1
    contract_last = (((1,), (1,)), ((), ()))
    for head in range(HEADS):
        span = slice(head * HD, (head + 1) * HD)
        heads = query[:, span]
        own = lax.dot_general(
            heads, own_both[0, :, span], contract_last, preferred_element_type=jnp.float32
        )
        before = lax.dot_general(
            heads, before_both[0, :, span], contract_last, preferred_element_type=jnp.float32
        )
        own = jnp.where(own_visible, own * HD ** (-0.5), -jnp.inf)
        before = jnp.where(before_visible, before * HD ** (-0.5), -jnp.inf)
        top = jnp.maximum(
            jnp.max(own, axis=1, keepdims=True), jnp.max(before, axis=1, keepdims=True)
        )
        own = jnp.exp(own - top)
        before = jnp.exp(before - top)
        total = jnp.sum(own, axis=1, keepdims=True) + jnp.sum(before, axis=1, keepdims=True)
        mixed = jnp.dot(
            own.astype(jnp.bfloat16), own_both[1, :, span], preferred_element_type=jnp.float32
        ) + jnp.dot(
            before.astype(jnp.bfloat16), before_both[1, :, span], preferred_element_type=jnp.float32
        )
        mixed = mixed / total
        swapped = pltpu.roll(mixed, HD // 2, 1)
        mixed = jnp.where(jnp.broadcast_to(info[CORE], mixed.shape) == 0, mixed, swapped)
        attended[head ^ info[CHIP]] = mixed.astype(jnp.bfloat16)

    slot = lax.broadcasted_iota(jnp.int32, (CAP, token_count), 0)
    earlier = (row < col).astype(jnp.bfloat16)
    for k in range(PASS_SPECIALISTS):
        matches = ids[...] == info[FIRST + 2 * k]
        named = jnp.max(matches.astype(jnp.float32), axis=0, keepdims=True)
        gate_row = jnp.sum(jnp.where(matches, gates[...], 0.0), axis=0, keepdims=True)
        gate_values[:, k : k + 1] = jnp.sum(
            jnp.where(row == col, jnp.broadcast_to(gate_row, row.shape), 0.0),
            axis=1,
            keepdims=True,
        )
        routed = jnp.broadcast_to(named, (CAP, token_count))
        rank = jnp.dot(
            routed.astype(jnp.bfloat16), earlier, preferred_element_type=jnp.float32
        ).astype(jnp.int32)
        kept = (routed > 0.0) & (rank == slot) & (rank < info[FIRST_CAP + 2 * k])
        select[k] = kept.astype(jnp.bfloat16)


def add_products(attended, chips, near, far, span, total):
    for pair in range(0, len(chips), 2):
        one, two = chips[pair], chips[pair + 1]
        left = jnp.concatenate([attended[one], attended[two]], axis=1)
        right = jnp.concatenate(
            [near[pair][:, span], far[pair][:, span]]
            + [near[pair + 1][:, span], far[pair + 1][:, span]],
            axis=0,
        )
        product = jnp.dot(left, right, preferred_element_type=jnp.float32)
        total = product if total is None else total + product
    return total


def early_kernel(chips, attended, *refs):
    near, far = refs[: len(chips)], refs[len(chips) : 2 * len(chips)]
    total = refs[-1]
    for start in range(0, total.shape[1], 512):
        span = slice(start, start + 512)
        total[:, span] = add_products(attended, chips, near, far, span, None)


def project_kernel(chips, info, attended, residual, gain, select, early, *refs):
    near, far = refs[: len(chips)], refs[len(chips) : 2 * len(chips)]
    attn_proj, kept, sent, second, _, _, combined = refs[-7:]
    token_count, width = residual.shape
    tile = 512
    squares = jnp.zeros((token_count, 1), jnp.float32)
    for start in range(0, width, tile):
        span = slice(start, start + tile)
        total = add_products(attended, chips, near, far, span, early[:, span])
        rounded = total.astype(jnp.bfloat16)
        attn_proj[:, span] = rounded
        added = residual[:, span].astype(jnp.float32) + rounded.astype(jnp.float32)
        combined[:, span] = added
        squares = squares + jnp.sum(added * added, axis=1, keepdims=True)
    scale = lax.rsqrt(squares / width + EPSILON)
    for start in range(0, width, tile):
        span = slice(start, start + tile)
        normed = (combined[:, span] * scale * gain[:, span]).astype(jnp.bfloat16)
        rows = [
            jnp.dot(select[k], normed, preferred_element_type=jnp.float32)
            for k in range(PASS_SPECIALISTS)
        ]
        kept[:, span] = rows[0].astype(jnp.bfloat16)
        second[:, span] = rows[1].astype(jnp.bfloat16)
        use_first = jnp.broadcast_to(info[SAME], rows[0].shape) != 0
        sent[:, span] = jnp.where(use_first, rows[0], rows[1]).astype(jnp.bfloat16)


def combine_kernel(info, step, own, other, last, second, select, gate_values, *outs):
    out, next_last, next_kept, next_sent = outs
    same = info[SAME] != 0
    contract_first = (((0,), (0,)), ((), ()))

    def add_up(first_rows, second_rows):
        total = 0.0
        for k, rows in enumerate((first_rows, second_rows)):
            picked = lax.dot_general(
                select[k], rows, contract_first, preferred_element_type=jnp.float32
            )
            total = total + gate_values[:, k : k + 1] * picked
        return total.astype(jnp.bfloat16)

    @pl.when(jnp.logical_not(same))
    def _():
        for start in range(0, own.shape[1], 512):
            span = slice(start, start + 512)
            out[:, span] = add_up(own[:, span], other[:, span])

    @pl.when(same)
    def _():
        here = jnp.where(step[0] == 0, info[FIRST_HERE], info[SECOND_HERE])
        for start in range(0, own.shape[1], 512):
            span = slice(start, start + 512)
            use_own = jnp.broadcast_to(here, (own.shape[0], 512)) != 0
            served = jnp.where(
                use_own, own[:, span].astype(jnp.float32), other[:, span].astype(jnp.float32)
            ).astype(jnp.bfloat16)
            out[:, span] = add_up(last[:, span], served)
            next_last[:, span] = served
            next_kept[:, span] = second[:, span]
            next_sent[:, span] = second[:, span]


def expert_kernel(
    info,
    step,
    rows,
    gate_up_near,
    gate_up_far,
    down_near,
    down_far,
    made,
    masks,
    gate_up,
    down,
    hidden,
    sems,
):
    units = down.shape[0]
    starts = list(range(0, units, 256))

    def copies(gate_up_from, down_from):
        out = []
        for k, start in enumerate(starts):
            size = min(256, units - start)
            span = pl.ds(start, size)
            for part in range(2):
                out.append(
                    pltpu.make_async_copy(
                        gate_up_from.at[part, span], gate_up.at[part, span], sems.at[2 * k + part]
                    )
                )
        out.append(pltpu.make_async_copy(down_from, down, sems.at[2 * len(starts)]))
        return out

    base = PASS_INFO + PASS_COUNT * step[0]
    use_far = info[base + USE_FAR]
    for k in (NEAR_LAST, NEAR_SECOND, OTHER_NEAR):
        masks[k] = jnp.broadcast_to(info[base + k].astype(jnp.float32), masks.shape[1:])

    @pl.when(use_far == 0)
    def _():
        for copy in copies(gate_up_near, down_near):
            copy.start()

    @pl.when(use_far != 0)
    def _():
        for copy in copies(gate_up_far, down_far):
            copy.start()

    arrived = copies(gate_up_near, down_near)
    contract_last = (((1,), (1,)), ((), ()))
    for k, start in enumerate(starts):
        size = min(256, units - start)
        span = slice(start, start + size)
        arrived[2 * k].wait()
        gate_proj = lax.dot_general(
            gate_up[0, span], rows[...], contract_last, preferred_element_type=jnp.float32
        )
        arrived[2 * k + 1].wait()
        up_proj = lax.dot_general(
            gate_up[1, span], rows[...], contract_last, preferred_element_type=jnp.float32
        )
        hidden[span] = (gate_proj / (1.0 + jnp.exp(-gate_proj)) * up_proj).astype(jnp.bfloat16)
    arrived[-1].wait()
    width = made.shape[1]
    contract_first = (((0,), (0,)), ((), ()))
    for start in range(0, width, 512):
        span = slice(start, start + 512)
        made[:, span] = lax.dot_general(
            hidden[...], down[:, span], contract_first, preferred_element_type=jnp.float32
        ).astype(jnp.bfloat16)


def gather_rows(kept, sent, first, bits, dp_size):
    second, last = bits
    unit = jnp.concatenate(
        [
            kept,
            hop(sent, "dp", dp_size, first),
            hop(kept, "dp", dp_size, second),
            hop(sent, "dp", dp_size, first | second),
        ],
        axis=0,
    )
    half = unit.shape[1] // 2
    left, right = unit[:, :half], unit[:, half:]
    left = jnp.stack([left, hop(left, "dp", dp_size, last)])
    right = jnp.stack([right, hop(right, "ctx", 2, 1)])
    left = jnp.stack([left, hop(left, "ctx", 2, 1)])
    right = jnp.stack([right, hop(right, "dp", dp_size, last)], axis=1)
    rows = jnp.concatenate([left, right], axis=-1)
    return rows.reshape(-1, rows.shape[-1])


def scatter_rows(rows, first, bits, dp_size, masks):
    second, last = bits
    half = rows.shape[1] // 2
    rows = rows.reshape(2, 2, -1, rows.shape[1])
    left, right = rows[..., :half], rows[..., half:]

    def add(kept, came):
        return (kept.astype(jnp.float32) + came.astype(jnp.float32)).astype(jnp.bfloat16)

    left = add(left[0], hop(left[1], "ctx", 2, 1))
    right = jnp.where(masks[NEAR_LAST, :, half:] != 0, right[:, 0], hop(right[:, 1], "dp", dp_size, last))
    left = jnp.where(masks[NEAR_LAST, :, :half] != 0, left[0], hop(left[1], "dp", dp_size, last))
    right = add(right[0], hop(right[1], "ctx", 2, 1))
    unit = jnp.concatenate([left, right], axis=-1)
    here, across, beside, beyond = lax.optimization_barrier(jnp.split(unit, 4, axis=0))
    across = hop(across, "dp", dp_size, first)
    beside = hop(beside, "dp", dp_size, second)
    beyond = hop(beyond, "dp", dp_size, first | second)
    return (
        jnp.where(masks[NEAR_SECOND] != 0, here, beside),
        jnp.where(masks[OTHER_NEAR] != 0, across, beyond),
    )


def smem(count):
    return [pl.BlockSpec(memory_space=pltpu.SMEM)] * count


def vmem(count):
    return [pl.BlockSpec(memory_space=pltpu.VMEM)] * count


def body_move_rows(
    query_vecs,
    key_vecs,
    value_vecs,
    residual,
    w_out,
    norm_gain,
    w_gate_up,
    w_down,
    expert_ids,
    route_gates,
    capacity,
    expert_owner,
):
    token_count = query_vecs.shape[1]
    width = residual.shape[2]
    dp_size = lax.axis_size("dp")
    bits = [1 << k for k in reversed(range(1, dp_size.bit_length() - 1))]

    own_both = jnp.stack([key_vecs[0], value_vecs[0]])
    before = lax.ppermute(own_both, "ctx", [(0, 1)])
    z_far, z_near, x_bit = bits
    z_both = z_far | z_near
    near = {0: w_out}
    for bit in (z_far, z_near, x_bit):
        near[bit] = hop(w_out, "dp", dp_size, bit)
    near[z_near], near[x_bit], near[z_far] = lax.optimization_barrier(
        (near[z_near], near[x_bit], near[z_far])
    )
    near[z_near | x_bit] = hop(near[z_near], "dp", dp_size, x_bit)
    near[z_both] = hop(near[z_far], "dp", dp_size, z_near)
    near[z_far | x_bit] = hop(near[z_far], "dp", dp_size, x_bit)
    before, near[z_near | x_bit] = lax.optimization_barrier((before, near[z_near | x_bit]))
    attended, select, gate_values, info = pl.pallas_call(
        functools.partial(attend_kernel, bits),
        out_shape=(
            jax.ShapeDtypeStruct((HEADS, token_count, HD), jnp.bfloat16),
            jax.ShapeDtypeStruct((PASS_SPECIALISTS, CAP, token_count), jnp.bfloat16),
            jax.ShapeDtypeStruct((token_count, PASS_SPECIALISTS), jnp.float32),
            jax.ShapeDtypeStruct((PASS_INFO + 2 * PASS_COUNT,), jnp.int32),
        ),
        in_specs=smem(2) + vmem(5),
        out_specs=tuple(vmem(3) + smem(1)),
        cost_estimate=pl.CostEstimate(
            flops=64 * HEADS * HD * 2 * token_count * token_count,
            bytes_accessed=6 * 2 * token_count * HEADS * HD,
            transcendentals=2 * HEADS * token_count * token_count,
        ),
        compiler_params=pltpu.CompilerParams(vmem_limit_bytes=8 * 2**20),
    )(
        expert_owner,
        capacity,
        query_vecs[0],
        own_both,
        before,
        jnp.transpose(expert_ids[0]),
        jnp.transpose(route_gates[0]),
    )
    last_share = hop(near[z_both], "dp", dp_size, x_bit)
    near[z_both | x_bit], attended = lax.optimization_barrier((last_share, attended))
    far = {bit: hop(near[bit], "dp", dp_size, 1) for bit in near}
    late_bits = (z_far | x_bit, z_both | x_bit)
    early_bits = tuple(bit for bit in near if bit not in late_bits)
    early_chips = [bit >> 1 for bit in early_bits]
    late_chips = [bit >> 1 for bit in late_bits]
    early = pl.pallas_call(
        functools.partial(early_kernel, early_chips),
        out_shape=jax.ShapeDtypeStruct((token_count, width), jnp.float32),
        in_specs=vmem(1 + 2 * len(early_bits)),
        out_specs=vmem(1)[0],
        cost_estimate=pl.CostEstimate(
            flops=4 * 2 * token_count * HEADS * HD * width,
            bytes_accessed=2 * HEADS * HD * width,
            transcendentals=0,
        ),
        compiler_params=pltpu.CompilerParams(vmem_limit_bytes=16 * 2**20),
    )(attended, *[near[bit] for bit in early_bits], *[far[bit] for bit in early_bits])
    gate_up_near = jnp.swapaxes(w_gate_up[0], 1, 2)

    some_rows = jax.ShapeDtypeStruct((CAP, width), jnp.bfloat16)
    all_rows = jax.ShapeDtypeStruct((token_count, width), jnp.bfloat16)
    attn_proj, kept, sent, second, last, expert_sum = pl.pallas_call(
        functools.partial(project_kernel, late_chips),
        out_shape=(all_rows, some_rows, some_rows, some_rows, some_rows, all_rows),
        in_specs=smem(1) + vmem(5 + 2 * len(late_bits)),
        out_specs=tuple(vmem(4) + [pl.BlockSpec(memory_space=pl.ANY)] * 2),
        scratch_shapes=[pltpu.VMEM((token_count, width), jnp.float32)],
        cost_estimate=pl.CostEstimate(
            flops=2 * token_count * HEADS * HD * width,
            bytes_accessed=2 * HEADS * HD * width,
            transcendentals=0,
        ),
        compiler_params=pltpu.CompilerParams(vmem_limit_bytes=16 * 2**20),
    )(
        info,
        attended,
        residual[0],
        norm_gain[None],
        select,
        early,
        *[near[bit] for bit in late_bits],
        *[far[bit] for bit in late_bits],
    )

    units = w_down.shape[1]
    row_count = dp_size * CAP

    def dispatch(bit):
        rest = [b for b in bits if b != bit]

        def run(kept, sent):
            gate_up_far = hop(gate_up_near, "dp", dp_size, 1)
            down_far = hop(w_down[0], "dp", dp_size, 1)
            rows = gather_rows(kept, sent, bit, rest, dp_size)
            return rows, gate_up_far, down_far

        return run

    def give_back(bit):
        rest = [b for b in bits if b != bit]

        def run(made, masks):
            return scatter_rows(made, bit, rest, dp_size, masks)

        return run

    branch = info[BRANCH]

    def one_pass(step, carried):
        kept, sent, last, _ = carried
        rows, gate_up_far, down_far = lax.switch(
            branch, [dispatch(bit) for bit in bits], kept, sent
        )
        made, masks = pl.pallas_call(
            expert_kernel,
            out_shape=(
                jax.ShapeDtypeStruct((row_count, width), jnp.bfloat16),
                jax.ShapeDtypeStruct((PASS_COUNT, 1, width), jnp.float32),
            ),
            in_specs=smem(2) + vmem(1) + [pl.BlockSpec(memory_space=pltpu.HBM)] * 4,
            out_specs=tuple(vmem(2)),
            scratch_shapes=[
                pltpu.VMEM((2, units, width), jnp.bfloat16),
                pltpu.VMEM((units, width), jnp.bfloat16),
                pltpu.VMEM((units, row_count), jnp.bfloat16),
                pltpu.SemaphoreType.DMA((2 * -(-units // 256) + 1,)),
            ],
            cost_estimate=pl.CostEstimate(
                flops=6 * row_count * units * width,
                bytes_accessed=6 * units * width,
                transcendentals=row_count * units,
            ),
            compiler_params=pltpu.CompilerParams(vmem_limit_bytes=22 * 2**20),
        )(info, step[None], rows, gate_up_near, gate_up_far, w_down[0], down_far)
        own, other = lax.switch(branch, [give_back(bit) for bit in bits], made, masks)
        expert_sum, last, kept, sent = pl.pallas_call(
            combine_kernel,
            out_shape=(all_rows, some_rows, some_rows, some_rows),
            in_specs=smem(2) + vmem(6),
            out_specs=tuple(vmem(4)),
            compiler_params=pltpu.CompilerParams(vmem_limit_bytes=8 * 2**20),
        )(info, step[None], own, other, last, second, select, gate_values)
        return kept, sent, last, expert_sum

    carried = (kept, sent, last, expert_sum)
    expert_sum = lax.fori_loop(0, info[PASSES], one_pass, carried)[3]
    return (attn_proj[None], expert_sum[None])


def solution(mesh):
    placed = (
        P("dp", "ctx", None),
        P("dp", "ctx", None),
        P("dp", "ctx", None),
        P("dp", "ctx", None),
        P("dp", None),
        P(),
        P("dp", None, None, "ctx"),
        P("dp", "ctx", None),
        P("dp", "ctx", None),
        P("dp", "ctx", None),
        P("dp", "ctx", None),
        P(),
    )
    dp_size, ctx_size = mesh.shape["dp"], mesh.shape["ctx"]
    small = ctx_size == 2 and dp_size == 2 * HEADS
    return jax.shard_map(
        body_move_rows if small else body_move_weights,
        mesh=mesh,
        in_specs=placed,
        out_specs=(P("dp", "ctx", None), P("dp", "ctx", None)),
        check_vma=False,
    )
```

```python
import functools

import jax
import jax.numpy as jnp
from jax import lax
from jax.experimental import pallas as pl
from jax.experimental.pallas import tpu as pltpu
from jax.sharding import PartitionSpec as P

HEADS = 8
HD = 128
PASS_SPECIALISTS = 2
CAP = 24


EPSILON = 1e-06
LOWEST = -1e30


def broadcast(array, axis, root):
    mine = lax.axis_index(axis) == root
    return lax.psum(jnp.where(mine, array, jnp.zeros_like(array)), axis)


def hop(array, axis, size, bit, wanted=None):
    pairs = [(i, i ^ bit) for i in range(size)]
    if wanted is not None:
        pairs = [pair for pair in pairs if wanted(*pair)]
    return lax.ppermute(array, axis, pairs)


def route_slots(expert_ids, route_gates, capacity, expert):
    matches = expert_ids == expert
    routed = jnp.any(matches, axis=1)
    gate_value = jnp.sum(jnp.where(matches, route_gates, 0.0), axis=1)
    slot_rank = jnp.cumsum(routed.astype(jnp.int32)) - 1
    kept_mask = routed & (slot_rank < capacity[expert])
    return (slot_rank, kept_mask, gate_value)


def attend(queries, key_block, value_block, visible):
    width = key_block.shape[0]
    token_count = queries.shape[0]
    query_heads = queries.reshape(token_count, HEADS, HD)
    key_heads = key_block.reshape(width, HEADS, HD)
    value_heads = value_block.reshape(width, HEADS, HD)
    gating_logits = jnp.einsum(
        "qhd,khd->qhk", query_heads, key_heads, preferred_element_type=jnp.float32
    ) * HD ** (-0.5)
    gating_logits = jnp.where(visible[:, None, :], gating_logits, -jnp.inf)
    row_top = jnp.max(gating_logits, axis=-1)
    weights = jnp.exp(gating_logits - row_top[:, :, None])
    denominator = jnp.sum(weights, axis=-1)
    weighted = jnp.einsum(
        "qhk,khd->qhd",
        weights.astype(jnp.bfloat16),
        value_heads,
        preferred_element_type=jnp.float32,
    )
    attended = (weighted / denominator[:, :, None]).astype(jnp.bfloat16)
    return attended.reshape(token_count, HEADS * HD)


def feed_forward(rows, gate_up, down_part):
    gate_proj = jnp.dot(rows, gate_up[0], preferred_element_type=jnp.float32)
    up_proj = jnp.dot(rows, gate_up[1], preferred_element_type=jnp.float32)
    hidden = (jax.nn.silu(gate_proj) * up_proj).astype(jnp.bfloat16)
    return jnp.dot(hidden, down_part, preferred_element_type=jnp.float32).astype(jnp.bfloat16)


def normalise(attn_proj, residual, norm_gain):
    combined = residual.astype(jnp.float32) + attn_proj.astype(jnp.float32)
    return (
        combined
        * lax.rsqrt(jnp.mean(combined * combined, axis=-1, keepdims=True) + EPSILON)
        * norm_gain
    ).astype(jnp.bfloat16)


def pick_rows(routing, normed):
    slot_ids = jnp.arange(CAP)
    select = [
        (slot_rank[None, :] == slot_ids[:, None]) & kept_mask[None, :]
        for slot_rank, kept_mask, _ in routing
    ]
    select = jnp.concatenate(select, axis=0).astype(jnp.bfloat16)
    chosen = jnp.dot(select, normed, preferred_element_type=jnp.float32).astype(jnp.bfloat16)
    return chosen.reshape(PASS_SPECIALISTS, CAP, normed.shape[1])


def combine_rows(routing, produced):
    slot_ids = jnp.arange(CAP)
    summed = 0.0
    for expert in range(PASS_SPECIALISTS):
        slot_rank, kept_mask, gate_value = routing[expert]
        place = ((slot_rank[:, None] == slot_ids[None, :]) & kept_mask[:, None]).astype(
            jnp.bfloat16
        )
        picked = jnp.dot(place, produced[expert], preferred_element_type=jnp.float32)
        summed = summed + gate_value[:, None] * picked
    return summed.astype(jnp.bfloat16)


def body_move_weights(
    query_vecs,
    key_vecs,
    value_vecs,
    residual,
    w_out,
    norm_gain,
    w_gate_up,
    w_down,
    expert_ids,
    route_gates,
    capacity,
    expert_owner,
):
    token_count = query_vecs.shape[1]
    weights_in = []
    for expert in range(PASS_SPECIALISTS):
        weights_in.append(
            (
                broadcast(w_gate_up[0], "dp", expert_owner[expert]),
                broadcast(w_down[0], "dp", expert_owner[expert]),
            )
        )
    keys = lax.all_gather(key_vecs[0], "ctx", axis=0, tiled=True)
    values = lax.all_gather(value_vecs[0], "ctx", axis=0, tiled=True)
    first_row = lax.axis_index("ctx") * token_count
    query_pos = first_row + jnp.arange(token_count)
    visible = jnp.arange(keys.shape[0])[None, :] <= query_pos[:, None]
    attended = attend(query_vecs[0], keys, values, visible)
    projected = jnp.dot(
        attended,
        lax.all_gather(w_out, "dp", axis=0, tiled=True),
        preferred_element_type=jnp.float32,
    )
    attn_proj = projected.astype(jnp.bfloat16)
    normed = normalise(attn_proj, residual[0], norm_gain)
    routing = [
        route_slots(expert_ids[0], route_gates[0], capacity[0, 0], expert)
        for expert in range(PASS_SPECIALISTS)
    ]
    chosen = pick_rows(routing, normed)
    routed_rows = lax.all_gather(jnp.swapaxes(chosen, 0, 1), "ctx", axis=0, tiled=True)
    outputs = [
        feed_forward(routed_rows[:, expert], *weights_in[expert])
        for expert in range(PASS_SPECIALISTS)
    ]
    expert_out = lax.psum_scatter(
        jnp.stack(outputs, axis=1), "ctx", scatter_dimension=0, tiled=True
    )
    expert_sum = combine_rows(routing, [expert_out[:, e] for e in range(PASS_SPECIALISTS)])
    return (attn_proj[None], expert_sum[None])


CTX, CHIP, CORE, FIRST, FIRST_CAP, SECOND, SECOND_CAP, SAME = range(8)
FIRST_HERE, SECOND_HERE, PASSES, BRANCH, PASS_INFO = range(8, 13)
USE_FAR, NEAR_LAST, NEAR_SECOND, OTHER_NEAR, PASS_COUNT = range(5)


def work_out_places(bits, owners, caps, info):
    me = lax.axis_index("dp")
    differ = owners[0] ^ owners[1]
    branch = 0
    split_bit = 0
    rest = [bits[1], bits[2]]
    for k in reversed(range(len(bits))):
        parted = (differ & bits[k]) != 0
        branch = jnp.where(parted, k, branch)
        split_bit = jnp.where(parted, bits[k], split_bit)
        others = [bit for bit in bits if bit != bits[k]]
        rest = [jnp.where(parted, others[i], rest[i]) for i in range(2)]
    same = split_bit == 0
    swapped = ((me ^ owners[0]) & split_bit) != 0
    first_offset = me ^ jnp.where(swapped, owners[1], owners[0])
    second_offset = me ^ jnp.where(swapped, owners[0], owners[1])

    def put(place, value):
        info[place] = value.astype(jnp.int32)

    put(CTX, lax.axis_index("ctx"))
    put(CHIP, me >> 1)
    put(CORE, me & 1)
    put(FIRST, jnp.where(swapped, 1, 0))
    put(FIRST_CAP, jnp.where(swapped, caps[0, 0, 1], caps[0, 0, 0]))
    put(SECOND, jnp.where(swapped, 0, 1))
    put(SECOND_CAP, jnp.where(swapped, caps[0, 0, 0], caps[0, 0, 1]))
    put(SAME, jnp.where(same, 1, 0))
    put(FIRST_HERE, jnp.where((first_offset & bits[0]) == 0, 1, 0))
    put(SECOND_HERE, jnp.where((second_offset & bits[0]) == 0, 1, 0))
    put(PASSES, jnp.where(same, 2, 1))
    on_one = (owners[0] & jnp.where(same, bits[0], split_bit)) != 0
    seconds = [jnp.where((owners[k] & rest[0]) == 0, 0, 1) for k in range(2)]
    at_zero = jnp.where(on_one, seconds[1], seconds[0])
    at_one = jnp.where(on_one, seconds[0], seconds[1])
    at_one = jnp.where(same, at_zero, at_one)
    put(BRANCH, jnp.where(branch == 0, 2 * at_zero + at_one, 2 + 2 * branch + at_zero))
    pairs = (
        (first_offset, jnp.where(same, first_offset, second_offset)),
        (second_offset, second_offset),
    )
    for k, (offset, other_offset) in enumerate(pairs):
        base = PASS_INFO + k * PASS_COUNT
        put(base + USE_FAR, offset & 1)
        put(base + NEAR_LAST, jnp.where((offset & rest[1]) == 0, 1, 0))
        put(base + NEAR_SECOND, jnp.where((offset & rest[0]) == 0, 1, 0))
        put(base + OTHER_NEAR, jnp.where((other_offset & rest[0]) == 0, 1, 0))


def branches(bits):
    return [(bits[0], (zero, one)) for zero in range(2) for one in range(2)] + [
        (bit, (both, both)) for bit in bits[1:] for both in range(2)
    ]


def attend_kernel(bits, owners, caps, query, key, value, key_before, value_before, *refs):
    ids, gates, attended, select, gate_values, info = refs
    work_out_places(bits, owners, caps, info)
    token_count = query.shape[0]
    row = lax.broadcasted_iota(jnp.int32, (token_count, token_count), 0)
    col = lax.broadcasted_iota(jnp.int32, (token_count, token_count), 1)
    own_visible = col <= row
    before_visible = jnp.broadcast_to(info[CTX], (token_count, token_count)) == 1
    contract_last = (((1,), (1,)), ((), ()))
    for head in range(HEADS):
        span = slice(head * HD, (head + 1) * HD)
        heads = query[:, span]
        own = lax.dot_general(
            heads, key[:, span], contract_last, preferred_element_type=jnp.float32
        )
        before = lax.dot_general(
            heads, key_before[:, span], contract_last, preferred_element_type=jnp.float32
        )
        own = jnp.where(own_visible, own * HD ** (-0.5), -jnp.inf)
        before = jnp.where(before_visible, before * HD ** (-0.5), -jnp.inf)
        top = jnp.maximum(
            jnp.max(own, axis=1, keepdims=True), jnp.max(before, axis=1, keepdims=True)
        )
        own = jnp.exp(own - top)
        before = jnp.exp(before - top)
        total = jnp.sum(own, axis=1, keepdims=True) + jnp.sum(before, axis=1, keepdims=True)
        mixed = jnp.dot(
            own.astype(jnp.bfloat16), value[:, span], preferred_element_type=jnp.float32
        ) + jnp.dot(
            before.astype(jnp.bfloat16), value_before[:, span], preferred_element_type=jnp.float32
        )
        mixed = mixed / total
        swapped = pltpu.roll(mixed, HD // 2, 1)
        mixed = jnp.where(jnp.broadcast_to(info[CORE], mixed.shape) == 0, mixed, swapped)
        attended[head ^ info[CHIP]] = mixed.astype(jnp.bfloat16)

    slot = lax.broadcasted_iota(jnp.int32, (CAP, token_count), 0)
    earlier = (row < col).astype(jnp.bfloat16)
    for k in range(PASS_SPECIALISTS):
        matches = ids[...] == info[FIRST + 2 * k]
        named = jnp.max(matches.astype(jnp.float32), axis=0, keepdims=True)
        gate_row = jnp.sum(jnp.where(matches, gates[...], 0.0), axis=0, keepdims=True)
        gate_values[:, k : k + 1] = jnp.sum(
            jnp.where(row == col, jnp.broadcast_to(gate_row, row.shape), 0.0),
            axis=1,
            keepdims=True,
        )
        routed = jnp.broadcast_to(named, (CAP, token_count))
        rank = jnp.dot(
            routed.astype(jnp.bfloat16), earlier, preferred_element_type=jnp.float32
        ).astype(jnp.int32)
        kept = (routed > 0.0) & (rank == slot) & (rank < info[FIRST_CAP + 2 * k])
        select[k] = kept.astype(jnp.bfloat16)


def add_products(attended, chips, near, far, span, total):
    for pair in range(0, len(chips), 2):
        one, two = chips[pair], chips[pair + 1]
        left = jnp.concatenate([attended[one], attended[two]], axis=1)
        right = jnp.concatenate(
            [near[pair][:, span], far[pair][:, span]]
            + [near[pair + 1][:, span], far[pair + 1][:, span]],
            axis=0,
        )
        product = jnp.dot(left, right, preferred_element_type=jnp.float32)
        total = product if total is None else total + product
    return total


def early_kernel(chips, attended, *refs):
    near, far = refs[: len(chips)], refs[len(chips) : -1]
    total = refs[-1]
    for start in range(0, total.shape[1], 512):
        span = slice(start, start + 512)
        total[:, span] = add_products(attended, chips, near, far, span, None)


def project_kernel(chips, info, attended, residual, gain, select, early, *refs):
    near, far = refs[: len(chips)], refs[len(chips) : 2 * len(chips)]
    attn_proj, kept, sent, second, _, _, combined = refs[-7:]
    token_count, width = residual.shape
    tile = 512
    squares = jnp.zeros((token_count, 1), jnp.float32)
    for start in range(0, width, tile):
        span = slice(start, start + tile)
        total = add_products(attended, chips, near, far, span, early[:, span])
        rounded = total.astype(jnp.bfloat16)
        attn_proj[:, span] = rounded
        added = residual[:, span].astype(jnp.float32) + rounded.astype(jnp.float32)
        combined[:, span] = added
        squares = squares + jnp.sum(added * added, axis=1, keepdims=True)
    scale = lax.rsqrt(squares / width + EPSILON)
    for start in range(0, width, tile):
        span = slice(start, start + tile)
        normed = (combined[:, span] * scale * gain[:, span]).astype(jnp.bfloat16)
        rows = [
            jnp.dot(select[k], normed, preferred_element_type=jnp.float32)
            for k in range(PASS_SPECIALISTS)
        ]
        kept[:, span] = rows[0].astype(jnp.bfloat16)
        second[:, span] = rows[1].astype(jnp.bfloat16)
        use_first = jnp.broadcast_to(info[SAME], rows[0].shape) != 0
        sent[:, span] = jnp.where(use_first, rows[0], rows[1]).astype(jnp.bfloat16)


def combine_kernel(info, step, own, other, last, second, select, gate_values, *outs):
    out, next_last, next_kept, next_sent = outs
    same = info[SAME] != 0
    contract_first = (((0,), (0,)), ((), ()))

    def add_up(first_rows, second_rows):
        total = 0.0
        for k, rows in enumerate((first_rows, second_rows)):
            picked = lax.dot_general(
                select[k], rows, contract_first, preferred_element_type=jnp.float32
            )
            total = total + gate_values[:, k : k + 1] * picked
        return total.astype(jnp.bfloat16)

    @pl.when(jnp.logical_not(same))
    def _():
        for start in range(0, own.shape[1], 512):
            span = slice(start, start + 512)
            out[:, span] = add_up(own[:, span], other[:, span])

    @pl.when(same)
    def _():
        here = jnp.where(step[0] == 0, info[FIRST_HERE], info[SECOND_HERE])
        for start in range(0, own.shape[1], 512):
            span = slice(start, start + 512)
            use_own = jnp.broadcast_to(here, (own.shape[0], 512)) != 0
            served = jnp.where(
                use_own, own[:, span].astype(jnp.float32), other[:, span].astype(jnp.float32)
            ).astype(jnp.bfloat16)
            out[:, span] = add_up(last[:, span], served)
            next_last[:, span] = served
            next_kept[:, span] = second[:, span]
            next_sent[:, span] = second[:, span]


def expert_kernel(
    info,
    step,
    rows,
    gate_up_near,
    gate_up_far,
    down_near,
    down_far,
    made,
    masks,
    gate_up,
    down,
    hidden,
    sems,
):
    units = down.shape[0]
    starts = list(range(0, units, 256))

    def copies(gate_up_from, down_from):
        out = []
        for k, start in enumerate(starts):
            size = min(256, units - start)
            span = pl.ds(start, size)
            for part in range(2):
                out.append(
                    pltpu.make_async_copy(
                        gate_up_from.at[part, span], gate_up.at[part, span], sems.at[2 * k + part]
                    )
                )
        out.append(pltpu.make_async_copy(down_from, down, sems.at[2 * len(starts)]))
        return out

    base = PASS_INFO + PASS_COUNT * step[0]
    use_far = info[base + USE_FAR]
    for k in (NEAR_LAST, NEAR_SECOND, OTHER_NEAR):
        masks[k] = jnp.broadcast_to(info[base + k].astype(jnp.float32), masks.shape[1:])

    @pl.when(use_far == 0)
    def _():
        for copy in copies(gate_up_near, down_near):
            copy.start()

    @pl.when(use_far != 0)
    def _():
        for copy in copies(gate_up_far, down_far):
            copy.start()

    arrived = copies(gate_up_near, down_near)
    contract_last = (((1,), (1,)), ((), ()))
    for k, start in enumerate(starts):
        size = min(256, units - start)
        span = slice(start, start + size)
        arrived[2 * k].wait()
        gate_proj = lax.dot_general(
            gate_up[0, span], rows[...], contract_last, preferred_element_type=jnp.float32
        )
        arrived[2 * k + 1].wait()
        up_proj = lax.dot_general(
            gate_up[1, span], rows[...], contract_last, preferred_element_type=jnp.float32
        )
        hidden[span] = (gate_proj / (1.0 + jnp.exp(-gate_proj)) * up_proj).astype(jnp.bfloat16)
    arrived[-1].wait()
    width = made.shape[1]
    contract_first = (((0,), (0,)), ((), ()))
    for start in range(0, width, 512):
        span = slice(start, start + 512)
        made[:, span] = lax.dot_general(
            hidden[...], down[:, span], contract_first, preferred_element_type=jnp.float32
        ).astype(jnp.bfloat16)


def gather_rows(kept, sent, first, places, bits, dp_size):
    second, last = bits

    def to_owner(_, target):
        return ((target & second) != 0) == places[(target & first) != 0]

    unit = jnp.concatenate(
        [
            kept,
            hop(sent, "dp", dp_size, first, to_owner),
            hop(kept, "dp", dp_size, second, to_owner),
            hop(sent, "dp", dp_size, first | second, to_owner),
        ],
        axis=0,
    )
    half = unit.shape[1] // 2
    left, right = unit[:, :half], unit[:, half:]
    left = jnp.stack([left, hop(left, "dp", dp_size, last)])
    right = jnp.stack([right, hop(right, "ctx", 2, 1)])
    left = jnp.stack([left, hop(left, "ctx", 2, 1)])
    right = jnp.stack([right, hop(right, "dp", dp_size, last)], axis=1)
    rows = jnp.concatenate([left, right], axis=-1)
    return rows.reshape(-1, rows.shape[-1])


def scatter_rows(rows, first, places, bits, dp_size, masks):
    second, last = bits
    half = rows.shape[1] // 2
    rows = rows.reshape(2, 2, -1, rows.shape[1])
    left, right = rows[..., :half], rows[..., half:]

    def add(kept, came):
        return (kept.astype(jnp.float32) + came.astype(jnp.float32)).astype(jnp.bfloat16)

    left = add(left[0], hop(left[1], "ctx", 2, 1))
    right = jnp.where(masks[NEAR_LAST, :, half:] != 0, right[:, 0], hop(right[:, 1], "dp", dp_size, last))
    left = jnp.where(masks[NEAR_LAST, :, :half] != 0, left[0], hop(left[1], "dp", dp_size, last))
    right = add(right[0], hop(right[1], "ctx", 2, 1))
    unit = jnp.concatenate([left, right], axis=-1)
    here, across, beside, beyond = lax.optimization_barrier(jnp.split(unit, 4, axis=0))

    def from_owner(source, _):
        return ((source & second) != 0) == places[(source & first) != 0]

    across = hop(across, "dp", dp_size, first, from_owner)
    beside = hop(beside, "dp", dp_size, second, from_owner)
    beyond = hop(beyond, "dp", dp_size, first | second, from_owner)
    return (
        jnp.where(masks[NEAR_SECOND] != 0, here, beside),
        jnp.where(masks[OTHER_NEAR] != 0, across, beyond),
    )


def smem(count):
    return [pl.BlockSpec(memory_space=pltpu.SMEM)] * count


def vmem(count):
    return [pl.BlockSpec(memory_space=pltpu.VMEM)] * count


def body_move_rows(
    query_vecs,
    key_vecs,
    value_vecs,
    residual,
    w_out,
    norm_gain,
    w_gate_up,
    w_down,
    expert_ids,
    route_gates,
    capacity,
    expert_owner,
):
    token_count = query_vecs.shape[1]
    width = residual.shape[2]
    dp_size = lax.axis_size("dp")
    bits = [1 << k for k in reversed(range(1, dp_size.bit_length() - 1))]

    key_before = lax.ppermute(key_vecs[0], "ctx", [(0, 1)])
    value_before = lax.ppermute(value_vecs[0], "ctx", [(0, 1)])
    z_far, z_near, x_bit = bits
    z_both = z_far | z_near
    near = {0: w_out}
    for bit in (z_far, z_near, x_bit):
        near[bit] = hop(w_out, "dp", dp_size, bit)
    far = {0: hop(w_out, "dp", dp_size, 1)}
    near[z_far], near[z_near], near[x_bit], key_before, far[0] = lax.optimization_barrier(
        (near[z_far], near[z_near], near[x_bit], key_before, far[0])
    )
    near[z_near | x_bit] = hop(near[z_near], "dp", dp_size, x_bit)
    near[z_both] = hop(near[z_far], "dp", dp_size, z_near)
    near[z_far | x_bit] = hop(near[z_far], "dp", dp_size, x_bit)
    value_before, near[z_near | x_bit] = lax.optimization_barrier(
        (value_before, near[z_near | x_bit])
    )
    attended, select, gate_values, info = pl.pallas_call(
        functools.partial(attend_kernel, bits),
        out_shape=(
            jax.ShapeDtypeStruct((HEADS, token_count, HD), jnp.bfloat16),
            jax.ShapeDtypeStruct((PASS_SPECIALISTS, CAP, token_count), jnp.bfloat16),
            jax.ShapeDtypeStruct((token_count, PASS_SPECIALISTS), jnp.float32),
            jax.ShapeDtypeStruct((PASS_INFO + 2 * PASS_COUNT,), jnp.int32),
        ),
        in_specs=smem(2) + vmem(7),
        out_specs=tuple(vmem(3) + smem(1)),
        cost_estimate=pl.CostEstimate(
            flops=64 * HEADS * HD * 2 * token_count * token_count,
            bytes_accessed=6 * 2 * token_count * HEADS * HD,
            transcendentals=2 * HEADS * token_count * token_count,
        ),
        compiler_params=pltpu.CompilerParams(vmem_limit_bytes=8 * 2**20),
    )(
        expert_owner,
        capacity,
        query_vecs[0],
        key_vecs[0],
        value_vecs[0],
        key_before,
        value_before,
        jnp.transpose(expert_ids[0]),
        jnp.transpose(route_gates[0]),
    )
    near[z_both | x_bit] = hop(near[z_both], "dp", dp_size, x_bit)
    (
        near[z_near | x_bit],
        near[z_far | x_bit],
        between,
        attended,
    ) = lax.optimization_barrier(
        (near[z_near | x_bit], near[z_far | x_bit], near[z_both], attended)
    )
    for bit in (z_far, z_near, x_bit, z_near | x_bit, z_far | x_bit, z_both | x_bit):
        far[bit] = hop(near[bit], "dp", dp_size, 1)
    far[z_both] = hop(between, "dp", dp_size, 1)
    late_bits = (z_far | x_bit, z_both | x_bit)
    early_bits = tuple(bit for bit in near if bit not in late_bits)
    early_chips = [bit >> 1 for bit in early_bits]
    late_chips = [bit >> 1 for bit in late_bits]
    early = pl.pallas_call(
        functools.partial(early_kernel, early_chips),
        out_shape=jax.ShapeDtypeStruct((token_count, width), jnp.float32),
        in_specs=vmem(1 + 2 * len(early_bits)),
        out_specs=vmem(1)[0],
        cost_estimate=pl.CostEstimate(
            flops=4 * 2 * token_count * HEADS * HD * width,
            bytes_accessed=2 * HEADS * HD * width,
            transcendentals=0,
        ),
        compiler_params=pltpu.CompilerParams(vmem_limit_bytes=16 * 2**20),
    )(attended, *[near[bit] for bit in early_bits], *[far[bit] for bit in early_bits])
    gate_up_near = jnp.swapaxes(w_gate_up[0], 1, 2)

    some_rows = jax.ShapeDtypeStruct((CAP, width), jnp.bfloat16)
    all_rows = jax.ShapeDtypeStruct((token_count, width), jnp.bfloat16)
    attn_proj, kept, sent, second, last, expert_sum = pl.pallas_call(
        functools.partial(project_kernel, late_chips),
        out_shape=(all_rows, some_rows, some_rows, some_rows, some_rows, all_rows),
        in_specs=smem(1) + vmem(5 + 2 * len(late_bits)),
        out_specs=tuple(vmem(4) + [pl.BlockSpec(memory_space=pl.ANY)] * 2),
        scratch_shapes=[pltpu.VMEM((token_count, width), jnp.float32)],
        cost_estimate=pl.CostEstimate(
            flops=2 * token_count * HEADS * HD * width,
            bytes_accessed=2 * HEADS * HD * width,
            transcendentals=0,
        ),
        compiler_params=pltpu.CompilerParams(vmem_limit_bytes=16 * 2**20),
    )(
        info,
        attended,
        residual[0],
        norm_gain[None],
        select,
        early,
        *[near[bit] for bit in late_bits],
        *[far[bit] for bit in late_bits],
    )

    units = w_down.shape[1]
    row_count = dp_size * CAP

    def dispatch(bit, places):
        rest = [b for b in bits if b != bit]

        def run(kept, sent):
            gate_up_far = hop(gate_up_near, "dp", dp_size, 1)
            down_far = hop(w_down[0], "dp", dp_size, 1)
            rows = gather_rows(kept, sent, bit, places, rest, dp_size)
            return rows, gate_up_far, down_far

        return run

    def give_back(bit, places):
        rest = [b for b in bits if b != bit]

        def run(made, masks):
            return scatter_rows(made, bit, places, rest, dp_size, masks)

        return run

    branch = info[BRANCH]

    def one_pass(step, carried):
        kept, sent, last, _ = carried
        rows, gate_up_far, down_far = lax.switch(
            branch, [dispatch(*way) for way in branches(bits)], kept, sent
        )
        made, masks = pl.pallas_call(
            expert_kernel,
            out_shape=(
                jax.ShapeDtypeStruct((row_count, width), jnp.bfloat16),
                jax.ShapeDtypeStruct((PASS_COUNT, 1, width), jnp.float32),
            ),
            in_specs=smem(2) + vmem(1) + [pl.BlockSpec(memory_space=pltpu.HBM)] * 4,
            out_specs=tuple(vmem(2)),
            scratch_shapes=[
                pltpu.VMEM((2, units, width), jnp.bfloat16),
                pltpu.VMEM((units, width), jnp.bfloat16),
                pltpu.VMEM((units, row_count), jnp.bfloat16),
                pltpu.SemaphoreType.DMA((2 * -(-units // 256) + 1,)),
            ],
            cost_estimate=pl.CostEstimate(
                flops=6 * row_count * units * width,
                bytes_accessed=6 * units * width,
                transcendentals=row_count * units,
            ),
            compiler_params=pltpu.CompilerParams(vmem_limit_bytes=22 * 2**20),
        )(info, step[None], rows, gate_up_near, gate_up_far, w_down[0], down_far)
        own, other = lax.switch(branch, [give_back(*way) for way in branches(bits)], made, masks)
        expert_sum, last, kept, sent = pl.pallas_call(
            combine_kernel,
            out_shape=(all_rows, some_rows, some_rows, some_rows),
            in_specs=smem(2) + vmem(6),
            out_specs=tuple(vmem(4)),
            compiler_params=pltpu.CompilerParams(vmem_limit_bytes=8 * 2**20),
        )(info, step[None], own, other, last, second, select, gate_values)
        return kept, sent, last, expert_sum

    carried = (kept, sent, last, expert_sum)
    expert_sum = lax.fori_loop(0, info[PASSES], one_pass, carried)[3]
    return (attn_proj[None], expert_sum[None])


def solution(mesh):
    placed = (
        P("dp", "ctx", None),
        P("dp", "ctx", None),
        P("dp", "ctx", None),
        P("dp", "ctx", None),
        P("dp", None),
        P(),
        P("dp", None, None, "ctx"),
        P("dp", "ctx", None),
        P("dp", "ctx", None),
        P("dp", "ctx", None),
        P("dp", "ctx", None),
        P(),
    )
    dp_size, ctx_size = mesh.shape["dp"], mesh.shape["ctx"]
    small = ctx_size == 2 and dp_size == 2 * HEADS
    return jax.shard_map(
        body_move_rows if small else body_move_weights,
        mesh=mesh,
        in_specs=placed,
        out_specs=(P("dp", "ctx", None), P("dp", "ctx", None)),
        check_vma=False,
    )
```

```python
import functools

import jax
import jax.numpy as jnp
from jax import lax
from jax.experimental import pallas as pl
from jax.experimental.pallas import tpu as pltpu
from jax.sharding import PartitionSpec as P

HEADS = 8
HD = 128
PASS_SPECIALISTS = 2
CAP = 24


EPSILON = 1e-06
LOWEST = -1e30


def broadcast(array, axis, root):
    mine = lax.axis_index(axis) == root
    return lax.psum(jnp.where(mine, array, jnp.zeros_like(array)), axis)


def hop(array, axis, size, bit, wanted=None):
    pairs = [(i, i ^ bit) for i in range(size)]
    if wanted is not None:
        pairs = [pair for pair in pairs if wanted(*pair)]
    return lax.ppermute(array, axis, pairs)


def route_slots(expert_ids, route_gates, capacity, expert):
    matches = expert_ids == expert
    routed = jnp.any(matches, axis=1)
    gate_value = jnp.sum(jnp.where(matches, route_gates, 0.0), axis=1)
    slot_rank = jnp.cumsum(routed.astype(jnp.int32)) - 1
    kept_mask = routed & (slot_rank < capacity[expert])
    return (slot_rank, kept_mask, gate_value)


def attend(queries, key_block, value_block, visible):
    width = key_block.shape[0]
    token_count = queries.shape[0]
    query_heads = queries.reshape(token_count, HEADS, HD)
    key_heads = key_block.reshape(width, HEADS, HD)
    value_heads = value_block.reshape(width, HEADS, HD)
    gating_logits = jnp.einsum(
        "qhd,khd->qhk", query_heads, key_heads, preferred_element_type=jnp.float32
    ) * HD ** (-0.5)
    gating_logits = jnp.where(visible[:, None, :], gating_logits, -jnp.inf)
    row_top = jnp.max(gating_logits, axis=-1)
    weights = jnp.exp(gating_logits - row_top[:, :, None])
    denominator = jnp.sum(weights, axis=-1)
    weighted = jnp.einsum(
        "qhk,khd->qhd",
        weights.astype(jnp.bfloat16),
        value_heads,
        preferred_element_type=jnp.float32,
    )
    attended = (weighted / denominator[:, :, None]).astype(jnp.bfloat16)
    return attended.reshape(token_count, HEADS * HD)


def feed_forward(rows, gate_up, down_part):
    gate_proj = jnp.dot(rows, gate_up[0], preferred_element_type=jnp.float32)
    up_proj = jnp.dot(rows, gate_up[1], preferred_element_type=jnp.float32)
    hidden = (jax.nn.silu(gate_proj) * up_proj).astype(jnp.bfloat16)
    return jnp.dot(hidden, down_part, preferred_element_type=jnp.float32).astype(jnp.bfloat16)


def normalise(attn_proj, residual, norm_gain):
    combined = residual.astype(jnp.float32) + attn_proj.astype(jnp.float32)
    return (
        combined
        * lax.rsqrt(jnp.mean(combined * combined, axis=-1, keepdims=True) + EPSILON)
        * norm_gain
    ).astype(jnp.bfloat16)


def pick_rows(routing, normed):
    slot_ids = jnp.arange(CAP)
    select = [
        (slot_rank[None, :] == slot_ids[:, None]) & kept_mask[None, :]
        for slot_rank, kept_mask, _ in routing
    ]
    select = jnp.concatenate(select, axis=0).astype(jnp.bfloat16)
    chosen = jnp.dot(select, normed, preferred_element_type=jnp.float32).astype(jnp.bfloat16)
    return chosen.reshape(PASS_SPECIALISTS, CAP, normed.shape[1])


def combine_rows(routing, produced):
    slot_ids = jnp.arange(CAP)
    summed = 0.0
    for expert in range(PASS_SPECIALISTS):
        slot_rank, kept_mask, gate_value = routing[expert]
        place = ((slot_rank[:, None] == slot_ids[None, :]) & kept_mask[:, None]).astype(
            jnp.bfloat16
        )
        picked = jnp.dot(place, produced[expert], preferred_element_type=jnp.float32)
        summed = summed + gate_value[:, None] * picked
    return summed.astype(jnp.bfloat16)


def body_move_weights(
    query_vecs,
    key_vecs,
    value_vecs,
    residual,
    w_out,
    norm_gain,
    w_gate_up,
    w_down,
    expert_ids,
    route_gates,
    capacity,
    expert_owner,
):
    token_count = query_vecs.shape[1]
    weights_in = []
    for expert in range(PASS_SPECIALISTS):
        weights_in.append(
            (
                broadcast(w_gate_up[0], "dp", expert_owner[expert]),
                broadcast(w_down[0], "dp", expert_owner[expert]),
            )
        )
    keys = lax.all_gather(key_vecs[0], "ctx", axis=0, tiled=True)
    values = lax.all_gather(value_vecs[0], "ctx", axis=0, tiled=True)
    first_row = lax.axis_index("ctx") * token_count
    query_pos = first_row + jnp.arange(token_count)
    visible = jnp.arange(keys.shape[0])[None, :] <= query_pos[:, None]
    attended = attend(query_vecs[0], keys, values, visible)
    projected = jnp.dot(
        attended,
        lax.all_gather(w_out, "dp", axis=0, tiled=True),
        preferred_element_type=jnp.float32,
    )
    attn_proj = projected.astype(jnp.bfloat16)
    normed = normalise(attn_proj, residual[0], norm_gain)
    routing = [
        route_slots(expert_ids[0], route_gates[0], capacity[0, 0], expert)
        for expert in range(PASS_SPECIALISTS)
    ]
    chosen = pick_rows(routing, normed)
    routed_rows = lax.all_gather(jnp.swapaxes(chosen, 0, 1), "ctx", axis=0, tiled=True)
    outputs = [
        feed_forward(routed_rows[:, expert], *weights_in[expert])
        for expert in range(PASS_SPECIALISTS)
    ]
    expert_out = lax.psum_scatter(
        jnp.stack(outputs, axis=1), "ctx", scatter_dimension=0, tiled=True
    )
    expert_sum = combine_rows(routing, [expert_out[:, e] for e in range(PASS_SPECIALISTS)])
    return (attn_proj[None], expert_sum[None])


CTX, CHIP, CORE, FIRST, FIRST_CAP, SECOND, SECOND_CAP, SAME = range(8)
FIRST_HERE, SECOND_HERE, PASSES, BRANCH, PASS_INFO = range(8, 13)
USE_FAR, NEAR_LAST, NEAR_SECOND, OTHER_NEAR, PASS_COUNT = range(5)


def work_out_places(bits, numbers, info):
    owners = [numbers[k] for k in range(PASS_SPECIALISTS)]
    caps = [numbers[PASS_SPECIALISTS + k] for k in range(PASS_SPECIALISTS)]
    me = lax.axis_index("dp")
    differ = owners[0] ^ owners[1]
    branch = 0
    split_bit = 0
    rest = [bits[1], bits[2]]
    for k in reversed(range(len(bits))):
        parted = (differ & bits[k]) != 0
        branch = jnp.where(parted, k, branch)
        split_bit = jnp.where(parted, bits[k], split_bit)
        others = [bit for bit in bits if bit != bits[k]]
        rest = [jnp.where(parted, others[i], rest[i]) for i in range(2)]
    same = split_bit == 0
    swapped = ((me ^ owners[0]) & split_bit) != 0
    first_offset = me ^ jnp.where(swapped, owners[1], owners[0])
    second_offset = me ^ jnp.where(swapped, owners[0], owners[1])

    def put(place, value):
        info[place] = value.astype(jnp.int32)

    put(CTX, lax.axis_index("ctx"))
    put(CHIP, me >> 1)
    put(CORE, me & 1)
    put(FIRST, jnp.where(swapped, 1, 0))
    put(FIRST_CAP, jnp.where(swapped, caps[1], caps[0]))
    put(SECOND, jnp.where(swapped, 0, 1))
    put(SECOND_CAP, jnp.where(swapped, caps[0], caps[1]))
    put(SAME, jnp.where(same, 1, 0))
    put(FIRST_HERE, jnp.where((first_offset & bits[0]) == 0, 1, 0))
    put(SECOND_HERE, jnp.where((second_offset & bits[0]) == 0, 1, 0))
    put(PASSES, jnp.where(same, 2, 1))
    on_one = (owners[0] & jnp.where(same, bits[0], split_bit)) != 0
    seconds = [jnp.where((owners[k] & rest[0]) == 0, 0, 1) for k in range(2)]
    at_zero = jnp.where(on_one, seconds[1], seconds[0])
    at_one = jnp.where(on_one, seconds[0], seconds[1])
    at_one = jnp.where(same, at_zero, at_one)
    put(BRANCH, jnp.where(branch == 0, 2 * at_zero + at_one, 2 + 2 * branch + at_zero))
    pairs = (
        (first_offset, jnp.where(same, first_offset, second_offset)),
        (second_offset, second_offset),
    )
    for k, (offset, other_offset) in enumerate(pairs):
        base = PASS_INFO + k * PASS_COUNT
        put(base + USE_FAR, offset & 1)
        put(base + NEAR_LAST, jnp.where((offset & rest[1]) == 0, 1, 0))
        put(base + NEAR_SECOND, jnp.where((offset & rest[0]) == 0, 1, 0))
        put(base + OTHER_NEAR, jnp.where((other_offset & rest[0]) == 0, 1, 0))


def branches(bits):
    return [(bits[0], (zero, one)) for zero in range(2) for one in range(2)] + [
        (bit, (both, both)) for bit in bits[1:] for both in range(2)
    ]


def attend_kernel(bits, numbers, own_vecs, key_before, value_before, ids, gates, *outs):
    attended, select, gate_values, info = outs
    query, key, value = (own_vecs.at[k] for k in range(3))
    work_out_places(bits, numbers, info)
    token_count = query.shape[0]
    row = lax.broadcasted_iota(jnp.int32, (token_count, token_count), 0)
    col = lax.broadcasted_iota(jnp.int32, (token_count, token_count), 1)
    own_visible = col <= row
    before_visible = jnp.broadcast_to(info[CTX], (token_count, token_count)) == 1
    contract_last = (((1,), (1,)), ((), ()))
    for head in range(HEADS):
        span = slice(head * HD, (head + 1) * HD)
        heads = query[:, span]
        own = lax.dot_general(
            heads, key[:, span], contract_last, preferred_element_type=jnp.float32
        )
        before = lax.dot_general(
            heads, key_before[:, span], contract_last, preferred_element_type=jnp.float32
        )
        own = jnp.where(own_visible, own * HD ** (-0.5), -jnp.inf)
        before = jnp.where(before_visible, before * HD ** (-0.5), -jnp.inf)
        top = jnp.maximum(
            jnp.max(own, axis=1, keepdims=True), jnp.max(before, axis=1, keepdims=True)
        )
        own = jnp.exp(own - top)
        before = jnp.exp(before - top)
        total = jnp.sum(own, axis=1, keepdims=True) + jnp.sum(before, axis=1, keepdims=True)
        mixed = jnp.dot(
            own.astype(jnp.bfloat16), value[:, span], preferred_element_type=jnp.float32
        ) + jnp.dot(
            before.astype(jnp.bfloat16), value_before[:, span], preferred_element_type=jnp.float32
        )
        mixed = mixed / total
        swapped = pltpu.roll(mixed, HD // 2, 1)
        mixed = jnp.where(jnp.broadcast_to(info[CORE], mixed.shape) == 0, mixed, swapped)
        attended[head ^ info[CHIP]] = mixed.astype(jnp.bfloat16)

    slot = lax.broadcasted_iota(jnp.int32, (CAP, token_count), 0)
    earlier = (row < col).astype(jnp.bfloat16)
    for k in range(PASS_SPECIALISTS):
        matches = ids[...] == info[FIRST + 2 * k]
        named = jnp.max(matches.astype(jnp.float32), axis=0, keepdims=True)
        gate_row = jnp.sum(jnp.where(matches, gates[...], 0.0), axis=0, keepdims=True)
        gate_values[:, k : k + 1] = jnp.sum(
            jnp.where(row == col, jnp.broadcast_to(gate_row, row.shape), 0.0),
            axis=1,
            keepdims=True,
        )
        routed = jnp.broadcast_to(named, (CAP, token_count))
        rank = jnp.dot(
            routed.astype(jnp.bfloat16), earlier, preferred_element_type=jnp.float32
        ).astype(jnp.int32)
        kept = (routed > 0.0) & (rank == slot) & (rank < info[FIRST_CAP + 2 * k])
        select[k] = kept.astype(jnp.bfloat16)


def add_products(attended, chips, near, far, span, total):
    for pair in range(0, len(chips), 2):
        one, two = chips[pair], chips[pair + 1]
        left = jnp.concatenate([attended[one], attended[two]], axis=1)
        right = jnp.concatenate(
            [near[pair][:, span], far[pair][:, span]]
            + [near[pair + 1][:, span], far[pair + 1][:, span]],
            axis=0,
        )
        product = jnp.dot(left, right, preferred_element_type=jnp.float32)
        total = product if total is None else total + product
    return total


def early_kernel(chips, attended, *refs):
    near, far = refs[: len(chips)], refs[len(chips) : -1]
    total = refs[-1]
    for start in range(0, total.shape[1], 512):
        span = slice(start, start + 512)
        total[:, span] = add_products(attended, chips, near, far, span, None)


def project_kernel(chips, info, attended, residual, gain, select, early, *refs):
    near, far = refs[: len(chips)], refs[len(chips) : 2 * len(chips)]
    attn_proj, kept, sent, second, _, _, combined = refs[-7:]
    token_count, width = residual.shape
    tile = 512
    squares = jnp.zeros((token_count, 1), jnp.float32)
    for start in range(0, width, tile):
        span = slice(start, start + tile)
        total = add_products(attended, chips, near, far, span, early[:, span])
        rounded = total.astype(jnp.bfloat16)
        attn_proj[:, span] = rounded
        added = residual[:, span].astype(jnp.float32) + rounded.astype(jnp.float32)
        combined[:, span] = added
        squares = squares + jnp.sum(added * added, axis=1, keepdims=True)
    scale = lax.rsqrt(squares / width + EPSILON)
    for start in range(0, width, tile):
        span = slice(start, start + tile)
        normed = (combined[:, span] * scale * gain[:, span]).astype(jnp.bfloat16)
        rows = [
            jnp.dot(select[k], normed, preferred_element_type=jnp.float32)
            for k in range(PASS_SPECIALISTS)
        ]
        kept[:, span] = rows[0].astype(jnp.bfloat16)
        second[:, span] = rows[1].astype(jnp.bfloat16)
        use_first = jnp.broadcast_to(info[SAME], rows[0].shape) != 0
        sent[:, span] = jnp.where(use_first, rows[0], rows[1]).astype(jnp.bfloat16)


def combine_kernel(info, step, own, other, last, second, select, gate_values, *outs):
    out, next_last, next_kept, next_sent = outs
    same = info[SAME] != 0
    contract_first = (((0,), (0,)), ((), ()))

    def add_up(first_rows, second_rows):
        total = 0.0
        for k, rows in enumerate((first_rows, second_rows)):
            picked = lax.dot_general(
                select[k], rows, contract_first, preferred_element_type=jnp.float32
            )
            total = total + gate_values[:, k : k + 1] * picked
        return total.astype(jnp.bfloat16)

    @pl.when(jnp.logical_not(same))
    def _():
        for start in range(0, own.shape[1], 512):
            span = slice(start, start + 512)
            out[:, span] = add_up(own[:, span], other[:, span])

    @pl.when(same)
    def _():
        here = jnp.where(step[0] == 0, info[FIRST_HERE], info[SECOND_HERE])
        for start in range(0, own.shape[1], 512):
            span = slice(start, start + 512)
            use_own = jnp.broadcast_to(here, (own.shape[0], 512)) != 0
            served = jnp.where(
                use_own, own[:, span].astype(jnp.float32), other[:, span].astype(jnp.float32)
            ).astype(jnp.bfloat16)
            out[:, span] = add_up(last[:, span], served)
            next_last[:, span] = served
            next_kept[:, span] = second[:, span]
            next_sent[:, span] = second[:, span]


def expert_kernel(
    info,
    step,
    rows,
    gate_up_near,
    gate_up_far,
    down_near,
    down_far,
    made,
    masks,
    gate_up,
    down,
    hidden,
    sems,
):
    units = down.shape[0]
    starts = list(range(0, units, 256))

    def copies(gate_up_from, down_from):
        out = []
        for k, start in enumerate(starts):
            size = min(256, units - start)
            span = pl.ds(start, size)
            for part in range(2):
                out.append(
                    pltpu.make_async_copy(
                        gate_up_from.at[part, span], gate_up.at[part, span], sems.at[2 * k + part]
                    )
                )
        out.append(pltpu.make_async_copy(down_from, down, sems.at[2 * len(starts)]))
        return out

    base = PASS_INFO + PASS_COUNT * step[0]
    use_far = info[base + USE_FAR]
    for k in (NEAR_LAST, NEAR_SECOND, OTHER_NEAR):
        masks[k] = jnp.broadcast_to(info[base + k].astype(jnp.float32), masks.shape[1:])

    @pl.when(use_far == 0)
    def _():
        for copy in copies(gate_up_near, down_near):
            copy.start()

    @pl.when(use_far != 0)
    def _():
        for copy in copies(gate_up_far, down_far):
            copy.start()

    arrived = copies(gate_up_near, down_near)
    contract_last = (((1,), (1,)), ((), ()))
    for k, start in enumerate(starts):
        size = min(256, units - start)
        span = slice(start, start + size)
        arrived[2 * k].wait()
        gate_proj = lax.dot_general(
            gate_up[0, span], rows[...], contract_last, preferred_element_type=jnp.float32
        )
        arrived[2 * k + 1].wait()
        up_proj = lax.dot_general(
            gate_up[1, span], rows[...], contract_last, preferred_element_type=jnp.float32
        )
        made_hidden = gate_proj / (1.0 + jnp.exp(-gate_proj)) * up_proj
        hidden[:, span] = jnp.transpose(made_hidden).astype(jnp.bfloat16)
    arrived[-1].wait()
    width = made.shape[1]
    for start in range(0, width, 512):
        span = slice(start, start + 512)
        made[:, span] = jnp.dot(
            hidden[...], down[:, span], preferred_element_type=jnp.float32
        ).astype(jnp.bfloat16)


def gather_rows(kept, sent, first, places, bits, dp_size):
    second, last = bits

    def to_owner(_, target):
        return ((target & second) != 0) == places[(target & first) != 0]

    unit = jnp.concatenate(
        [
            kept,
            hop(sent, "dp", dp_size, first, to_owner),
            hop(kept, "dp", dp_size, second, to_owner),
            hop(sent, "dp", dp_size, first | second, to_owner),
        ],
        axis=0,
    )
    half = unit.shape[1] // 2
    left, right = unit[:, :half], unit[:, half:]
    left = jnp.stack([left, hop(left, "dp", dp_size, last)])
    right = jnp.stack([right, hop(right, "ctx", 2, 1)])
    left = jnp.stack([left, hop(left, "ctx", 2, 1)])
    right = jnp.stack([right, hop(right, "dp", dp_size, last)], axis=1)
    rows = jnp.concatenate([left, right], axis=-1)
    return rows.reshape(-1, rows.shape[-1])


def scatter_rows(rows, first, places, bits, dp_size, masks):
    second, last = bits
    half = rows.shape[1] // 2
    rows = rows.reshape(2, 2, -1, rows.shape[1])
    left, right = rows[..., :half], rows[..., half:]

    def add(kept, came):
        return (kept.astype(jnp.float32) + came.astype(jnp.float32)).astype(jnp.bfloat16)

    left = add(left[0], hop(left[1], "ctx", 2, 1))
    right = jnp.where(masks[NEAR_LAST, :, half:] != 0, right[:, 0], hop(right[:, 1], "dp", dp_size, last))
    left = jnp.where(masks[NEAR_LAST, :, :half] != 0, left[0], hop(left[1], "dp", dp_size, last))
    right = add(right[0], hop(right[1], "ctx", 2, 1))
    unit = jnp.concatenate([left, right], axis=-1)
    here, across, beside, beyond = lax.optimization_barrier(jnp.split(unit, 4, axis=0))

    def from_owner(source, _):
        return ((source & second) != 0) == places[(source & first) != 0]

    across = hop(across, "dp", dp_size, first, from_owner)
    beside = hop(beside, "dp", dp_size, second, from_owner)
    beyond = hop(beyond, "dp", dp_size, first | second, from_owner)
    return (
        jnp.where(masks[NEAR_SECOND] != 0, here, beside),
        jnp.where(masks[OTHER_NEAR] != 0, across, beyond),
    )


def smem(count):
    return [pl.BlockSpec(memory_space=pltpu.SMEM)] * count


def vmem(count):
    return [pl.BlockSpec(memory_space=pltpu.VMEM)] * count


def body_move_rows(
    query_vecs,
    key_vecs,
    value_vecs,
    residual,
    w_out,
    norm_gain,
    w_gate_up,
    w_down,
    expert_ids,
    route_gates,
    capacity,
    expert_owner,
):
    token_count = query_vecs.shape[1]
    width = residual.shape[2]
    dp_size = lax.axis_size("dp")
    bits = [1 << k for k in reversed(range(1, dp_size.bit_length() - 1))]

    z_far, z_near, x_bit = bits
    z_both = z_far | z_near
    near = {0: w_out}
    for bit in (z_far, z_near, x_bit):
        near[bit] = hop(w_out, "dp", dp_size, bit)
    far = {0: hop(w_out, "dp", dp_size, 1)}
    key_before = lax.ppermute(key_vecs[0], "ctx", [(0, 1)])
    value_before = lax.ppermute(value_vecs[0], "ctx", [(0, 1)])
    own = jnp.stack([query_vecs[0], key_vecs[0], value_vecs[0]])
    numbers = jnp.concatenate([expert_owner[:PASS_SPECIALISTS], capacity[0, 0]])
    (
        near[z_far],
        near[z_near],
        near[x_bit],
        far[0],
        key_before,
        own,
        numbers,
        ids,
        gates,
    ) = lax.optimization_barrier(
        (
            near[z_far],
            near[z_near],
            near[x_bit],
            far[0],
            key_before,
            own,
            numbers,
            jnp.transpose(expert_ids[0]),
            jnp.transpose(route_gates[0]),
        )
    )
    near[z_near | x_bit] = hop(near[z_near], "dp", dp_size, x_bit)
    near[z_both] = hop(near[z_far], "dp", dp_size, z_near)
    near[z_far | x_bit] = hop(near[z_far], "dp", dp_size, x_bit)
    value_before, near[z_near | x_bit] = lax.optimization_barrier(
        (value_before, near[z_near | x_bit])
    )
    attended, select, gate_values, info = pl.pallas_call(
        functools.partial(attend_kernel, bits),
        out_shape=(
            jax.ShapeDtypeStruct((HEADS, token_count, HD), jnp.bfloat16),
            jax.ShapeDtypeStruct((PASS_SPECIALISTS, CAP, token_count), jnp.bfloat16),
            jax.ShapeDtypeStruct((token_count, PASS_SPECIALISTS), jnp.float32),
            jax.ShapeDtypeStruct((PASS_INFO + 2 * PASS_COUNT,), jnp.int32),
        ),
        in_specs=smem(1) + vmem(5),
        out_specs=tuple(vmem(3) + smem(1)),
        cost_estimate=pl.CostEstimate(
            flops=64 * HEADS * HD * 2 * token_count * token_count,
            bytes_accessed=6 * 2 * token_count * HEADS * HD,
            transcendentals=2 * HEADS * token_count * token_count,
        ),
        compiler_params=pltpu.CompilerParams(vmem_limit_bytes=8 * 2**20),
    )(numbers, own, key_before, value_before, ids, gates)
    near[z_both | x_bit] = hop(near[z_both], "dp", dp_size, x_bit)
    (
        near[z_near | x_bit],
        near[z_far | x_bit],
        between,
        attended,
    ) = lax.optimization_barrier(
        (near[z_near | x_bit], near[z_far | x_bit], near[z_both], attended)
    )
    for bit in (z_far, z_near, x_bit, z_near | x_bit, z_far | x_bit, z_both | x_bit):
        far[bit] = hop(near[bit], "dp", dp_size, 1)
    far[z_both] = hop(between, "dp", dp_size, 1)
    late_bits = (z_far | x_bit, z_both | x_bit)
    early_bits = tuple(bit for bit in near if bit not in late_bits)
    early_chips = [bit >> 1 for bit in early_bits]
    late_chips = [bit >> 1 for bit in late_bits]
    early = pl.pallas_call(
        functools.partial(early_kernel, early_chips),
        out_shape=jax.ShapeDtypeStruct((token_count, width), jnp.float32),
        in_specs=vmem(1 + 2 * len(early_bits)),
        out_specs=vmem(1)[0],
        cost_estimate=pl.CostEstimate(
            flops=4 * 2 * token_count * HEADS * HD * width,
            bytes_accessed=2 * HEADS * HD * width,
            transcendentals=0,
        ),
        compiler_params=pltpu.CompilerParams(vmem_limit_bytes=16 * 2**20),
    )(attended, *[near[bit] for bit in early_bits], *[far[bit] for bit in early_bits])
    gate_up_near = jnp.swapaxes(w_gate_up[0], 1, 2)

    some_rows = jax.ShapeDtypeStruct((CAP, width), jnp.bfloat16)
    all_rows = jax.ShapeDtypeStruct((token_count, width), jnp.bfloat16)
    attn_proj, kept, sent, second, last, expert_sum = pl.pallas_call(
        functools.partial(project_kernel, late_chips),
        out_shape=(all_rows, some_rows, some_rows, some_rows, some_rows, all_rows),
        in_specs=smem(1) + vmem(5 + 2 * len(late_bits)),
        out_specs=tuple(vmem(4) + [pl.BlockSpec(memory_space=pl.ANY)] * 2),
        scratch_shapes=[pltpu.VMEM((token_count, width), jnp.float32)],
        cost_estimate=pl.CostEstimate(
            flops=2 * token_count * HEADS * HD * width,
            bytes_accessed=2 * HEADS * HD * width,
            transcendentals=0,
        ),
        compiler_params=pltpu.CompilerParams(vmem_limit_bytes=16 * 2**20),
    )(
        info,
        attended,
        residual[0],
        norm_gain[None],
        select,
        early,
        *[near[bit] for bit in late_bits],
        *[far[bit] for bit in late_bits],
    )

    units = w_down.shape[1]
    row_count = dp_size * CAP

    def dispatch(bit, places):
        rest = [b for b in bits if b != bit]

        def run(kept, sent):
            gate_up_far = hop(gate_up_near, "dp", dp_size, 1)
            down_far = hop(w_down[0], "dp", dp_size, 1)
            rows = gather_rows(kept, sent, bit, places, rest, dp_size)
            return rows, gate_up_far, down_far

        return run

    def give_back(bit, places):
        rest = [b for b in bits if b != bit]

        def run(made, masks):
            return scatter_rows(made, bit, places, rest, dp_size, masks)

        return run

    branch = info[BRANCH]

    def one_pass(step, carried):
        kept, sent, last, _ = carried
        rows, gate_up_far, down_far = lax.switch(
            branch, [dispatch(*way) for way in branches(bits)], kept, sent
        )
        made, masks = pl.pallas_call(
            expert_kernel,
            out_shape=(
                jax.ShapeDtypeStruct((row_count, width), jnp.bfloat16),
                jax.ShapeDtypeStruct((PASS_COUNT, 1, width), jnp.float32),
            ),
            in_specs=smem(2) + vmem(1) + [pl.BlockSpec(memory_space=pltpu.HBM)] * 4,
            out_specs=tuple(vmem(2)),
            scratch_shapes=[
                pltpu.VMEM((2, units, width), jnp.bfloat16),
                pltpu.VMEM((units, width), jnp.bfloat16),
                pltpu.VMEM((row_count, units), jnp.bfloat16),
                pltpu.SemaphoreType.DMA((2 * -(-units // 256) + 1,)),
            ],
            cost_estimate=pl.CostEstimate(
                flops=6 * row_count * units * width,
                bytes_accessed=6 * units * width,
                transcendentals=row_count * units,
            ),
            compiler_params=pltpu.CompilerParams(vmem_limit_bytes=22 * 2**20),
        )(info, step[None], rows, gate_up_near, gate_up_far, w_down[0], down_far)
        own, other = lax.switch(branch, [give_back(*way) for way in branches(bits)], made, masks)
        expert_sum, last, kept, sent = pl.pallas_call(
            combine_kernel,
            out_shape=(all_rows, some_rows, some_rows, some_rows),
            in_specs=smem(2) + vmem(6),
            out_specs=tuple(vmem(4)),
            compiler_params=pltpu.CompilerParams(vmem_limit_bytes=8 * 2**20),
        )(info, step[None], own, other, last, second, select, gate_values)
        return kept, sent, last, expert_sum

    carried = (kept, sent, last, expert_sum)
    expert_sum = lax.fori_loop(0, info[PASSES], one_pass, carried)[3]
    return (attn_proj[None], expert_sum[None])


def solution(mesh):
    placed = (
        P("dp", "ctx", None),
        P("dp", "ctx", None),
        P("dp", "ctx", None),
        P("dp", "ctx", None),
        P("dp", None),
        P(),
        P("dp", None, None, "ctx"),
        P("dp", "ctx", None),
        P("dp", "ctx", None),
        P("dp", "ctx", None),
        P("dp", "ctx", None),
        P(),
    )
    dp_size, ctx_size = mesh.shape["dp"], mesh.shape["ctx"]
    small = ctx_size == 2 and dp_size == 2 * HEADS
    return jax.shard_map(
        body_move_rows if small else body_move_weights,
        mesh=mesh,
        in_specs=placed,
        out_specs=(P("dp", "ctx", None), P("dp", "ctx", None)),
        check_vma=False,
    )
```

```python
import functools

import jax
import jax.numpy as jnp
from jax import lax
from jax.experimental import pallas as pl
from jax.experimental.pallas import tpu as pltpu
from jax.sharding import PartitionSpec as P

HEADS = 8
HD = 128
PASS_SPECIALISTS = 2
CAP = 24


EPSILON = 1e-06
LOWEST = -1e30


def broadcast(array, axis, root):
    mine = lax.axis_index(axis) == root
    return lax.psum(jnp.where(mine, array, jnp.zeros_like(array)), axis)


def hop(array, axis, size, bit, wanted=None):
    pairs = [(i, i ^ bit) for i in range(size)]
    if wanted is not None:
        pairs = [pair for pair in pairs if wanted(*pair)]
    return lax.ppermute(array, axis, pairs)


def route_slots(expert_ids, route_gates, capacity, expert):
    matches = expert_ids == expert
    routed = jnp.any(matches, axis=1)
    gate_value = jnp.sum(jnp.where(matches, route_gates, 0.0), axis=1)
    slot_rank = jnp.cumsum(routed.astype(jnp.int32)) - 1
    kept_mask = routed & (slot_rank < capacity[expert])
    return (slot_rank, kept_mask, gate_value)


def attend(queries, key_block, value_block, visible):
    width = key_block.shape[0]
    token_count = queries.shape[0]
    query_heads = queries.reshape(token_count, HEADS, HD)
    key_heads = key_block.reshape(width, HEADS, HD)
    value_heads = value_block.reshape(width, HEADS, HD)
    gating_logits = jnp.einsum(
        "qhd,khd->qhk", query_heads, key_heads, preferred_element_type=jnp.float32
    ) * HD ** (-0.5)
    gating_logits = jnp.where(visible[:, None, :], gating_logits, -jnp.inf)
    row_top = jnp.max(gating_logits, axis=-1)
    weights = jnp.exp(gating_logits - row_top[:, :, None])
    denominator = jnp.sum(weights, axis=-1)
    weighted = jnp.einsum(
        "qhk,khd->qhd",
        weights.astype(jnp.bfloat16),
        value_heads,
        preferred_element_type=jnp.float32,
    )
    attended = (weighted / denominator[:, :, None]).astype(jnp.bfloat16)
    return attended.reshape(token_count, HEADS * HD)


def feed_forward(rows, gate_up, down_part):
    gate_proj = jnp.dot(rows, gate_up[0], preferred_element_type=jnp.float32)
    up_proj = jnp.dot(rows, gate_up[1], preferred_element_type=jnp.float32)
    hidden = (jax.nn.silu(gate_proj) * up_proj).astype(jnp.bfloat16)
    return jnp.dot(hidden, down_part, preferred_element_type=jnp.float32).astype(jnp.bfloat16)


def normalise(attn_proj, residual, norm_gain):
    combined = residual.astype(jnp.float32) + attn_proj.astype(jnp.float32)
    return (
        combined
        * lax.rsqrt(jnp.mean(combined * combined, axis=-1, keepdims=True) + EPSILON)
        * norm_gain
    ).astype(jnp.bfloat16)


def pick_rows(routing, normed):
    slot_ids = jnp.arange(CAP)
    select = [
        (slot_rank[None, :] == slot_ids[:, None]) & kept_mask[None, :]
        for slot_rank, kept_mask, _ in routing
    ]
    select = jnp.concatenate(select, axis=0).astype(jnp.bfloat16)
    chosen = jnp.dot(select, normed, preferred_element_type=jnp.float32).astype(jnp.bfloat16)
    return chosen.reshape(PASS_SPECIALISTS, CAP, normed.shape[1])


def combine_rows(routing, produced):
    slot_ids = jnp.arange(CAP)
    summed = 0.0
    for expert in range(PASS_SPECIALISTS):
        slot_rank, kept_mask, gate_value = routing[expert]
        place = ((slot_rank[:, None] == slot_ids[None, :]) & kept_mask[:, None]).astype(
            jnp.bfloat16
        )
        picked = jnp.dot(place, produced[expert], preferred_element_type=jnp.float32)
        summed = summed + gate_value[:, None] * picked
    return summed.astype(jnp.bfloat16)


def body_move_weights(
    query_vecs,
    key_vecs,
    value_vecs,
    residual,
    w_out,
    norm_gain,
    w_gate_up,
    w_down,
    expert_ids,
    route_gates,
    capacity,
    expert_owner,
):
    token_count = query_vecs.shape[1]
    weights_in = []
    for expert in range(PASS_SPECIALISTS):
        weights_in.append(
            (
                broadcast(w_gate_up[0], "dp", expert_owner[expert]),
                broadcast(w_down[0], "dp", expert_owner[expert]),
            )
        )
    keys = lax.all_gather(key_vecs[0], "ctx", axis=0, tiled=True)
    values = lax.all_gather(value_vecs[0], "ctx", axis=0, tiled=True)
    first_row = lax.axis_index("ctx") * token_count
    query_pos = first_row + jnp.arange(token_count)
    visible = jnp.arange(keys.shape[0])[None, :] <= query_pos[:, None]
    attended = attend(query_vecs[0], keys, values, visible)
    projected = jnp.dot(
        attended,
        lax.all_gather(w_out, "dp", axis=0, tiled=True),
        preferred_element_type=jnp.float32,
    )
    attn_proj = projected.astype(jnp.bfloat16)
    normed = normalise(attn_proj, residual[0], norm_gain)
    routing = [
        route_slots(expert_ids[0], route_gates[0], capacity[0, 0], expert)
        for expert in range(PASS_SPECIALISTS)
    ]
    chosen = pick_rows(routing, normed)
    routed_rows = lax.all_gather(jnp.swapaxes(chosen, 0, 1), "ctx", axis=0, tiled=True)
    outputs = [
        feed_forward(routed_rows[:, expert], *weights_in[expert])
        for expert in range(PASS_SPECIALISTS)
    ]
    expert_out = lax.psum_scatter(
        jnp.stack(outputs, axis=1), "ctx", scatter_dimension=0, tiled=True
    )
    expert_sum = combine_rows(routing, [expert_out[:, e] for e in range(PASS_SPECIALISTS)])
    return (attn_proj[None], expert_sum[None])


CTX, CHIP, CORE, FIRST, FIRST_CAP, SECOND, SECOND_CAP, SAME = range(8)
FIRST_HERE, SECOND_HERE, PASSES, BRANCH, PASS_INFO = range(8, 13)
USE_FAR, NEAR_LAST, NEAR_SECOND, OTHER_NEAR, PASS_COUNT = range(5)


def work_out_places(bits, numbers, info):
    owners = [numbers[k] for k in range(PASS_SPECIALISTS)]
    caps = [numbers[PASS_SPECIALISTS + k] for k in range(PASS_SPECIALISTS)]
    me = lax.axis_index("dp")
    differ = owners[0] ^ owners[1]
    branch = 0
    split_bit = 0
    rest = [bits[1], bits[2]]
    for k in reversed(range(len(bits))):
        parted = (differ & bits[k]) != 0
        branch = jnp.where(parted, k, branch)
        split_bit = jnp.where(parted, bits[k], split_bit)
        others = [bit for bit in bits if bit != bits[k]]
        rest = [jnp.where(parted, others[i], rest[i]) for i in range(2)]
    same = split_bit == 0
    swapped = ((me ^ owners[0]) & split_bit) != 0
    first_offset = me ^ jnp.where(swapped, owners[1], owners[0])
    second_offset = me ^ jnp.where(swapped, owners[0], owners[1])

    def put(place, value):
        info[place] = value.astype(jnp.int32)

    put(CTX, lax.axis_index("ctx"))
    put(CHIP, me >> 1)
    put(CORE, me & 1)
    put(FIRST, jnp.where(swapped, 1, 0))
    put(FIRST_CAP, jnp.where(swapped, caps[1], caps[0]))
    put(SECOND, jnp.where(swapped, 0, 1))
    put(SECOND_CAP, jnp.where(swapped, caps[0], caps[1]))
    put(SAME, jnp.where(same, 1, 0))
    put(FIRST_HERE, jnp.where((first_offset & bits[0]) == 0, 1, 0))
    put(SECOND_HERE, jnp.where((second_offset & bits[0]) == 0, 1, 0))
    put(PASSES, jnp.where(same, 2, 1))
    on_one = (owners[0] & jnp.where(same, bits[0], split_bit)) != 0
    seconds = [jnp.where((owners[k] & rest[0]) == 0, 0, 1) for k in range(2)]
    at_zero = jnp.where(on_one, seconds[1], seconds[0])
    at_one = jnp.where(on_one, seconds[0], seconds[1])
    at_one = jnp.where(same, at_zero, at_one)
    put(BRANCH, jnp.where(branch == 0, 2 * at_zero + at_one, 2 + 2 * branch + at_zero))
    pairs = (
        (first_offset, jnp.where(same, first_offset, second_offset)),
        (second_offset, second_offset),
    )
    for k, (offset, other_offset) in enumerate(pairs):
        base = PASS_INFO + k * PASS_COUNT
        put(base + USE_FAR, offset & 1)
        put(base + NEAR_LAST, jnp.where((offset & rest[1]) == 0, 1, 0))
        put(base + NEAR_SECOND, jnp.where((offset & rest[0]) == 0, 1, 0))
        put(base + OTHER_NEAR, jnp.where((other_offset & rest[0]) == 0, 1, 0))


def branches(bits):
    return [(bits[0], (zero, one)) for zero in range(2) for one in range(2)] + [
        (bit, (both, both)) for bit in bits[1:] for both in range(2)
    ]


def attend_kernel(bits, numbers, own_vecs, key_before, value_before, ids, gates, *outs):
    attended, select, gate_values, info = outs
    query, key, value = (own_vecs.at[k] for k in range(3))
    work_out_places(bits, numbers, info)
    token_count = query.shape[0]
    row = lax.broadcasted_iota(jnp.int32, (token_count, token_count), 0)
    col = lax.broadcasted_iota(jnp.int32, (token_count, token_count), 1)
    own_visible = col <= row
    before_visible = jnp.broadcast_to(info[CTX], (token_count, token_count)) == 1
    contract_last = (((1,), (1,)), ((), ()))
    for head in range(HEADS):
        span = slice(head * HD, (head + 1) * HD)
        heads = query[:, span]
        own = lax.dot_general(
            heads, key[:, span], contract_last, preferred_element_type=jnp.float32
        )
        before = lax.dot_general(
            heads, key_before[:, span], contract_last, preferred_element_type=jnp.float32
        )
        own = jnp.where(own_visible, own * HD ** (-0.5), -jnp.inf)
        before = jnp.where(before_visible, before * HD ** (-0.5), -jnp.inf)
        top = jnp.maximum(
            jnp.max(own, axis=1, keepdims=True), jnp.max(before, axis=1, keepdims=True)
        )
        own = jnp.exp(own - top)
        before = jnp.exp(before - top)
        total = jnp.sum(own, axis=1, keepdims=True) + jnp.sum(before, axis=1, keepdims=True)
        mixed = jnp.dot(
            own.astype(jnp.bfloat16), value[:, span], preferred_element_type=jnp.float32
        ) + jnp.dot(
            before.astype(jnp.bfloat16), value_before[:, span], preferred_element_type=jnp.float32
        )
        mixed = mixed / total
        swapped = pltpu.roll(mixed, HD // 2, 1)
        mixed = jnp.where(jnp.broadcast_to(info[CORE], mixed.shape) == 0, mixed, swapped)
        attended[head ^ info[CHIP]] = mixed.astype(jnp.bfloat16)

    slot = lax.broadcasted_iota(jnp.int32, (CAP, token_count), 0)
    earlier = (row < col).astype(jnp.bfloat16)
    for k in range(PASS_SPECIALISTS):
        matches = ids[...] == info[FIRST + 2 * k]
        named = jnp.max(matches.astype(jnp.float32), axis=0, keepdims=True)
        gate_row = jnp.sum(jnp.where(matches, gates[...], 0.0), axis=0, keepdims=True)
        gate_values[:, k : k + 1] = jnp.sum(
            jnp.where(row == col, jnp.broadcast_to(gate_row, row.shape), 0.0),
            axis=1,
            keepdims=True,
        )
        routed = jnp.broadcast_to(named, (CAP, token_count))
        rank = jnp.dot(
            routed.astype(jnp.bfloat16), earlier, preferred_element_type=jnp.float32
        ).astype(jnp.int32)
        kept = (routed > 0.0) & (rank == slot) & (rank < info[FIRST_CAP + 2 * k])
        select[k] = kept.astype(jnp.bfloat16)


def add_products(attended, chips, near, far, span, total):
    for pair in range(0, len(chips), 2):
        one, two = chips[pair], chips[pair + 1]
        left = jnp.concatenate([attended[one], attended[two]], axis=1)
        right = jnp.concatenate(
            [near[pair][:, span], far[pair][:, span]]
            + [near[pair + 1][:, span], far[pair + 1][:, span]],
            axis=0,
        )
        product = jnp.dot(left, right, preferred_element_type=jnp.float32)
        total = product if total is None else total + product
    return total


def early_kernel(chips, attended, *refs):
    near, far = refs[: len(chips)], refs[len(chips) : -1]
    total = refs[-1]
    for start in range(0, total.shape[1], 512):
        span = slice(start, start + 512)
        total[:, span] = add_products(attended, chips, near, far, span, None)


def project_kernel(chips, info, attended, residual, gain, select, early, *refs):
    near, far = refs[: len(chips)], refs[len(chips) : 2 * len(chips)]
    attn_proj, kept, sent, second, _, _, combined = refs[-7:]
    token_count, width = residual.shape
    tile = 512
    squares = jnp.zeros((token_count, 1), jnp.float32)
    for start in range(0, width, tile):
        span = slice(start, start + tile)
        total = add_products(attended, chips, near, far, span, early[:, span])
        rounded = total.astype(jnp.bfloat16)
        attn_proj[:, span] = rounded
        added = residual[:, span].astype(jnp.float32) + rounded.astype(jnp.float32)
        combined[:, span] = added
        squares = squares + jnp.sum(added * added, axis=1, keepdims=True)
    scale = lax.rsqrt(squares / width + EPSILON)
    for start in range(0, width, tile):
        span = slice(start, start + tile)
        normed = (combined[:, span] * scale * gain[:, span]).astype(jnp.bfloat16)
        rows = [
            jnp.dot(select[k], normed, preferred_element_type=jnp.float32)
            for k in range(PASS_SPECIALISTS)
        ]
        kept[:, span] = rows[0].astype(jnp.bfloat16)
        second[:, span] = rows[1].astype(jnp.bfloat16)
        use_first = jnp.broadcast_to(info[SAME], rows[0].shape) != 0
        sent[:, span] = jnp.where(use_first, rows[0], rows[1]).astype(jnp.bfloat16)


def combine_kernel(info, step, own, other, last, second, select, gate_values, *outs):
    out, next_last, next_kept, next_sent = outs
    same = info[SAME] != 0
    contract_first = (((0,), (0,)), ((), ()))

    def add_up(first_rows, second_rows):
        total = 0.0
        for k, rows in enumerate((first_rows, second_rows)):
            picked = lax.dot_general(
                select[k], rows, contract_first, preferred_element_type=jnp.float32
            )
            total = total + gate_values[:, k : k + 1] * picked
        return total.astype(jnp.bfloat16)

    @pl.when(jnp.logical_not(same))
    def _():
        for start in range(0, own.shape[1], 512):
            span = slice(start, start + 512)
            out[:, span] = add_up(own[:, span], other[:, span])

    @pl.when(same)
    def _():
        here = jnp.where(step[0] == 0, info[FIRST_HERE], info[SECOND_HERE])
        for start in range(0, own.shape[1], 512):
            span = slice(start, start + 512)
            use_own = jnp.broadcast_to(here, (own.shape[0], 512)) != 0
            served = jnp.where(
                use_own, own[:, span].astype(jnp.float32), other[:, span].astype(jnp.float32)
            ).astype(jnp.bfloat16)
            out[:, span] = add_up(last[:, span], served)
            next_last[:, span] = served
            next_kept[:, span] = second[:, span]
            next_sent[:, span] = second[:, span]


def expert_kernel(
    info,
    step,
    rows,
    gate_up_near,
    gate_up_far,
    down_near,
    down_far,
    made,
    masks,
    gate_up,
    down,
    sums,
    hidden,
    sems,
):
    units, width = down.shape
    piece = 512
    starts = list(range(0, width, piece))

    def copies(gate_up_from, down_from):
        spans = [pl.ds(start, piece) for start in starts]
        out = [
            pltpu.make_async_copy(gate_up_from.at[:, :, span], gate_up.at[:, :, span], sems.at[k])
            for k, span in enumerate(spans)
        ]
        return out + [pltpu.make_async_copy(down_from, down, sems.at[len(starts)])]

    base = PASS_INFO + PASS_COUNT * step[0]
    use_far = info[base + USE_FAR]

    def start_copy(stage):
        @pl.when(use_far == 0)
        def _():
            copies(gate_up_near, down_near)[stage].start()

        @pl.when(use_far != 0)
        def _():
            copies(gate_up_far, down_far)[stage].start()

    start_copy(0)
    start_copy(1)
    for k in (NEAR_LAST, NEAR_SECOND, OTHER_NEAR):
        masks[k] = jnp.broadcast_to(info[base + k].astype(jnp.float32), masks.shape[1:])

    arrived = copies(gate_up_near, down_near)
    contract_last = (((1,), (1,)), ((), ()))
    for k, start in enumerate(starts):
        span = slice(start, start + piece)
        arrived[k].wait()
        if k + 2 < len(arrived):
            start_copy(k + 2)
        product = lax.dot_general(
            gate_up[:, :, span].reshape(2 * units, piece),
            rows[:, span],
            contract_last,
            preferred_element_type=jnp.float32,
        )
        if k == 0:
            sums[...] = product
        else:
            sums[...] += product
    for start in range(0, units, 256):
        stop = min(start + 256, units)
        gate_proj, up_proj = sums[start:stop], sums[units + start : units + stop]
        made_hidden = gate_proj / (1.0 + jnp.exp(-gate_proj)) * up_proj
        hidden[:, start:stop] = jnp.transpose(made_hidden).astype(jnp.bfloat16)
    arrived[-1].wait()
    for start in range(0, width, 512):
        span = slice(start, start + 512)
        made[:, span] = jnp.dot(
            hidden[...], down[:, span], preferred_element_type=jnp.float32
        ).astype(jnp.bfloat16)


def gather_rows(kept, sent, first, places, bits, dp_size):
    second, last = bits

    def to_owner(_, target):
        return ((target & second) != 0) == places[(target & first) != 0]

    beside = hop(kept, "dp", dp_size, second, to_owner)
    across = hop(sent, "dp", dp_size, first, to_owner)
    beyond = hop(sent, "dp", dp_size, first | second, to_owner)
    unit = jnp.concatenate([kept, beside, across, beyond], axis=0)
    half = unit.shape[1] // 2
    left, right = unit[:, :half], unit[:, half:]
    left = jnp.stack([left, hop(left, "dp", dp_size, last)])
    right = jnp.stack([right, hop(right, "ctx", 2, 1)])
    left = jnp.stack([left, hop(left, "ctx", 2, 1)])
    right = jnp.stack([right, hop(right, "dp", dp_size, last)], axis=1)
    rows = jnp.concatenate([left, right], axis=-1)
    return rows.reshape(-1, rows.shape[-1])


def scatter_rows(rows, first, places, bits, dp_size, masks):
    second, last = bits
    half = rows.shape[1] // 2
    rows = rows.reshape(2, 2, -1, rows.shape[1])
    left, right = rows[..., :half], rows[..., half:]

    def add(kept, came):
        return (kept.astype(jnp.float32) + came.astype(jnp.float32)).astype(jnp.bfloat16)

    left = add(left[0], hop(left[1], "ctx", 2, 1))
    right = jnp.where(masks[NEAR_LAST, :, half:] != 0, right[:, 0], hop(right[:, 1], "dp", dp_size, last))
    left = jnp.where(masks[NEAR_LAST, :, :half] != 0, left[0], hop(left[1], "dp", dp_size, last))
    right = add(right[0], hop(right[1], "ctx", 2, 1))
    unit = jnp.concatenate([left, right], axis=-1)
    here, beside, across, beyond = lax.optimization_barrier(jnp.split(unit, 4, axis=0))

    def from_owner(source, _):
        return ((source & second) != 0) == places[(source & first) != 0]

    across = hop(across, "dp", dp_size, first, from_owner)
    beside = hop(beside, "dp", dp_size, second, from_owner)
    beyond = hop(beyond, "dp", dp_size, first | second, from_owner)
    return (
        jnp.where(masks[NEAR_SECOND] != 0, here, beside),
        jnp.where(masks[OTHER_NEAR] != 0, across, beyond),
    )


def smem(count):
    return [pl.BlockSpec(memory_space=pltpu.SMEM)] * count


def vmem(count):
    return [pl.BlockSpec(memory_space=pltpu.VMEM)] * count


def body_move_rows(
    query_vecs,
    key_vecs,
    value_vecs,
    residual,
    w_out,
    norm_gain,
    w_gate_up,
    w_down,
    expert_ids,
    route_gates,
    capacity,
    expert_owner,
):
    token_count = query_vecs.shape[1]
    width = residual.shape[2]
    dp_size = lax.axis_size("dp")
    bits = [1 << k for k in reversed(range(1, dp_size.bit_length() - 1))]

    z_far, z_near, x_bit = bits
    z_both = z_far | z_near
    near = {0: w_out}
    for bit in (z_far, z_near, x_bit):
        near[bit] = hop(w_out, "dp", dp_size, bit)
    far = {0: hop(w_out, "dp", dp_size, 1)}
    key_before = lax.ppermute(key_vecs[0], "ctx", [(0, 1)])
    value_before = lax.ppermute(value_vecs[0], "ctx", [(0, 1)])
    own = jnp.stack([query_vecs[0], key_vecs[0], value_vecs[0]])
    numbers = jnp.concatenate([expert_owner[:PASS_SPECIALISTS], capacity[0, 0]])
    (
        near[z_far],
        near[z_near],
        near[x_bit],
        far[0],
        key_before,
        own,
        numbers,
        ids,
        gates,
    ) = lax.optimization_barrier(
        (
            near[z_far],
            near[z_near],
            near[x_bit],
            far[0],
            key_before,
            own,
            numbers,
            jnp.transpose(expert_ids[0]),
            jnp.transpose(route_gates[0]),
        )
    )
    near[z_near | x_bit] = hop(near[z_near], "dp", dp_size, x_bit)
    near[z_both] = hop(near[z_far], "dp", dp_size, z_near)
    near[z_far | x_bit] = hop(near[z_far], "dp", dp_size, x_bit)
    value_before, near[z_near | x_bit] = lax.optimization_barrier(
        (value_before, near[z_near | x_bit])
    )
    attended, select, gate_values, info = pl.pallas_call(
        functools.partial(attend_kernel, bits),
        out_shape=(
            jax.ShapeDtypeStruct((HEADS, token_count, HD), jnp.bfloat16),
            jax.ShapeDtypeStruct((PASS_SPECIALISTS, CAP, token_count), jnp.bfloat16),
            jax.ShapeDtypeStruct((token_count, PASS_SPECIALISTS), jnp.float32),
            jax.ShapeDtypeStruct((PASS_INFO + 2 * PASS_COUNT,), jnp.int32),
        ),
        in_specs=smem(1) + vmem(5),
        out_specs=tuple(vmem(3) + smem(1)),
        cost_estimate=pl.CostEstimate(
            flops=64 * HEADS * HD * 2 * token_count * token_count,
            bytes_accessed=6 * 2 * token_count * HEADS * HD,
            transcendentals=2 * HEADS * token_count * token_count,
        ),
        compiler_params=pltpu.CompilerParams(vmem_limit_bytes=8 * 2**20),
    )(numbers, own, key_before, value_before, ids, gates)
    near[z_both | x_bit] = hop(near[z_both], "dp", dp_size, x_bit)
    (
        near[z_near | x_bit],
        near[z_far | x_bit],
        between,
        attended,
    ) = lax.optimization_barrier(
        (near[z_near | x_bit], near[z_far | x_bit], near[z_both], attended)
    )
    for bit in (z_far, z_near, x_bit, z_near | x_bit, z_far | x_bit, z_both | x_bit):
        far[bit] = hop(near[bit], "dp", dp_size, 1)
    far[z_both] = hop(between, "dp", dp_size, 1)
    late_bits = (z_far | x_bit, z_both | x_bit)
    early_bits = tuple(bit for bit in near if bit not in late_bits)
    early_chips = [bit >> 1 for bit in early_bits]
    late_chips = [bit >> 1 for bit in late_bits]
    early = pl.pallas_call(
        functools.partial(early_kernel, early_chips),
        out_shape=jax.ShapeDtypeStruct((token_count, width), jnp.float32),
        in_specs=vmem(1 + 2 * len(early_bits)),
        out_specs=vmem(1)[0],
        cost_estimate=pl.CostEstimate(
            flops=4 * 2 * token_count * HEADS * HD * width,
            bytes_accessed=2 * HEADS * HD * width,
            transcendentals=0,
        ),
        compiler_params=pltpu.CompilerParams(vmem_limit_bytes=16 * 2**20),
    )(attended, *[near[bit] for bit in early_bits], *[far[bit] for bit in early_bits])
    gate_up_near = jnp.swapaxes(w_gate_up[0], 1, 2)

    some_rows = jax.ShapeDtypeStruct((CAP, width), jnp.bfloat16)
    all_rows = jax.ShapeDtypeStruct((token_count, width), jnp.bfloat16)
    attn_proj, kept, sent, second, last, expert_sum = pl.pallas_call(
        functools.partial(project_kernel, late_chips),
        out_shape=(all_rows, some_rows, some_rows, some_rows, some_rows, all_rows),
        in_specs=smem(1) + vmem(5 + 2 * len(late_bits)),
        out_specs=tuple(vmem(4) + [pl.BlockSpec(memory_space=pl.ANY)] * 2),
        scratch_shapes=[pltpu.VMEM((token_count, width), jnp.float32)],
        cost_estimate=pl.CostEstimate(
            flops=2 * token_count * HEADS * HD * width,
            bytes_accessed=2 * HEADS * HD * width,
            transcendentals=0,
        ),
        compiler_params=pltpu.CompilerParams(vmem_limit_bytes=16 * 2**20),
    )(
        info,
        attended,
        residual[0],
        norm_gain[None],
        select,
        early,
        *[near[bit] for bit in late_bits],
        *[far[bit] for bit in late_bits],
    )

    units = w_down.shape[1]
    row_count = dp_size * CAP

    def dispatch(bit, places):
        rest = [b for b in bits if b != bit]

        def run(kept, sent):
            gate_up_far = hop(gate_up_near, "dp", dp_size, 1)
            down_far = hop(w_down[0], "dp", dp_size, 1)
            rows = gather_rows(kept, sent, bit, places, rest, dp_size)
            return rows, gate_up_far, down_far

        return run

    def give_back(bit, places):
        rest = [b for b in bits if b != bit]

        def run(made, masks):
            return scatter_rows(made, bit, places, rest, dp_size, masks)

        return run

    branch = info[BRANCH]

    def one_pass(step, carried):
        kept, sent, last, _ = carried
        rows, gate_up_far, down_far = lax.switch(
            branch, [dispatch(*way) for way in branches(bits)], kept, sent
        )
        made, masks = pl.pallas_call(
            expert_kernel,
            out_shape=(
                jax.ShapeDtypeStruct((row_count, width), jnp.bfloat16),
                jax.ShapeDtypeStruct((PASS_COUNT, 1, width), jnp.float32),
            ),
            in_specs=smem(2) + vmem(1) + [pl.BlockSpec(memory_space=pltpu.HBM)] * 4,
            out_specs=tuple(vmem(2)),
            scratch_shapes=[
                pltpu.VMEM((2, units, width), jnp.bfloat16),
                pltpu.VMEM((units, width), jnp.bfloat16),
                pltpu.VMEM((2 * units, row_count), jnp.float32),
                pltpu.VMEM((row_count, units), jnp.bfloat16),
                pltpu.SemaphoreType.DMA((width // 512 + 1,)),
            ],
            cost_estimate=pl.CostEstimate(
                flops=6 * row_count * units * width,
                bytes_accessed=6 * units * width,
                transcendentals=row_count * units,
            ),
            compiler_params=pltpu.CompilerParams(vmem_limit_bytes=26 * 2**20),
        )(info, step[None], rows, gate_up_near, gate_up_far, w_down[0], down_far)
        own, other = lax.switch(branch, [give_back(*way) for way in branches(bits)], made, masks)
        expert_sum, last, kept, sent = pl.pallas_call(
            combine_kernel,
            out_shape=(all_rows, some_rows, some_rows, some_rows),
            in_specs=smem(2) + vmem(6),
            out_specs=tuple(vmem(4)),
            compiler_params=pltpu.CompilerParams(vmem_limit_bytes=8 * 2**20),
        )(info, step[None], own, other, last, second, select, gate_values)
        return kept, sent, last, expert_sum

    carried = (kept, sent, last, expert_sum)
    expert_sum = lax.fori_loop(0, info[PASSES], one_pass, carried)[3]
    return (attn_proj[None], expert_sum[None])


def solution(mesh):
    placed = (
        P("dp", "ctx", None),
        P("dp", "ctx", None),
        P("dp", "ctx", None),
        P("dp", "ctx", None),
        P("dp", None),
        P(),
        P("dp", None, None, "ctx"),
        P("dp", "ctx", None),
        P("dp", "ctx", None),
        P("dp", "ctx", None),
        P("dp", "ctx", None),
        P(),
    )
    dp_size, ctx_size = mesh.shape["dp"], mesh.shape["ctx"]
    small = ctx_size == 2 and dp_size == 2 * HEADS
    return jax.shard_map(
        body_move_rows if small else body_move_weights,
        mesh=mesh,
        in_specs=placed,
        out_specs=(P("dp", "ctx", None), P("dp", "ctx", None)),
        check_vma=False,
    )
```

```python
import functools

import jax
import jax.numpy as jnp
from jax import lax
from jax.experimental import pallas as pl
from jax.experimental.pallas import tpu as pltpu
from jax.sharding import PartitionSpec as P

HEADS = 8
HD = 128
PASS_SPECIALISTS = 2
CAP = 24


EPSILON = 1e-06
LOWEST = -1e30


def broadcast(array, axis, root):
    mine = lax.axis_index(axis) == root
    return lax.psum(jnp.where(mine, array, jnp.zeros_like(array)), axis)


def hop(array, axis, size, bit, wanted=None):
    pairs = [(i, i ^ bit) for i in range(size)]
    if wanted is not None:
        pairs = [pair for pair in pairs if wanted(*pair)]
    return lax.ppermute(array, axis, pairs)


def route_slots(expert_ids, route_gates, capacity, expert):
    matches = expert_ids == expert
    routed = jnp.any(matches, axis=1)
    gate_value = jnp.sum(jnp.where(matches, route_gates, 0.0), axis=1)
    slot_rank = jnp.cumsum(routed.astype(jnp.int32)) - 1
    kept_mask = routed & (slot_rank < capacity[expert])
    return (slot_rank, kept_mask, gate_value)


def attend(queries, key_block, value_block, visible):
    width = key_block.shape[0]
    token_count = queries.shape[0]
    query_heads = queries.reshape(token_count, HEADS, HD)
    key_heads = key_block.reshape(width, HEADS, HD)
    value_heads = value_block.reshape(width, HEADS, HD)
    gating_logits = jnp.einsum(
        "qhd,khd->qhk", query_heads, key_heads, preferred_element_type=jnp.float32
    ) * HD ** (-0.5)
    gating_logits = jnp.where(visible[:, None, :], gating_logits, -jnp.inf)
    row_top = jnp.max(gating_logits, axis=-1)
    weights = jnp.exp(gating_logits - row_top[:, :, None])
    denominator = jnp.sum(weights, axis=-1)
    weighted = jnp.einsum(
        "qhk,khd->qhd",
        weights.astype(jnp.bfloat16),
        value_heads,
        preferred_element_type=jnp.float32,
    )
    attended = (weighted / denominator[:, :, None]).astype(jnp.bfloat16)
    return attended.reshape(token_count, HEADS * HD)


def feed_forward(rows, gate_up, down_part):
    gate_proj = jnp.dot(rows, gate_up[0], preferred_element_type=jnp.float32)
    up_proj = jnp.dot(rows, gate_up[1], preferred_element_type=jnp.float32)
    hidden = (jax.nn.silu(gate_proj) * up_proj).astype(jnp.bfloat16)
    return jnp.dot(hidden, down_part, preferred_element_type=jnp.float32).astype(jnp.bfloat16)


def normalise(attn_proj, residual, norm_gain):
    combined = residual.astype(jnp.float32) + attn_proj.astype(jnp.float32)
    return (
        combined
        * lax.rsqrt(jnp.mean(combined * combined, axis=-1, keepdims=True) + EPSILON)
        * norm_gain
    ).astype(jnp.bfloat16)


def pick_rows(routing, normed):
    slot_ids = jnp.arange(CAP)
    select = [
        (slot_rank[None, :] == slot_ids[:, None]) & kept_mask[None, :]
        for slot_rank, kept_mask, _ in routing
    ]
    select = jnp.concatenate(select, axis=0).astype(jnp.bfloat16)
    chosen = jnp.dot(select, normed, preferred_element_type=jnp.float32).astype(jnp.bfloat16)
    return chosen.reshape(PASS_SPECIALISTS, CAP, normed.shape[1])


def combine_rows(routing, produced):
    slot_ids = jnp.arange(CAP)
    summed = 0.0
    for expert in range(PASS_SPECIALISTS):
        slot_rank, kept_mask, gate_value = routing[expert]
        place = ((slot_rank[:, None] == slot_ids[None, :]) & kept_mask[:, None]).astype(
            jnp.bfloat16
        )
        picked = jnp.dot(place, produced[expert], preferred_element_type=jnp.float32)
        summed = summed + gate_value[:, None] * picked
    return summed.astype(jnp.bfloat16)


def body_move_weights(
    query_vecs,
    key_vecs,
    value_vecs,
    residual,
    w_out,
    norm_gain,
    w_gate_up,
    w_down,
    expert_ids,
    route_gates,
    capacity,
    expert_owner,
):
    token_count = query_vecs.shape[1]
    weights_in = []
    for expert in range(PASS_SPECIALISTS):
        weights_in.append(
            (
                broadcast(w_gate_up[0], "dp", expert_owner[expert]),
                broadcast(w_down[0], "dp", expert_owner[expert]),
            )
        )
    keys = lax.all_gather(key_vecs[0], "ctx", axis=0, tiled=True)
    values = lax.all_gather(value_vecs[0], "ctx", axis=0, tiled=True)
    first_row = lax.axis_index("ctx") * token_count
    query_pos = first_row + jnp.arange(token_count)
    visible = jnp.arange(keys.shape[0])[None, :] <= query_pos[:, None]
    attended = attend(query_vecs[0], keys, values, visible)
    projected = jnp.dot(
        attended,
        lax.all_gather(w_out, "dp", axis=0, tiled=True),
        preferred_element_type=jnp.float32,
    )
    attn_proj = projected.astype(jnp.bfloat16)
    normed = normalise(attn_proj, residual[0], norm_gain)
    routing = [
        route_slots(expert_ids[0], route_gates[0], capacity[0, 0], expert)
        for expert in range(PASS_SPECIALISTS)
    ]
    chosen = pick_rows(routing, normed)
    routed_rows = lax.all_gather(jnp.swapaxes(chosen, 0, 1), "ctx", axis=0, tiled=True)
    outputs = [
        feed_forward(routed_rows[:, expert], *weights_in[expert])
        for expert in range(PASS_SPECIALISTS)
    ]
    expert_out = lax.psum_scatter(
        jnp.stack(outputs, axis=1), "ctx", scatter_dimension=0, tiled=True
    )
    expert_sum = combine_rows(routing, [expert_out[:, e] for e in range(PASS_SPECIALISTS)])
    return (attn_proj[None], expert_sum[None])


CTX, CHIP, CORE, FIRST, FIRST_CAP, SECOND, SECOND_CAP, SAME = range(8)
FIRST_HERE, SECOND_HERE, PASSES, BRANCH, PASS_INFO = range(8, 13)
USE_FAR, NEAR_LAST, NEAR_SECOND, OTHER_NEAR, PASS_COUNT = range(5)


def work_out_places(bits, numbers, info):
    owners = [numbers[k] for k in range(PASS_SPECIALISTS)]
    caps = [numbers[PASS_SPECIALISTS + k] for k in range(PASS_SPECIALISTS)]
    me = lax.axis_index("dp")
    differ = owners[0] ^ owners[1]
    branch = 0
    split_bit = 0
    rest = [bits[1], bits[2]]
    for k in reversed(range(len(bits))):
        parted = (differ & bits[k]) != 0
        branch = jnp.where(parted, k, branch)
        split_bit = jnp.where(parted, bits[k], split_bit)
        others = [bit for bit in bits if bit != bits[k]]
        rest = [jnp.where(parted, others[i], rest[i]) for i in range(2)]
    same = split_bit == 0
    swapped = ((me ^ owners[0]) & split_bit) != 0
    first_offset = me ^ jnp.where(swapped, owners[1], owners[0])
    second_offset = me ^ jnp.where(swapped, owners[0], owners[1])

    def put(place, value):
        info[place] = value.astype(jnp.int32)

    put(CTX, lax.axis_index("ctx"))
    put(CHIP, me >> 1)
    put(CORE, me & 1)
    put(FIRST, jnp.where(swapped, 1, 0))
    put(FIRST_CAP, jnp.where(swapped, caps[1], caps[0]))
    put(SECOND, jnp.where(swapped, 0, 1))
    put(SECOND_CAP, jnp.where(swapped, caps[0], caps[1]))
    put(SAME, jnp.where(same, 1, 0))
    put(FIRST_HERE, jnp.where((first_offset & bits[0]) == 0, 1, 0))
    put(SECOND_HERE, jnp.where((second_offset & bits[0]) == 0, 1, 0))
    put(PASSES, jnp.where(same, 2, 1))
    on_one = (owners[0] & jnp.where(same, bits[0], split_bit)) != 0
    seconds = [jnp.where((owners[k] & rest[0]) == 0, 0, 1) for k in range(2)]
    at_zero = jnp.where(on_one, seconds[1], seconds[0])
    at_one = jnp.where(on_one, seconds[0], seconds[1])
    at_one = jnp.where(same, at_zero, at_one)
    put(BRANCH, jnp.where(branch == 0, 2 * at_zero + at_one, 2 + 2 * branch + at_zero))
    pairs = (
        (first_offset, jnp.where(same, first_offset, second_offset)),
        (second_offset, second_offset),
    )
    for k, (offset, other_offset) in enumerate(pairs):
        base = PASS_INFO + k * PASS_COUNT
        put(base + USE_FAR, offset & 1)
        put(base + NEAR_LAST, jnp.where((offset & rest[1]) == 0, 1, 0))
        put(base + NEAR_SECOND, jnp.where((offset & rest[0]) == 0, 1, 0))
        put(base + OTHER_NEAR, jnp.where((other_offset & rest[0]) == 0, 1, 0))


def branches(bits):
    return [(bits[0], (zero, one)) for zero in range(2) for one in range(2)] + [
        (bit, (both, both)) for bit in bits[1:] for both in range(2)
    ]


def attend_kernel(bits, numbers, own_vecs, key_before, value_before, ids, gates, *outs):
    attended, select, gate_values, info = outs
    query, key, value = (own_vecs.at[k] for k in range(3))
    work_out_places(bits, numbers, info)
    token_count = query.shape[0]
    row = lax.broadcasted_iota(jnp.int32, (token_count, token_count), 0)
    col = lax.broadcasted_iota(jnp.int32, (token_count, token_count), 1)
    own_visible = col <= row
    before_visible = jnp.broadcast_to(info[CTX], (token_count, token_count)) == 1
    contract_last = (((1,), (1,)), ((), ()))
    for head in range(HEADS):
        span = slice(head * HD, (head + 1) * HD)
        heads = query[:, span]
        own = lax.dot_general(
            heads, key[:, span], contract_last, preferred_element_type=jnp.float32
        )
        before = lax.dot_general(
            heads, key_before[:, span], contract_last, preferred_element_type=jnp.float32
        )
        own = jnp.where(own_visible, own * HD ** (-0.5), -jnp.inf)
        before = jnp.where(before_visible, before * HD ** (-0.5), -jnp.inf)
        top = jnp.maximum(
            jnp.max(own, axis=1, keepdims=True), jnp.max(before, axis=1, keepdims=True)
        )
        own = jnp.exp(own - top)
        before = jnp.exp(before - top)
        total = jnp.sum(own, axis=1, keepdims=True) + jnp.sum(before, axis=1, keepdims=True)
        mixed = jnp.dot(
            own.astype(jnp.bfloat16), value[:, span], preferred_element_type=jnp.float32
        ) + jnp.dot(
            before.astype(jnp.bfloat16), value_before[:, span], preferred_element_type=jnp.float32
        )
        mixed = mixed / total
        swapped = pltpu.roll(mixed, HD // 2, 1)
        mixed = jnp.where(jnp.broadcast_to(info[CORE], mixed.shape) == 0, mixed, swapped)
        attended[head ^ info[CHIP]] = mixed.astype(jnp.bfloat16)

    slot = lax.broadcasted_iota(jnp.int32, (CAP, token_count), 0)
    earlier = (row < col).astype(jnp.bfloat16)
    for k in range(PASS_SPECIALISTS):
        matches = ids[...] == info[FIRST + 2 * k]
        named = jnp.max(matches.astype(jnp.float32), axis=0, keepdims=True)
        gate_row = jnp.sum(jnp.where(matches, gates[...], 0.0), axis=0, keepdims=True)
        gate_values[:, k : k + 1] = jnp.sum(
            jnp.where(row == col, jnp.broadcast_to(gate_row, row.shape), 0.0),
            axis=1,
            keepdims=True,
        )
        routed = jnp.broadcast_to(named, (CAP, token_count))
        rank = jnp.dot(
            routed.astype(jnp.bfloat16), earlier, preferred_element_type=jnp.float32
        ).astype(jnp.int32)
        kept = (routed > 0.0) & (rank == slot) & (rank < info[FIRST_CAP + 2 * k])
        select[k] = kept.astype(jnp.bfloat16)


def add_products(attended, chips, near, far, span, total):
    for pair in range(0, len(chips), 2):
        one, two = chips[pair], chips[pair + 1]
        left = jnp.concatenate([attended[one], attended[two]], axis=1)
        right = jnp.concatenate(
            [near[pair][:, span], far[pair][:, span]]
            + [near[pair + 1][:, span], far[pair + 1][:, span]],
            axis=0,
        )
        product = jnp.dot(left, right, preferred_element_type=jnp.float32)
        total = product if total is None else total + product
    return total


def early_kernel(chips, attended, *refs):
    near, far = refs[: len(chips)], refs[len(chips) : -1]
    total = refs[-1]
    for start in range(0, total.shape[1], 512):
        span = slice(start, start + 512)
        total[:, span] = add_products(attended, chips, near, far, span, None)


def project_kernel(chips, info, attended, residual, gain, select, early, *refs):
    near, far = refs[: len(chips)], refs[len(chips) : 2 * len(chips)]
    attn_proj, kept, sent, second, _, _, combined = refs[-7:]
    token_count, width = residual.shape
    tile = 512
    squares = jnp.zeros((token_count, 1), jnp.float32)
    for start in range(0, width, tile):
        span = slice(start, start + tile)
        total = add_products(attended, chips, near, far, span, early[:, span])
        rounded = total.astype(jnp.bfloat16)
        attn_proj[:, span] = rounded
        added = residual[:, span].astype(jnp.float32) + rounded.astype(jnp.float32)
        combined[:, span] = added
        squares = squares + jnp.sum(added * added, axis=1, keepdims=True)
    scale = lax.rsqrt(squares / width + EPSILON)
    for start in range(0, width, tile):
        span = slice(start, start + tile)
        normed = (combined[:, span] * scale * gain[:, span]).astype(jnp.bfloat16)
        rows = [
            jnp.dot(select[k], normed, preferred_element_type=jnp.float32)
            for k in range(PASS_SPECIALISTS)
        ]
        kept[:, span] = rows[0].astype(jnp.bfloat16)
        second[:, span] = rows[1].astype(jnp.bfloat16)
        use_first = jnp.broadcast_to(info[SAME], rows[0].shape) != 0
        sent[:, span] = jnp.where(use_first, rows[0], rows[1]).astype(jnp.bfloat16)


def combine_kernel(info, step, own, other, last, second, select, gate_values, *outs):
    out, next_last, next_kept, next_sent = outs
    same = info[SAME] != 0
    contract_first = (((0,), (0,)), ((), ()))

    def add_up(first_rows, second_rows):
        total = 0.0
        for k, rows in enumerate((first_rows, second_rows)):
            picked = lax.dot_general(
                select[k], rows, contract_first, preferred_element_type=jnp.float32
            )
            total = total + gate_values[:, k : k + 1] * picked
        return total.astype(jnp.bfloat16)

    @pl.when(jnp.logical_not(same))
    def _():
        for start in range(0, own.shape[1], 512):
            span = slice(start, start + 512)
            out[:, span] = add_up(own[:, span], other[:, span])

    @pl.when(same)
    def _():
        here = jnp.where(step[0] == 0, info[FIRST_HERE], info[SECOND_HERE])
        for start in range(0, own.shape[1], 512):
            span = slice(start, start + 512)
            use_own = jnp.broadcast_to(here, (own.shape[0], 512)) != 0
            served = jnp.where(
                use_own, own[:, span].astype(jnp.float32), other[:, span].astype(jnp.float32)
            ).astype(jnp.bfloat16)
            out[:, span] = add_up(last[:, span], served)
            next_last[:, span] = served
            next_kept[:, span] = second[:, span]
            next_sent[:, span] = second[:, span]


def expert_kernel(
    info,
    step,
    rows,
    gate_up_near,
    gate_up_far,
    down_near,
    down_far,
    made,
    masks,
    gate_up,
    down,
    sums,
    hidden,
    sems,
):
    units, width = down.shape
    piece = 512
    starts = list(range(0, width, piece))

    def copies(gate_up_from, down_from):
        spans = [pl.ds(start, piece) for start in starts]
        out = [
            pltpu.make_async_copy(gate_up_from.at[:, :, span], gate_up.at[:, :, span], sems.at[k])
            for k, span in enumerate(spans)
        ]
        return out + [pltpu.make_async_copy(down_from, down, sems.at[len(starts)])]

    base = PASS_INFO + PASS_COUNT * step[0]
    use_far = info[base + USE_FAR]

    def start_copy(stage):
        @pl.when(use_far == 0)
        def _():
            copies(gate_up_near, down_near)[stage].start()

        @pl.when(use_far != 0)
        def _():
            copies(gate_up_far, down_far)[stage].start()

    start_copy(0)
    start_copy(1)
    for k in (NEAR_LAST, NEAR_SECOND, OTHER_NEAR):
        masks[k] = jnp.broadcast_to(info[base + k].astype(jnp.float32), masks.shape[1:])

    arrived = copies(gate_up_near, down_near)
    contract_last = (((1,), (1,)), ((), ()))
    for k, start in enumerate(starts):
        span = slice(start, start + piece)
        arrived[k].wait()
        if k + 2 < len(arrived):
            start_copy(k + 2)
        product = lax.dot_general(
            gate_up[:, :, span].reshape(2 * units, piece),
            rows[:, span],
            contract_last,
            preferred_element_type=jnp.float32,
        )
        if k == 0:
            sums[...] = product
        else:
            sums[...] += product
    for start in range(0, units, 256):
        stop = min(start + 256, units)
        gate_proj, up_proj = sums[start:stop], sums[units + start : units + stop]
        made_hidden = gate_proj / (1.0 + jnp.exp(-gate_proj)) * up_proj
        hidden[:, start:stop] = jnp.transpose(made_hidden).astype(jnp.bfloat16)
    arrived[-1].wait()
    for start in range(0, width, 512):
        span = slice(start, start + 512)
        made[:, span] = jnp.dot(
            hidden[...], down[:, span], preferred_element_type=jnp.float32
        ).astype(jnp.bfloat16)


def gather_rows(kept, sent, first, places, bits, dp_size):
    second, last = bits

    def to_owner(_, target):
        return ((target & second) != 0) == places[(target & first) != 0]

    beside = hop(kept, "dp", dp_size, second, to_owner)
    across = hop(sent, "dp", dp_size, first, to_owner)
    beyond = hop(sent, "dp", dp_size, first | second, to_owner)
    unit = jnp.concatenate([kept, beside, across, beyond], axis=0)
    half = unit.shape[1] // 2
    left, right = unit[:, :half], unit[:, half:]
    left = jnp.stack([left, hop(left, "dp", dp_size, last)])
    right = jnp.stack([right, hop(right, "ctx", 2, 1)])
    left = jnp.stack([left, hop(left, "ctx", 2, 1)])
    right = jnp.stack([right, hop(right, "dp", dp_size, last)], axis=1)
    rows = jnp.concatenate([left, right], axis=-1)
    return rows.reshape(-1, rows.shape[-1])


def scatter_rows(rows, first, places, bits, dp_size, masks):
    second, last = bits
    half = rows.shape[1] // 2
    rows = rows.reshape(2, 2, -1, rows.shape[1])
    left, right = rows[..., :half], rows[..., half:]

    def add(kept, came):
        return (kept.astype(jnp.float32) + came.astype(jnp.float32)).astype(jnp.bfloat16)

    left = add(left[0], hop(left[1], "ctx", 2, 1))
    right = jnp.where(masks[NEAR_LAST, :, half:] != 0, right[:, 0], hop(right[:, 1], "dp", dp_size, last))
    left = jnp.where(masks[NEAR_LAST, :, :half] != 0, left[0], hop(left[1], "dp", dp_size, last))
    right = add(right[0], hop(right[1], "ctx", 2, 1))
    unit = jnp.concatenate([left, right], axis=-1)
    here, beside, across, beyond = lax.optimization_barrier(jnp.split(unit, 4, axis=0))

    def from_owner(source, _):
        return ((source & second) != 0) == places[(source & first) != 0]

    across = hop(across, "dp", dp_size, first, from_owner)
    beside = hop(beside, "dp", dp_size, second, from_owner)
    beyond = hop(beyond, "dp", dp_size, first | second, from_owner)
    return (
        jnp.where(masks[NEAR_SECOND] != 0, here, beside),
        jnp.where(masks[OTHER_NEAR] != 0, across, beyond),
    )


def smem(count):
    return [pl.BlockSpec(memory_space=pltpu.SMEM)] * count


def vmem(count):
    return [pl.BlockSpec(memory_space=pltpu.VMEM)] * count


def body_move_rows(
    query_vecs,
    key_vecs,
    value_vecs,
    residual,
    w_out,
    norm_gain,
    w_gate_up,
    w_down,
    expert_ids,
    route_gates,
    capacity,
    expert_owner,
):
    token_count = query_vecs.shape[1]
    width = residual.shape[2]
    dp_size = lax.axis_size("dp")
    bits = [1 << k for k in reversed(range(1, dp_size.bit_length() - 1))]

    z_far, z_near, x_bit = bits
    z_both = z_far | z_near
    near = {0: w_out}
    for bit in (z_far, z_near, x_bit):
        near[bit] = hop(w_out, "dp", dp_size, bit)
    key_before = lax.ppermute(key_vecs[0], "ctx", [(0, 1)])
    value_before = lax.ppermute(value_vecs[0], "ctx", [(0, 1)])
    own = jnp.stack([query_vecs[0], key_vecs[0], value_vecs[0]])
    numbers = jnp.concatenate([expert_owner[:PASS_SPECIALISTS], capacity[0, 0]])
    (
        near[z_far],
        near[z_near],
        near[x_bit],
        near[0],
        key_before,
        own,
        numbers,
        ids,
        gates,
    ) = lax.optimization_barrier(
        (
            near[z_far],
            near[z_near],
            near[x_bit],
            near[0],
            key_before,
            own,
            numbers,
            jnp.transpose(expert_ids[0]),
            jnp.transpose(route_gates[0]),
        )
    )
    near[z_near | x_bit] = hop(near[z_near], "dp", dp_size, x_bit)
    near[z_both] = hop(near[z_far], "dp", dp_size, z_near)
    near[z_far | x_bit] = hop(near[z_far], "dp", dp_size, x_bit)
    value_before, near[z_both] = lax.optimization_barrier((value_before, near[z_both]))
    attended, select, gate_values, info = pl.pallas_call(
        functools.partial(attend_kernel, bits),
        out_shape=(
            jax.ShapeDtypeStruct((HEADS, token_count, HD), jnp.bfloat16),
            jax.ShapeDtypeStruct((PASS_SPECIALISTS, CAP, token_count), jnp.bfloat16),
            jax.ShapeDtypeStruct((token_count, PASS_SPECIALISTS), jnp.float32),
            jax.ShapeDtypeStruct((PASS_INFO + 2 * PASS_COUNT,), jnp.int32),
        ),
        in_specs=smem(1) + vmem(5),
        out_specs=tuple(vmem(3) + smem(1)),
        cost_estimate=pl.CostEstimate(
            flops=64 * HEADS * HD * 2 * token_count * token_count,
            bytes_accessed=6 * 2 * token_count * HEADS * HD,
            transcendentals=2 * HEADS * token_count * token_count,
        ),
        compiler_params=pltpu.CompilerParams(vmem_limit_bytes=8 * 2**20),
    )(numbers, own, key_before, value_before, ids, gates)
    near[z_both | x_bit] = hop(near[z_both], "dp", dp_size, x_bit)
    (
        near[z_near | x_bit],
        near[z_far | x_bit],
        between,
        attended,
    ) = lax.optimization_barrier(
        (near[z_near | x_bit], near[z_far | x_bit], near[z_both], attended)
    )
    far = {}
    for bit in (0, z_far, z_near, x_bit, z_near | x_bit, z_far | x_bit, z_both | x_bit):
        far[bit] = hop(near[bit], "dp", dp_size, 1)
    far[z_both] = hop(between, "dp", dp_size, 1)
    late_bits = (z_far | x_bit, z_both | x_bit)
    early_bits = tuple(bit for bit in near if bit not in late_bits)
    early_chips = [bit >> 1 for bit in early_bits]
    late_chips = [bit >> 1 for bit in late_bits]
    early = pl.pallas_call(
        functools.partial(early_kernel, early_chips),
        out_shape=jax.ShapeDtypeStruct((token_count, width), jnp.float32),
        in_specs=vmem(1 + 2 * len(early_bits)),
        out_specs=vmem(1)[0],
        cost_estimate=pl.CostEstimate(
            flops=4 * 2 * token_count * HEADS * HD * width,
            bytes_accessed=2 * HEADS * HD * width,
            transcendentals=0,
        ),
        compiler_params=pltpu.CompilerParams(vmem_limit_bytes=16 * 2**20),
    )(attended, *[near[bit] for bit in early_bits], *[far[bit] for bit in early_bits])
    gate_up_near = jnp.swapaxes(w_gate_up[0], 1, 2)

    some_rows = jax.ShapeDtypeStruct((CAP, width), jnp.bfloat16)
    all_rows = jax.ShapeDtypeStruct((token_count, width), jnp.bfloat16)
    attn_proj, kept, sent, second, last, expert_sum = pl.pallas_call(
        functools.partial(project_kernel, late_chips),
        out_shape=(all_rows, some_rows, some_rows, some_rows, some_rows, all_rows),
        in_specs=smem(1) + vmem(5 + 2 * len(late_bits)),
        out_specs=tuple(vmem(4) + [pl.BlockSpec(memory_space=pl.ANY)] * 2),
        scratch_shapes=[pltpu.VMEM((token_count, width), jnp.float32)],
        cost_estimate=pl.CostEstimate(
            flops=2 * token_count * HEADS * HD * width,
            bytes_accessed=2 * HEADS * HD * width,
            transcendentals=0,
        ),
        compiler_params=pltpu.CompilerParams(vmem_limit_bytes=16 * 2**20),
    )(
        info,
        attended,
        residual[0],
        norm_gain[None],
        select,
        early,
        *[near[bit] for bit in late_bits],
        *[far[bit] for bit in late_bits],
    )

    units = w_down.shape[1]
    row_count = dp_size * CAP

    def dispatch(bit, places):
        rest = [b for b in bits if b != bit]

        def run(kept, sent):
            gate_up_far = hop(gate_up_near, "dp", dp_size, 1)
            down_far = hop(w_down[0], "dp", dp_size, 1)
            rows = gather_rows(kept, sent, bit, places, rest, dp_size)
            return rows, gate_up_far, down_far

        return run

    def give_back(bit, places):
        rest = [b for b in bits if b != bit]

        def run(made, masks):
            return scatter_rows(made, bit, places, rest, dp_size, masks)

        return run

    branch = info[BRANCH]

    def one_pass(step, carried):
        kept, sent, last, _ = carried
        rows, gate_up_far, down_far = lax.switch(
            branch, [dispatch(*way) for way in branches(bits)], kept, sent
        )
        made, masks = pl.pallas_call(
            expert_kernel,
            out_shape=(
                jax.ShapeDtypeStruct((row_count, width), jnp.bfloat16),
                jax.ShapeDtypeStruct((PASS_COUNT, 1, width), jnp.float32),
            ),
            in_specs=smem(2) + vmem(1) + [pl.BlockSpec(memory_space=pltpu.HBM)] * 4,
            out_specs=tuple(vmem(2)),
            scratch_shapes=[
                pltpu.VMEM((2, units, width), jnp.bfloat16),
                pltpu.VMEM((units, width), jnp.bfloat16),
                pltpu.VMEM((2 * units, row_count), jnp.float32),
                pltpu.VMEM((row_count, units), jnp.bfloat16),
                pltpu.SemaphoreType.DMA((width // 512 + 1,)),
            ],
            cost_estimate=pl.CostEstimate(
                flops=6 * row_count * units * width,
                bytes_accessed=6 * units * width,
                transcendentals=row_count * units,
            ),
            compiler_params=pltpu.CompilerParams(vmem_limit_bytes=26 * 2**20),
        )(info, step[None], rows, gate_up_near, gate_up_far, w_down[0], down_far)
        own, other = lax.switch(branch, [give_back(*way) for way in branches(bits)], made, masks)
        expert_sum, last, kept, sent = pl.pallas_call(
            combine_kernel,
            out_shape=(all_rows, some_rows, some_rows, some_rows),
            in_specs=smem(2) + vmem(6),
            out_specs=tuple(vmem(4)),
            compiler_params=pltpu.CompilerParams(vmem_limit_bytes=8 * 2**20),
        )(info, step[None], own, other, last, second, select, gate_values)
        return kept, sent, last, expert_sum

    carried = (kept, sent, last, expert_sum)
    expert_sum = lax.fori_loop(0, info[PASSES], one_pass, carried)[3]
    return (attn_proj[None], expert_sum[None])


def solution(mesh):
    placed = (
        P("dp", "ctx", None),
        P("dp", "ctx", None),
        P("dp", "ctx", None),
        P("dp", "ctx", None),
        P("dp", None),
        P(),
        P("dp", None, None, "ctx"),
        P("dp", "ctx", None),
        P("dp", "ctx", None),
        P("dp", "ctx", None),
        P("dp", "ctx", None),
        P(),
    )
    dp_size, ctx_size = mesh.shape["dp"], mesh.shape["ctx"]
    small = ctx_size == 2 and dp_size == 2 * HEADS
    return jax.shard_map(
        body_move_rows if small else body_move_weights,
        mesh=mesh,
        in_specs=placed,
        out_specs=(P("dp", "ctx", None), P("dp", "ctx", None)),
        check_vma=False,
    )
```

```python
import functools

import jax
import jax.numpy as jnp
from jax import lax
from jax.experimental import pallas as pl
from jax.experimental.pallas import tpu as pltpu
from jax.sharding import PartitionSpec as P

HEADS = 8
HD = 128
PASS_SPECIALISTS = 2
CAP = 24


EPSILON = 1e-06
LOWEST = -1e30


def broadcast(array, axis, root):
    mine = lax.axis_index(axis) == root
    return lax.psum(jnp.where(mine, array, jnp.zeros_like(array)), axis)


def hop(array, axis, size, bit):
    return lax.ppermute(array, axis, [(i, i ^ bit) for i in range(size)])


def route_slots(expert_ids, route_gates, capacity, expert):
    matches = expert_ids == expert
    routed = jnp.any(matches, axis=1)
    gate_value = jnp.sum(jnp.where(matches, route_gates, 0.0), axis=1)
    slot_rank = jnp.cumsum(routed.astype(jnp.int32)) - 1
    kept_mask = routed & (slot_rank < capacity[expert])
    return (slot_rank, kept_mask, gate_value)


def attend(queries, key_block, value_block, visible):
    width = key_block.shape[0]
    token_count = queries.shape[0]
    query_heads = queries.reshape(token_count, HEADS, HD)
    key_heads = key_block.reshape(width, HEADS, HD)
    value_heads = value_block.reshape(width, HEADS, HD)
    gating_logits = jnp.einsum(
        "qhd,khd->qhk", query_heads, key_heads, preferred_element_type=jnp.float32
    ) * HD ** (-0.5)
    gating_logits = jnp.where(visible[:, None, :], gating_logits, -jnp.inf)
    row_top = jnp.max(gating_logits, axis=-1)
    weights = jnp.exp(gating_logits - row_top[:, :, None])
    denominator = jnp.sum(weights, axis=-1)
    weighted = jnp.einsum(
        "qhk,khd->qhd",
        weights.astype(jnp.bfloat16),
        value_heads,
        preferred_element_type=jnp.float32,
    )
    attended = (weighted / denominator[:, :, None]).astype(jnp.bfloat16)
    return attended.reshape(token_count, HEADS * HD)


def feed_forward(rows, gate_up, down_part):
    gate_proj = jnp.dot(rows, gate_up[0], preferred_element_type=jnp.float32)
    up_proj = jnp.dot(rows, gate_up[1], preferred_element_type=jnp.float32)
    hidden = (jax.nn.silu(gate_proj) * up_proj).astype(jnp.bfloat16)
    return jnp.dot(hidden, down_part, preferred_element_type=jnp.float32).astype(jnp.bfloat16)


def normalise(attn_proj, residual, norm_gain):
    combined = residual.astype(jnp.float32) + attn_proj.astype(jnp.float32)
    return (
        combined
        * lax.rsqrt(jnp.mean(combined * combined, axis=-1, keepdims=True) + EPSILON)
        * norm_gain
    ).astype(jnp.bfloat16)


def pick_rows(routing, normed):
    slot_ids = jnp.arange(CAP)
    select = [
        (slot_rank[None, :] == slot_ids[:, None]) & kept_mask[None, :]
        for slot_rank, kept_mask, _ in routing
    ]
    select = jnp.concatenate(select, axis=0).astype(jnp.bfloat16)
    chosen = jnp.dot(select, normed, preferred_element_type=jnp.float32).astype(jnp.bfloat16)
    return chosen.reshape(PASS_SPECIALISTS, CAP, normed.shape[1])


def combine_rows(routing, produced):
    slot_ids = jnp.arange(CAP)
    summed = 0.0
    for expert in range(PASS_SPECIALISTS):
        slot_rank, kept_mask, gate_value = routing[expert]
        place = ((slot_rank[:, None] == slot_ids[None, :]) & kept_mask[:, None]).astype(
            jnp.bfloat16
        )
        picked = jnp.dot(place, produced[expert], preferred_element_type=jnp.float32)
        summed = summed + gate_value[:, None] * picked
    return summed.astype(jnp.bfloat16)


def body_move_weights(
    query_vecs,
    key_vecs,
    value_vecs,
    residual,
    w_out,
    norm_gain,
    w_gate_up,
    w_down,
    expert_ids,
    route_gates,
    capacity,
    expert_owner,
):
    token_count = query_vecs.shape[1]
    weights_in = []
    for expert in range(PASS_SPECIALISTS):
        weights_in.append(
            (
                broadcast(w_gate_up[0], "dp", expert_owner[expert]),
                broadcast(w_down[0], "dp", expert_owner[expert]),
            )
        )
    keys = lax.all_gather(key_vecs[0], "ctx", axis=0, tiled=True)
    values = lax.all_gather(value_vecs[0], "ctx", axis=0, tiled=True)
    first_row = lax.axis_index("ctx") * token_count
    query_pos = first_row + jnp.arange(token_count)
    visible = jnp.arange(keys.shape[0])[None, :] <= query_pos[:, None]
    attended = attend(query_vecs[0], keys, values, visible)
    projected = jnp.dot(
        attended,
        lax.all_gather(w_out, "dp", axis=0, tiled=True),
        preferred_element_type=jnp.float32,
    )
    attn_proj = projected.astype(jnp.bfloat16)
    normed = normalise(attn_proj, residual[0], norm_gain)
    routing = [
        route_slots(expert_ids[0], route_gates[0], capacity[0, 0], expert)
        for expert in range(PASS_SPECIALISTS)
    ]
    chosen = pick_rows(routing, normed)
    routed_rows = lax.all_gather(jnp.swapaxes(chosen, 0, 1), "ctx", axis=0, tiled=True)
    outputs = [
        feed_forward(routed_rows[:, expert], *weights_in[expert])
        for expert in range(PASS_SPECIALISTS)
    ]
    expert_out = lax.psum_scatter(
        jnp.stack(outputs, axis=1), "ctx", scatter_dimension=0, tiled=True
    )
    expert_sum = combine_rows(routing, [expert_out[:, e] for e in range(PASS_SPECIALISTS)])
    return (attn_proj[None], expert_sum[None])


CTX, CHIP, CORE, FIRST, FIRST_CAP, SECOND, SECOND_CAP, SAME = range(8)
FIRST_HERE, SECOND_HERE, PASSES, BRANCH, PASS_INFO = range(8, 13)
USE_FAR, NEAR_LAST, NEAR_SECOND, OTHER_NEAR, PASS_COUNT = range(5)


def work_out_places(bits, numbers, info):
    owners = [numbers[k] for k in range(PASS_SPECIALISTS)]
    caps = [numbers[PASS_SPECIALISTS + k] for k in range(PASS_SPECIALISTS)]
    me = lax.axis_index("dp")
    differ = owners[0] ^ owners[1]
    branch = 0
    split_bit = 0
    rest = [bits[1], bits[2]]
    for k in reversed(range(len(bits))):
        parted = (differ & bits[k]) != 0
        branch = jnp.where(parted, k, branch)
        split_bit = jnp.where(parted, bits[k], split_bit)
        others = [bit for bit in bits if bit != bits[k]]
        rest = [jnp.where(parted, others[i], rest[i]) for i in range(2)]
    same = split_bit == 0
    swapped = ((me ^ owners[0]) & split_bit) != 0
    first_offset = me ^ jnp.where(swapped, owners[1], owners[0])
    second_offset = me ^ jnp.where(swapped, owners[0], owners[1])

    def put(place, value):
        info[place] = value.astype(jnp.int32)

    put(CTX, lax.axis_index("ctx"))
    put(CHIP, me >> 1)
    put(CORE, me & 1)
    put(FIRST, jnp.where(swapped, 1, 0))
    put(FIRST_CAP, jnp.where(swapped, caps[1], caps[0]))
    put(SECOND, jnp.where(swapped, 0, 1))
    put(SECOND_CAP, jnp.where(swapped, caps[0], caps[1]))
    put(SAME, jnp.where(same, 1, 0))
    put(FIRST_HERE, jnp.where((first_offset & bits[0]) == 0, 1, 0))
    put(SECOND_HERE, jnp.where((second_offset & bits[0]) == 0, 1, 0))
    put(PASSES, jnp.where(same, 2, 1))
    put(BRANCH, branch)
    pairs = (
        (first_offset, jnp.where(same, first_offset, second_offset)),
        (second_offset, second_offset),
    )
    for k, (offset, other_offset) in enumerate(pairs):
        base = PASS_INFO + k * PASS_COUNT
        put(base + USE_FAR, offset & 1)
        put(base + NEAR_LAST, jnp.where((offset & rest[1]) == 0, 1, 0))
        put(base + NEAR_SECOND, jnp.where((offset & rest[0]) == 0, 1, 0))
        put(base + OTHER_NEAR, jnp.where((other_offset & rest[0]) == 0, 1, 0))


def attend_kernel(bits, numbers, own_vecs, key_before, value_before, ids, gates, *outs):
    attended, select, gate_values, info = outs
    query, key, value = (own_vecs.at[k] for k in range(3))
    work_out_places(bits, numbers, info)
    token_count = query.shape[0]
    row = lax.broadcasted_iota(jnp.int32, (token_count, token_count), 0)
    col = lax.broadcasted_iota(jnp.int32, (token_count, token_count), 1)
    own_visible = col <= row
    before_visible = jnp.broadcast_to(info[CTX], (token_count, token_count)) == 1
    contract_last = (((1,), (1,)), ((), ()))
    for head in range(HEADS):
        span = slice(head * HD, (head + 1) * HD)
        heads = query[:, span]
        own = lax.dot_general(
            heads, key[:, span], contract_last, preferred_element_type=jnp.float32
        )
        before = lax.dot_general(
            heads, key_before[:, span], contract_last, preferred_element_type=jnp.float32
        )
        own = jnp.where(own_visible, own * HD ** (-0.5), -jnp.inf)
        before = jnp.where(before_visible, before * HD ** (-0.5), -jnp.inf)
        top = jnp.maximum(
            jnp.max(own, axis=1, keepdims=True), jnp.max(before, axis=1, keepdims=True)
        )
        own = jnp.exp(own - top)
        before = jnp.exp(before - top)
        total = jnp.sum(own, axis=1, keepdims=True) + jnp.sum(before, axis=1, keepdims=True)
        mixed = jnp.dot(
            own.astype(jnp.bfloat16), value[:, span], preferred_element_type=jnp.float32
        ) + jnp.dot(
            before.astype(jnp.bfloat16), value_before[:, span], preferred_element_type=jnp.float32
        )
        mixed = mixed / total
        swapped = pltpu.roll(mixed, HD // 2, 1)
        mixed = jnp.where(jnp.broadcast_to(info[CORE], mixed.shape) == 0, mixed, swapped)
        attended[head ^ info[CHIP]] = mixed.astype(jnp.bfloat16)

    slot = lax.broadcasted_iota(jnp.int32, (CAP, token_count), 0)
    earlier = (row < col).astype(jnp.bfloat16)
    for k in range(PASS_SPECIALISTS):
        matches = ids[...] == info[FIRST + 2 * k]
        named = jnp.max(matches.astype(jnp.float32), axis=0, keepdims=True)
        gate_row = jnp.sum(jnp.where(matches, gates[...], 0.0), axis=0, keepdims=True)
        gate_values[:, k : k + 1] = jnp.sum(
            jnp.where(row == col, jnp.broadcast_to(gate_row, row.shape), 0.0),
            axis=1,
            keepdims=True,
        )
        routed = jnp.broadcast_to(named, (CAP, token_count))
        rank = jnp.dot(
            routed.astype(jnp.bfloat16), earlier, preferred_element_type=jnp.float32
        ).astype(jnp.int32)
        kept = (routed > 0.0) & (rank == slot) & (rank < info[FIRST_CAP + 2 * k])
        select[k] = kept.astype(jnp.bfloat16)


def add_products(attended, chips, near, far, span, total):
    for pair in range(0, len(chips), 2):
        one, two = chips[pair], chips[pair + 1]
        left = jnp.concatenate([attended[one], attended[two]], axis=1)
        right = jnp.concatenate(
            [near[pair][:, span], far[pair][:, span]]
            + [near[pair + 1][:, span], far[pair + 1][:, span]],
            axis=0,
        )
        product = jnp.dot(left, right, preferred_element_type=jnp.float32)
        total = product if total is None else total + product
    return total


def early_kernel(chips, attended, *refs):
    near, far = refs[: len(chips)], refs[len(chips) : -1]
    total = refs[-1]
    for start in range(0, total.shape[1], 512):
        span = slice(start, start + 512)
        total[:, span] = add_products(attended, chips, near, far, span, None)


def project_kernel(chips, info, attended, residual, gain, select, early, *refs):
    near, far = refs[: len(chips)], refs[len(chips) : 2 * len(chips)]
    attn_proj, kept, sent, second, _, _, combined = refs[-7:]
    token_count, width = residual.shape
    tile = 512
    squares = jnp.zeros((token_count, 1), jnp.float32)
    for start in range(0, width, tile):
        span = slice(start, start + tile)
        total = add_products(attended, chips, near, far, span, early[:, span])
        rounded = total.astype(jnp.bfloat16)
        attn_proj[:, span] = rounded
        added = residual[:, span].astype(jnp.float32) + rounded.astype(jnp.float32)
        combined[:, span] = added
        squares = squares + jnp.sum(added * added, axis=1, keepdims=True)
    scale = lax.rsqrt(squares / width + EPSILON)
    for start in range(0, width, tile):
        span = slice(start, start + tile)
        normed = (combined[:, span] * scale * gain[:, span]).astype(jnp.bfloat16)
        rows = [
            jnp.dot(select[k], normed, preferred_element_type=jnp.float32)
            for k in range(PASS_SPECIALISTS)
        ]
        kept[:, span] = rows[0].astype(jnp.bfloat16)
        second[:, span] = rows[1].astype(jnp.bfloat16)
        use_first = jnp.broadcast_to(info[SAME], rows[0].shape) != 0
        sent[:, span] = jnp.where(use_first, rows[0], rows[1]).astype(jnp.bfloat16)


def combine_kernel(info, step, own, other, last, second, select, gate_values, *outs):
    out, next_last, next_kept, next_sent = outs
    same = info[SAME] != 0
    contract_first = (((0,), (0,)), ((), ()))

    def add_up(first_rows, second_rows):
        total = 0.0
        for k, rows in enumerate((first_rows, second_rows)):
            picked = lax.dot_general(
                select[k], rows, contract_first, preferred_element_type=jnp.float32
            )
            total = total + gate_values[:, k : k + 1] * picked
        return total.astype(jnp.bfloat16)

    @pl.when(jnp.logical_not(same))
    def _():
        for start in range(0, own.shape[1], 512):
            span = slice(start, start + 512)
            out[:, span] = add_up(own[:, span], other[:, span])

    @pl.when(same)
    def _():
        here = jnp.where(step[0] == 0, info[FIRST_HERE], info[SECOND_HERE])
        for start in range(0, own.shape[1], 512):
            span = slice(start, start + 512)
            use_own = jnp.broadcast_to(here, (own.shape[0], 512)) != 0
            served = jnp.where(
                use_own, own[:, span].astype(jnp.float32), other[:, span].astype(jnp.float32)
            ).astype(jnp.bfloat16)
            out[:, span] = add_up(last[:, span], served)
            next_last[:, span] = served
            next_kept[:, span] = second[:, span]
            next_sent[:, span] = second[:, span]


def expert_kernel(
    info,
    step,
    rows,
    gate_up_near,
    gate_up_far,
    down_near,
    down_far,
    made,
    masks,
    gate_up,
    down,
    sums,
    hidden,
    sems,
):
    units, width = down.shape
    piece = 512
    starts = list(range(0, width, piece))

    def copies(gate_up_from, down_from):
        spans = [pl.ds(start, piece) for start in starts]
        out = [
            pltpu.make_async_copy(gate_up_from.at[:, :, span], gate_up.at[:, :, span], sems.at[k])
            for k, span in enumerate(spans)
        ]
        return out + [pltpu.make_async_copy(down_from, down, sems.at[len(starts)])]

    base = PASS_INFO + PASS_COUNT * step[0]
    use_far = info[base + USE_FAR]

    def start_copy(stage):
        @pl.when(use_far == 0)
        def _():
            copies(gate_up_near, down_near)[stage].start()

        @pl.when(use_far != 0)
        def _():
            copies(gate_up_far, down_far)[stage].start()

    start_copy(0)
    start_copy(1)
    for k in (NEAR_LAST, NEAR_SECOND, OTHER_NEAR):
        masks[k] = jnp.broadcast_to(info[base + k].astype(jnp.float32), masks.shape[1:])

    arrived = copies(gate_up_near, down_near)
    contract_last = (((1,), (1,)), ((), ()))
    for k, start in enumerate(starts):
        span = slice(start, start + piece)
        arrived[k].wait()
        if k + 2 < len(arrived):
            start_copy(k + 2)
        product = lax.dot_general(
            gate_up[:, :, span].reshape(2 * units, piece),
            rows[:, span],
            contract_last,
            preferred_element_type=jnp.float32,
        )
        if k == 0:
            sums[...] = product
        else:
            sums[...] += product
    for start in range(0, units, 256):
        stop = min(start + 256, units)
        gate_proj, up_proj = sums[start:stop], sums[units + start : units + stop]
        made_hidden = gate_proj / (1.0 + jnp.exp(-gate_proj)) * up_proj
        hidden[:, start:stop] = jnp.transpose(made_hidden).astype(jnp.bfloat16)
    arrived[-1].wait()
    for start in range(0, width, 512):
        span = slice(start, start + 512)
        made[:, span] = jnp.dot(
            hidden[...], down[:, span], preferred_element_type=jnp.float32
        ).astype(jnp.bfloat16)


def gather_rows(kept, sent, first, bits, dp_size):
    second, last = bits

    beside = hop(kept, "dp", dp_size, second)
    across = hop(sent, "dp", dp_size, first)
    beyond = hop(sent, "dp", dp_size, first | second)
    unit = jnp.concatenate([kept, beside, across, beyond], axis=0)
    half = unit.shape[1] // 2
    left, right = unit[:, :half], unit[:, half:]
    left = jnp.stack([left, hop(left, "dp", dp_size, last)])
    right = jnp.stack([right, hop(right, "ctx", 2, 1)])
    left = jnp.stack([left, hop(left, "ctx", 2, 1)])
    right = jnp.stack([right, hop(right, "dp", dp_size, last)], axis=1)
    rows = jnp.concatenate([left, right], axis=-1)
    return rows.reshape(-1, rows.shape[-1])


def scatter_rows(rows, first, bits, dp_size, masks):
    second, last = bits
    half = rows.shape[1] // 2
    rows = rows.reshape(2, 2, -1, rows.shape[1])
    left, right = rows[..., :half], rows[..., half:]

    def add(kept, came):
        return (kept.astype(jnp.float32) + came.astype(jnp.float32)).astype(jnp.bfloat16)

    left = add(left[0], hop(left[1], "ctx", 2, 1))
    right = jnp.where(masks[NEAR_LAST, :, half:] != 0, right[:, 0], hop(right[:, 1], "dp", dp_size, last))
    left = jnp.where(masks[NEAR_LAST, :, :half] != 0, left[0], hop(left[1], "dp", dp_size, last))
    right = add(right[0], hop(right[1], "ctx", 2, 1))
    unit = jnp.concatenate([left, right], axis=-1)
    here, beside, across, beyond = lax.optimization_barrier(jnp.split(unit, 4, axis=0))

    across = hop(across, "dp", dp_size, first)
    beside = hop(beside, "dp", dp_size, second)
    beyond = hop(beyond, "dp", dp_size, first | second)
    return (
        jnp.where(masks[NEAR_SECOND] != 0, here, beside),
        jnp.where(masks[OTHER_NEAR] != 0, across, beyond),
    )


def smem(count):
    return [pl.BlockSpec(memory_space=pltpu.SMEM)] * count


def vmem(count):
    return [pl.BlockSpec(memory_space=pltpu.VMEM)] * count


def body_move_rows(
    query_vecs,
    key_vecs,
    value_vecs,
    residual,
    w_out,
    norm_gain,
    w_gate_up,
    w_down,
    expert_ids,
    route_gates,
    capacity,
    expert_owner,
):
    token_count = query_vecs.shape[1]
    width = residual.shape[2]
    dp_size = lax.axis_size("dp")
    bits = [1 << k for k in reversed(range(1, dp_size.bit_length() - 1))]

    z_far, z_near, x_bit = bits
    z_both = z_far | z_near
    near = {0: w_out}
    for bit in (z_far, z_near, x_bit):
        near[bit] = hop(w_out, "dp", dp_size, bit)
    key_before = lax.ppermute(key_vecs[0], "ctx", [(0, 1)])
    value_before = lax.ppermute(value_vecs[0], "ctx", [(0, 1)])
    own = jnp.stack([query_vecs[0], key_vecs[0], value_vecs[0]])
    numbers = jnp.concatenate([expert_owner[:PASS_SPECIALISTS], capacity[0, 0]])
    (
        near[z_far],
        near[z_near],
        near[x_bit],
        near[0],
        key_before,
        own,
        numbers,
        ids,
        gates,
    ) = lax.optimization_barrier(
        (
            near[z_far],
            near[z_near],
            near[x_bit],
            near[0],
            key_before,
            own,
            numbers,
            jnp.transpose(expert_ids[0]),
            jnp.transpose(route_gates[0]),
        )
    )
    near[z_near | x_bit] = hop(near[z_near], "dp", dp_size, x_bit)
    near[z_both] = hop(near[z_far], "dp", dp_size, z_near)
    near[z_far | x_bit] = hop(near[z_far], "dp", dp_size, x_bit)
    value_before, near[z_both] = lax.optimization_barrier((value_before, near[z_both]))
    attended, select, gate_values, info = pl.pallas_call(
        functools.partial(attend_kernel, bits),
        out_shape=(
            jax.ShapeDtypeStruct((HEADS, token_count, HD), jnp.bfloat16),
            jax.ShapeDtypeStruct((PASS_SPECIALISTS, CAP, token_count), jnp.bfloat16),
            jax.ShapeDtypeStruct((token_count, PASS_SPECIALISTS), jnp.float32),
            jax.ShapeDtypeStruct((PASS_INFO + 2 * PASS_COUNT,), jnp.int32),
        ),
        in_specs=smem(1) + vmem(5),
        out_specs=tuple(vmem(3) + smem(1)),
        cost_estimate=pl.CostEstimate(
            flops=64 * HEADS * HD * 2 * token_count * token_count,
            bytes_accessed=6 * 2 * token_count * HEADS * HD,
            transcendentals=2 * HEADS * token_count * token_count,
        ),
        compiler_params=pltpu.CompilerParams(vmem_limit_bytes=8 * 2**20),
    )(numbers, own, key_before, value_before, ids, gates)
    near[z_both | x_bit] = hop(near[z_both], "dp", dp_size, x_bit)
    (
        near[z_near | x_bit],
        near[z_far | x_bit],
        between,
        attended,
    ) = lax.optimization_barrier(
        (near[z_near | x_bit], near[z_far | x_bit], near[z_both], attended)
    )
    far = {}
    for bit in (0, z_far, z_near, x_bit, z_near | x_bit, z_far | x_bit, z_both | x_bit):
        far[bit] = hop(near[bit], "dp", dp_size, 1)
    far[z_both] = hop(between, "dp", dp_size, 1)
    late_bits = (z_far | x_bit, z_both | x_bit)
    early_bits = tuple(bit for bit in near if bit not in late_bits)
    early_chips = [bit >> 1 for bit in early_bits]
    late_chips = [bit >> 1 for bit in late_bits]
    early = pl.pallas_call(
        functools.partial(early_kernel, early_chips),
        out_shape=jax.ShapeDtypeStruct((token_count, width), jnp.float32),
        in_specs=vmem(1 + 2 * len(early_bits)),
        out_specs=vmem(1)[0],
        cost_estimate=pl.CostEstimate(
            flops=4 * 2 * token_count * HEADS * HD * width,
            bytes_accessed=2 * HEADS * HD * width,
            transcendentals=0,
        ),
        compiler_params=pltpu.CompilerParams(vmem_limit_bytes=16 * 2**20),
    )(attended, *[near[bit] for bit in early_bits], *[far[bit] for bit in early_bits])
    gate_up_near = jnp.swapaxes(w_gate_up[0], 1, 2)

    some_rows = jax.ShapeDtypeStruct((CAP, width), jnp.bfloat16)
    all_rows = jax.ShapeDtypeStruct((token_count, width), jnp.bfloat16)
    attn_proj, kept, sent, second, last, expert_sum = pl.pallas_call(
        functools.partial(project_kernel, late_chips),
        out_shape=(all_rows, some_rows, some_rows, some_rows, some_rows, all_rows),
        in_specs=smem(1) + vmem(5 + 2 * len(late_bits)),
        out_specs=tuple(vmem(4) + [pl.BlockSpec(memory_space=pl.ANY)] * 2),
        scratch_shapes=[pltpu.VMEM((token_count, width), jnp.float32)],
        cost_estimate=pl.CostEstimate(
            flops=2 * token_count * HEADS * HD * width,
            bytes_accessed=2 * HEADS * HD * width,
            transcendentals=0,
        ),
        compiler_params=pltpu.CompilerParams(vmem_limit_bytes=16 * 2**20),
    )(
        info,
        attended,
        residual[0],
        norm_gain[None],
        select,
        early,
        *[near[bit] for bit in late_bits],
        *[far[bit] for bit in late_bits],
    )

    units = w_down.shape[1]
    row_count = dp_size * CAP

    def dispatch(bit):
        rest = [b for b in bits if b != bit]

        def run(kept, sent):
            gate_up_far = hop(gate_up_near, "dp", dp_size, 1)
            down_far = hop(w_down[0], "dp", dp_size, 1)
            rows = gather_rows(kept, sent, bit, rest, dp_size)
            return rows, gate_up_far, down_far

        return run

    def give_back(bit):
        rest = [b for b in bits if b != bit]

        def run(made, masks):
            return scatter_rows(made, bit, rest, dp_size, masks)

        return run

    branch = info[BRANCH]

    def one_pass(step, carried):
        kept, sent, last, _ = carried
        rows, gate_up_far, down_far = lax.switch(
            branch, [dispatch(bit) for bit in bits], kept, sent
        )
        made, masks = pl.pallas_call(
            expert_kernel,
            out_shape=(
                jax.ShapeDtypeStruct((row_count, width), jnp.bfloat16),
                jax.ShapeDtypeStruct((PASS_COUNT, 1, width), jnp.float32),
            ),
            in_specs=smem(2) + vmem(1) + [pl.BlockSpec(memory_space=pltpu.HBM)] * 4,
            out_specs=tuple(vmem(2)),
            scratch_shapes=[
                pltpu.VMEM((2, units, width), jnp.bfloat16),
                pltpu.VMEM((units, width), jnp.bfloat16),
                pltpu.VMEM((2 * units, row_count), jnp.float32),
                pltpu.VMEM((row_count, units), jnp.bfloat16),
                pltpu.SemaphoreType.DMA((width // 512 + 1,)),
            ],
            cost_estimate=pl.CostEstimate(
                flops=6 * row_count * units * width,
                bytes_accessed=6 * units * width,
                transcendentals=row_count * units,
            ),
            compiler_params=pltpu.CompilerParams(vmem_limit_bytes=26 * 2**20),
        )(info, step[None], rows, gate_up_near, gate_up_far, w_down[0], down_far)
        own, other = lax.switch(branch, [give_back(bit) for bit in bits], made, masks)
        expert_sum, last, kept, sent = pl.pallas_call(
            combine_kernel,
            out_shape=(all_rows, some_rows, some_rows, some_rows),
            in_specs=smem(2) + vmem(6),
            out_specs=tuple(vmem(4)),
            compiler_params=pltpu.CompilerParams(vmem_limit_bytes=8 * 2**20),
        )(info, step[None], own, other, last, second, select, gate_values)
        return kept, sent, last, expert_sum

    carried = (kept, sent, last, expert_sum)
    expert_sum = lax.fori_loop(0, info[PASSES], one_pass, carried)[3]
    return (attn_proj[None], expert_sum[None])


def solution(mesh):
    placed = (
        P("dp", "ctx", None),
        P("dp", "ctx", None),
        P("dp", "ctx", None),
        P("dp", "ctx", None),
        P("dp", None),
        P(),
        P("dp", None, None, "ctx"),
        P("dp", "ctx", None),
        P("dp", "ctx", None),
        P("dp", "ctx", None),
        P("dp", "ctx", None),
        P(),
    )
    dp_size, ctx_size = mesh.shape["dp"], mesh.shape["ctx"]
    small = ctx_size == 2 and dp_size == 2 * HEADS
    return jax.shard_map(
        body_move_rows if small else body_move_weights,
        mesh=mesh,
        in_specs=placed,
        out_specs=(P("dp", "ctx", None), P("dp", "ctx", None)),
        check_vma=False,
    )
```

```python
import functools

import jax
import jax.numpy as jnp
from jax import lax
from jax.experimental import pallas as pl
from jax.experimental.pallas import tpu as pltpu
from jax.sharding import PartitionSpec as P

HEADS = 8
HD = 128
PASS_SPECIALISTS = 2
CAP = 24


EPSILON = 1e-06
LOWEST = -1e30


def broadcast(array, axis, root):
    mine = lax.axis_index(axis) == root
    return lax.psum(jnp.where(mine, array, jnp.zeros_like(array)), axis)


def hop(array, axis, size, bit):
    return lax.ppermute(array, axis, [(i, i ^ bit) for i in range(size)])


def route_slots(expert_ids, route_gates, capacity, expert):
    matches = expert_ids == expert
    routed = jnp.any(matches, axis=1)
    gate_value = jnp.sum(jnp.where(matches, route_gates, 0.0), axis=1)
    slot_rank = jnp.cumsum(routed.astype(jnp.int32)) - 1
    kept_mask = routed & (slot_rank < capacity[expert])
    return (slot_rank, kept_mask, gate_value)


def attend(queries, key_block, value_block, visible):
    width = key_block.shape[0]
    token_count = queries.shape[0]
    query_heads = queries.reshape(token_count, HEADS, HD)
    key_heads = key_block.reshape(width, HEADS, HD)
    value_heads = value_block.reshape(width, HEADS, HD)
    gating_logits = jnp.einsum(
        "qhd,khd->qhk", query_heads, key_heads, preferred_element_type=jnp.float32
    ) * HD ** (-0.5)
    gating_logits = jnp.where(visible[:, None, :], gating_logits, -jnp.inf)
    row_top = jnp.max(gating_logits, axis=-1)
    weights = jnp.exp(gating_logits - row_top[:, :, None])
    denominator = jnp.sum(weights, axis=-1)
    weighted = jnp.einsum(
        "qhk,khd->qhd",
        weights.astype(jnp.bfloat16),
        value_heads,
        preferred_element_type=jnp.float32,
    )
    attended = (weighted / denominator[:, :, None]).astype(jnp.bfloat16)
    return attended.reshape(token_count, HEADS * HD)


def feed_forward(rows, gate_up, down_part):
    gate_proj = jnp.dot(rows, gate_up[0], preferred_element_type=jnp.float32)
    up_proj = jnp.dot(rows, gate_up[1], preferred_element_type=jnp.float32)
    hidden = (jax.nn.silu(gate_proj) * up_proj).astype(jnp.bfloat16)
    return jnp.dot(hidden, down_part, preferred_element_type=jnp.float32).astype(jnp.bfloat16)


def normalise(attn_proj, residual, norm_gain):
    combined = residual.astype(jnp.float32) + attn_proj.astype(jnp.float32)
    return (
        combined
        * lax.rsqrt(jnp.mean(combined * combined, axis=-1, keepdims=True) + EPSILON)
        * norm_gain
    ).astype(jnp.bfloat16)


def pick_rows(routing, normed):
    slot_ids = jnp.arange(CAP)
    select = [
        (slot_rank[None, :] == slot_ids[:, None]) & kept_mask[None, :]
        for slot_rank, kept_mask, _ in routing
    ]
    select = jnp.concatenate(select, axis=0).astype(jnp.bfloat16)
    chosen = jnp.dot(select, normed, preferred_element_type=jnp.float32).astype(jnp.bfloat16)
    return chosen.reshape(PASS_SPECIALISTS, CAP, normed.shape[1])


def combine_rows(routing, produced):
    slot_ids = jnp.arange(CAP)
    summed = 0.0
    for expert in range(PASS_SPECIALISTS):
        slot_rank, kept_mask, gate_value = routing[expert]
        place = ((slot_rank[:, None] == slot_ids[None, :]) & kept_mask[:, None]).astype(
            jnp.bfloat16
        )
        picked = jnp.dot(place, produced[expert], preferred_element_type=jnp.float32)
        summed = summed + gate_value[:, None] * picked
    return summed.astype(jnp.bfloat16)


def body_move_weights(
    query_vecs,
    key_vecs,
    value_vecs,
    residual,
    w_out,
    norm_gain,
    w_gate_up,
    w_down,
    expert_ids,
    route_gates,
    capacity,
    expert_owner,
):
    token_count = query_vecs.shape[1]
    weights_in = []
    for expert in range(PASS_SPECIALISTS):
        weights_in.append(
            (
                broadcast(w_gate_up[0], "dp", expert_owner[expert]),
                broadcast(w_down[0], "dp", expert_owner[expert]),
            )
        )
    keys = lax.all_gather(key_vecs[0], "ctx", axis=0, tiled=True)
    values = lax.all_gather(value_vecs[0], "ctx", axis=0, tiled=True)
    first_row = lax.axis_index("ctx") * token_count
    query_pos = first_row + jnp.arange(token_count)
    visible = jnp.arange(keys.shape[0])[None, :] <= query_pos[:, None]
    attended = attend(query_vecs[0], keys, values, visible)
    projected = jnp.dot(
        attended,
        lax.all_gather(w_out, "dp", axis=0, tiled=True),
        preferred_element_type=jnp.float32,
    )
    attn_proj = projected.astype(jnp.bfloat16)
    normed = normalise(attn_proj, residual[0], norm_gain)
    routing = [
        route_slots(expert_ids[0], route_gates[0], capacity[0, 0], expert)
        for expert in range(PASS_SPECIALISTS)
    ]
    chosen = pick_rows(routing, normed)
    routed_rows = lax.all_gather(jnp.swapaxes(chosen, 0, 1), "ctx", axis=0, tiled=True)
    outputs = [
        feed_forward(routed_rows[:, expert], *weights_in[expert])
        for expert in range(PASS_SPECIALISTS)
    ]
    expert_out = lax.psum_scatter(
        jnp.stack(outputs, axis=1), "ctx", scatter_dimension=0, tiled=True
    )
    expert_sum = combine_rows(routing, [expert_out[:, e] for e in range(PASS_SPECIALISTS)])
    return (attn_proj[None], expert_sum[None])


CTX, CHIP, CORE, FIRST, FIRST_CAP, SECOND, SECOND_CAP, SAME = range(8)
FIRST_HERE, SECOND_HERE, PASSES, BRANCH, PASS_INFO = range(8, 13)
USE_FAR, NEAR_LAST, NEAR_SECOND, OTHER_NEAR, PASS_COUNT = range(5)


def work_out_places(bits, numbers, info):
    owners = [numbers[k] for k in range(PASS_SPECIALISTS)]
    caps = [numbers[PASS_SPECIALISTS + k] for k in range(PASS_SPECIALISTS)]
    me = lax.axis_index("dp")
    differ = owners[0] ^ owners[1]
    branch = 0
    split_bit = 0
    rest = [bits[1], bits[2]]
    for k in reversed(range(len(bits))):
        parted = (differ & bits[k]) != 0
        branch = jnp.where(parted, k, branch)
        split_bit = jnp.where(parted, bits[k], split_bit)
        others = [bit for bit in bits if bit != bits[k]]
        rest = [jnp.where(parted, others[i], rest[i]) for i in range(2)]
    same = split_bit == 0
    swapped = ((me ^ owners[0]) & split_bit) != 0
    first_offset = me ^ jnp.where(swapped, owners[1], owners[0])
    second_offset = me ^ jnp.where(swapped, owners[0], owners[1])

    def put(place, value):
        info[place] = value.astype(jnp.int32)

    put(CTX, lax.axis_index("ctx"))
    put(CHIP, me >> 1)
    put(CORE, me & 1)
    put(FIRST, jnp.where(swapped, 1, 0))
    put(FIRST_CAP, jnp.where(swapped, caps[1], caps[0]))
    put(SECOND, jnp.where(swapped, 0, 1))
    put(SECOND_CAP, jnp.where(swapped, caps[0], caps[1]))
    put(SAME, jnp.where(same, 1, 0))
    put(FIRST_HERE, jnp.where((first_offset & bits[0]) == 0, 1, 0))
    put(SECOND_HERE, jnp.where((second_offset & bits[0]) == 0, 1, 0))
    put(PASSES, jnp.where(same, 2, 1))
    put(BRANCH, branch)
    pairs = (
        (first_offset, jnp.where(same, first_offset, second_offset)),
        (second_offset, second_offset),
    )
    for k, (offset, other_offset) in enumerate(pairs):
        base = PASS_INFO + k * PASS_COUNT
        put(base + USE_FAR, offset & 1)
        put(base + NEAR_LAST, jnp.where((offset & rest[1]) == 0, 1, 0))
        put(base + NEAR_SECOND, jnp.where((offset & rest[0]) == 0, 1, 0))
        put(base + OTHER_NEAR, jnp.where((other_offset & rest[0]) == 0, 1, 0))


def attend_kernel(bits, numbers, own_vecs, key_before, value_before, ids, gates, *outs):
    attended, select, gate_values, info = outs
    query, key, value = (own_vecs.at[k] for k in range(3))
    work_out_places(bits, numbers, info)
    token_count = query.shape[0]
    row = lax.broadcasted_iota(jnp.int32, (token_count, token_count), 0)
    col = lax.broadcasted_iota(jnp.int32, (token_count, token_count), 1)
    own_visible = col <= row
    before_visible = jnp.broadcast_to(info[CTX], (token_count, token_count)) == 1
    contract_last = (((1,), (1,)), ((), ()))
    for head in range(HEADS):
        span = slice(head * HD, (head + 1) * HD)
        heads = query[:, span]
        own = lax.dot_general(
            heads, key[:, span], contract_last, preferred_element_type=jnp.float32
        )
        before = lax.dot_general(
            heads, key_before[:, span], contract_last, preferred_element_type=jnp.float32
        )
        own = jnp.where(own_visible, own * HD ** (-0.5), -jnp.inf)
        before = jnp.where(before_visible, before * HD ** (-0.5), -jnp.inf)
        top = jnp.maximum(
            jnp.max(own, axis=1, keepdims=True), jnp.max(before, axis=1, keepdims=True)
        )
        own = jnp.exp(own - top)
        before = jnp.exp(before - top)
        total = jnp.sum(own, axis=1, keepdims=True) + jnp.sum(before, axis=1, keepdims=True)
        mixed = jnp.dot(
            own.astype(jnp.bfloat16), value[:, span], preferred_element_type=jnp.float32
        ) + jnp.dot(
            before.astype(jnp.bfloat16), value_before[:, span], preferred_element_type=jnp.float32
        )
        mixed = mixed / total
        swapped = pltpu.roll(mixed, HD // 2, 1)
        mixed = jnp.where(jnp.broadcast_to(info[CORE], mixed.shape) == 0, mixed, swapped)
        attended[head ^ info[CHIP]] = mixed.astype(jnp.bfloat16)

    slot = lax.broadcasted_iota(jnp.int32, (CAP, token_count), 0)
    earlier = (row < col).astype(jnp.bfloat16)
    for k in range(PASS_SPECIALISTS):
        matches = ids[...] == info[FIRST + 2 * k]
        named = jnp.max(matches.astype(jnp.float32), axis=0, keepdims=True)
        gate_row = jnp.sum(jnp.where(matches, gates[...], 0.0), axis=0, keepdims=True)
        gate_values[:, k : k + 1] = jnp.sum(
            jnp.where(row == col, jnp.broadcast_to(gate_row, row.shape), 0.0),
            axis=1,
            keepdims=True,
        )
        routed = jnp.broadcast_to(named, (CAP, token_count))
        rank = jnp.dot(
            routed.astype(jnp.bfloat16), earlier, preferred_element_type=jnp.float32
        ).astype(jnp.int32)
        kept = (routed > 0.0) & (rank == slot) & (rank < info[FIRST_CAP + 2 * k])
        select[k] = kept.astype(jnp.bfloat16)


def add_products(attended, chips, near, far, span, total):
    for pair in range(0, len(chips), 2):
        one, two = chips[pair], chips[pair + 1]
        left = jnp.concatenate([attended[one], attended[two]], axis=1)
        right = jnp.concatenate(
            [near[pair][:, span], far[pair][:, span]]
            + [near[pair + 1][:, span], far[pair + 1][:, span]],
            axis=0,
        )
        product = jnp.dot(left, right, preferred_element_type=jnp.float32)
        total = product if total is None else total + product
    return total


def early_kernel(chips, attended, *refs):
    near, far = refs[: len(chips)], refs[len(chips) : -1]
    total = refs[-1]
    for start in range(0, total.shape[1], 512):
        span = slice(start, start + 512)
        total[:, span] = add_products(attended, chips, near, far, span, None)


def project_kernel(chips, info, attended, residual, gain, select, early, *refs):
    near, far = refs[: len(chips)], refs[len(chips) : 2 * len(chips)]
    attn_proj, kept, sent, second, _, _, combined = refs[-7:]
    token_count, width = residual.shape
    tile = 512
    squares = jnp.zeros((token_count, 1), jnp.float32)
    for start in range(0, width, tile):
        span = slice(start, start + tile)
        total = add_products(attended, chips, near, far, span, early[:, span])
        rounded = total.astype(jnp.bfloat16)
        attn_proj[:, span] = rounded
        added = residual[:, span].astype(jnp.float32) + rounded.astype(jnp.float32)
        combined[:, span] = added
        squares = squares + jnp.sum(added * added, axis=1, keepdims=True)
    scale = lax.rsqrt(squares / width + EPSILON)
    for start in range(0, width, tile):
        span = slice(start, start + tile)
        normed = (combined[:, span] * scale * gain[:, span]).astype(jnp.bfloat16)
        rows = [
            jnp.dot(select[k], normed, preferred_element_type=jnp.float32)
            for k in range(PASS_SPECIALISTS)
        ]
        kept[:, span] = rows[0].astype(jnp.bfloat16)
        second[:, span] = rows[1].astype(jnp.bfloat16)
        use_first = jnp.broadcast_to(info[SAME], rows[0].shape) != 0
        sent[:, span] = jnp.where(use_first, rows[0], rows[1]).astype(jnp.bfloat16)


def combine_kernel(info, step, own, other, last, second, select, gate_values, *outs):
    out, next_last, next_kept, next_sent = outs
    same = info[SAME] != 0
    contract_first = (((0,), (0,)), ((), ()))

    def add_up(first_rows, second_rows):
        total = 0.0
        for k, rows in enumerate((first_rows, second_rows)):
            picked = lax.dot_general(
                select[k], rows, contract_first, preferred_element_type=jnp.float32
            )
            total = total + gate_values[:, k : k + 1] * picked
        return total.astype(jnp.bfloat16)

    @pl.when(jnp.logical_not(same))
    def _():
        for start in range(0, own.shape[1], 512):
            span = slice(start, start + 512)
            out[:, span] = add_up(own[:, span], other[:, span])

    @pl.when(same)
    def _():
        here = jnp.where(step[0] == 0, info[FIRST_HERE], info[SECOND_HERE])
        for start in range(0, own.shape[1], 512):
            span = slice(start, start + 512)
            use_own = jnp.broadcast_to(here, (own.shape[0], 512)) != 0
            served = jnp.where(
                use_own, own[:, span].astype(jnp.float32), other[:, span].astype(jnp.float32)
            ).astype(jnp.bfloat16)
            out[:, span] = add_up(last[:, span], served)
            next_last[:, span] = served
            next_kept[:, span] = second[:, span]
            next_sent[:, span] = second[:, span]


def expert_kernel(
    info,
    step,
    rows,
    gate_up_near,
    gate_up_far,
    down_near,
    down_far,
    made,
    masks,
    gate_up,
    down,
    sums,
    hidden,
    sems,
):
    units, width = down.shape
    piece = 512
    starts = list(range(0, width, piece))

    def copies(gate_up_from, down_from):
        spans = [pl.ds(start, piece) for start in starts]
        out = [
            pltpu.make_async_copy(gate_up_from.at[:, :, span], gate_up.at[:, :, span], sems.at[k])
            for k, span in enumerate(spans)
        ]
        return out + [pltpu.make_async_copy(down_from, down, sems.at[len(starts)])]

    base = PASS_INFO + PASS_COUNT * step[0]
    use_far = info[base + USE_FAR]

    def start_copy(stage):
        @pl.when(use_far == 0)
        def _():
            copies(gate_up_near, down_near)[stage].start()

        @pl.when(use_far != 0)
        def _():
            copies(gate_up_far, down_far)[stage].start()

    start_copy(0)
    start_copy(1)
    for k in (NEAR_LAST, NEAR_SECOND, OTHER_NEAR):
        masks[k] = jnp.broadcast_to(info[base + k].astype(jnp.float32), masks.shape[1:])

    arrived = copies(gate_up_near, down_near)
    contract_last = (((1,), (1,)), ((), ()))
    for k, start in enumerate(starts):
        span = slice(start, start + piece)
        arrived[k].wait()
        if k + 2 < len(arrived):
            start_copy(k + 2)
        product = lax.dot_general(
            gate_up[:, :, span].reshape(2 * units, piece),
            rows[:, span],
            contract_last,
            preferred_element_type=jnp.float32,
        )
        if k == 0:
            sums[...] = product
        else:
            sums[...] += product
    for start in range(0, units, 256):
        stop = min(start + 256, units)
        gate_proj, up_proj = sums[start:stop], sums[units + start : units + stop]
        made_hidden = gate_proj / (1.0 + jnp.exp(-gate_proj)) * up_proj
        hidden[:, start:stop] = jnp.transpose(made_hidden).astype(jnp.bfloat16)
    arrived[-1].wait()
    for start in range(0, width, 512):
        span = slice(start, start + 512)
        made[:, span] = jnp.dot(
            hidden[...], down[:, span], preferred_element_type=jnp.float32
        ).astype(jnp.bfloat16)


def gather_rows(kept, sent, first, bits, dp_size):
    second, last = bits

    beside = hop(kept, "dp", dp_size, second)
    across = hop(sent, "dp", dp_size, first)
    beyond = hop(sent, "dp", dp_size, first | second)
    unit = jnp.concatenate([kept, beside, across, beyond], axis=0)
    half = unit.shape[1] // 2
    left, right = unit[:, :half], unit[:, half:]
    left = jnp.stack([left, hop(left, "dp", dp_size, last)])
    right = jnp.stack([right, hop(right, "ctx", 2, 1)])
    left = jnp.stack([left, hop(left, "ctx", 2, 1)])
    right = jnp.stack([right, hop(right, "dp", dp_size, last)], axis=1)
    rows = jnp.concatenate([left, right], axis=-1)
    return rows.reshape(-1, rows.shape[-1])


def scatter_rows(rows, first, bits, dp_size, masks):
    second, last = bits
    half = rows.shape[1] // 2
    rows = rows.reshape(2, 2, -1, rows.shape[1])
    left, right = rows[..., :half], rows[..., half:]

    def add(kept, came):
        return (kept.astype(jnp.float32) + came.astype(jnp.float32)).astype(jnp.bfloat16)

    left = add(left[0], hop(left[1], "ctx", 2, 1))
    right = jnp.where(masks[NEAR_LAST, :, half:] != 0, right[:, 0], hop(right[:, 1], "dp", dp_size, last))
    left = jnp.where(masks[NEAR_LAST, :, :half] != 0, left[0], hop(left[1], "dp", dp_size, last))
    right = add(right[0], hop(right[1], "ctx", 2, 1))
    unit = jnp.concatenate([left, right], axis=-1)
    here, beside, across, beyond = lax.optimization_barrier(jnp.split(unit, 4, axis=0))

    across = hop(across, "dp", dp_size, first)
    beside = hop(beside, "dp", dp_size, second)
    beyond = hop(beyond, "dp", dp_size, first | second)
    return (
        jnp.where(masks[NEAR_SECOND] != 0, here, beside),
        jnp.where(masks[OTHER_NEAR] != 0, across, beyond),
    )


def smem(count):
    return [pl.BlockSpec(memory_space=pltpu.SMEM)] * count


def vmem(count):
    return [pl.BlockSpec(memory_space=pltpu.VMEM)] * count


def body_move_rows(
    query_vecs,
    key_vecs,
    value_vecs,
    residual,
    w_out,
    norm_gain,
    w_gate_up,
    w_down,
    expert_ids,
    route_gates,
    capacity,
    expert_owner,
):
    token_count = query_vecs.shape[1]
    width = residual.shape[2]
    dp_size = lax.axis_size("dp")
    bits = [1 << k for k in reversed(range(1, dp_size.bit_length() - 1))]

    z_far, z_near, x_bit = bits
    z_both = z_far | z_near
    near = {0: w_out}
    for bit in (z_far, z_near, x_bit):
        near[bit] = hop(w_out, "dp", dp_size, bit)
    key_before = lax.ppermute(key_vecs[0], "ctx", [(0, 1)])
    value_before = lax.ppermute(value_vecs[0], "ctx", [(0, 1)])
    own = jnp.stack([query_vecs[0], key_vecs[0], value_vecs[0]])
    numbers = jnp.concatenate([expert_owner[:PASS_SPECIALISTS], capacity[0, 0]])
    (
        near[z_far],
        near[z_near],
        near[x_bit],
        near[0],
        key_before,
        own,
        numbers,
        ids,
        gates,
    ) = lax.optimization_barrier(
        (
            near[z_far],
            near[z_near],
            near[x_bit],
            near[0],
            key_before,
            own,
            numbers,
            jnp.transpose(expert_ids[0]),
            jnp.transpose(route_gates[0]),
        )
    )
    near[z_near | x_bit] = hop(near[z_near], "dp", dp_size, x_bit)
    near[z_both] = hop(near[z_far], "dp", dp_size, z_near)
    near[z_far | x_bit] = hop(near[z_far], "dp", dp_size, x_bit)
    value_before, near[z_both] = lax.optimization_barrier((value_before, near[z_both]))
    attended, select, gate_values, info = pl.pallas_call(
        functools.partial(attend_kernel, bits),
        out_shape=(
            jax.ShapeDtypeStruct((HEADS, token_count, HD), jnp.bfloat16),
            jax.ShapeDtypeStruct((PASS_SPECIALISTS, CAP, token_count), jnp.bfloat16),
            jax.ShapeDtypeStruct((token_count, PASS_SPECIALISTS), jnp.float32),
            jax.ShapeDtypeStruct((PASS_INFO + 2 * PASS_COUNT,), jnp.int32),
        ),
        in_specs=smem(1) + vmem(5),
        out_specs=tuple(vmem(3) + smem(1)),
        cost_estimate=pl.CostEstimate(
            flops=64 * HEADS * HD * 2 * token_count * token_count,
            bytes_accessed=6 * 2 * token_count * HEADS * HD,
            transcendentals=2 * HEADS * token_count * token_count,
        ),
        compiler_params=pltpu.CompilerParams(vmem_limit_bytes=8 * 2**20),
    )(numbers, own, key_before, value_before, ids, gates)
    near[z_both | x_bit] = hop(near[z_both], "dp", dp_size, x_bit)
    (
        near[z_near | x_bit],
        near[z_far | x_bit],
        between,
        attended,
    ) = lax.optimization_barrier(
        (near[z_near | x_bit], near[z_far | x_bit], near[z_both], attended)
    )
    near[z_both | x_bit], select = lax.optimization_barrier((near[z_both | x_bit], select))
    far = {}
    for bit in (0, z_far, z_near, x_bit, z_near | x_bit, z_far | x_bit, z_both | x_bit):
        far[bit] = hop(near[bit], "dp", dp_size, 1)
    far[z_both] = hop(between, "dp", dp_size, 1)
    late_bits = (z_far | x_bit, z_both | x_bit)
    early_bits = tuple(bit for bit in near if bit not in late_bits)
    early_chips = [bit >> 1 for bit in early_bits]
    late_chips = [bit >> 1 for bit in late_bits]
    early = pl.pallas_call(
        functools.partial(early_kernel, early_chips),
        out_shape=jax.ShapeDtypeStruct((token_count, width), jnp.float32),
        in_specs=vmem(1 + 2 * len(early_bits)),
        out_specs=vmem(1)[0],
        cost_estimate=pl.CostEstimate(
            flops=4 * 2 * token_count * HEADS * HD * width,
            bytes_accessed=2 * HEADS * HD * width,
            transcendentals=0,
        ),
        compiler_params=pltpu.CompilerParams(vmem_limit_bytes=16 * 2**20),
    )(attended, *[near[bit] for bit in early_bits], *[far[bit] for bit in early_bits])
    gate_up_near = jnp.swapaxes(w_gate_up[0], 1, 2)

    some_rows = jax.ShapeDtypeStruct((CAP, width), jnp.bfloat16)
    all_rows = jax.ShapeDtypeStruct((token_count, width), jnp.bfloat16)
    attn_proj, kept, sent, second, last, expert_sum = pl.pallas_call(
        functools.partial(project_kernel, late_chips),
        out_shape=(all_rows, some_rows, some_rows, some_rows, some_rows, all_rows),
        in_specs=smem(1) + vmem(5 + 2 * len(late_bits)),
        out_specs=tuple(vmem(4) + [pl.BlockSpec(memory_space=pl.ANY)] * 2),
        scratch_shapes=[pltpu.VMEM((token_count, width), jnp.float32)],
        cost_estimate=pl.CostEstimate(
            flops=2 * token_count * HEADS * HD * width,
            bytes_accessed=2 * HEADS * HD * width,
            transcendentals=0,
        ),
        compiler_params=pltpu.CompilerParams(vmem_limit_bytes=16 * 2**20),
    )(
        info,
        attended,
        residual[0],
        norm_gain[None],
        select,
        early,
        *[near[bit] for bit in late_bits],
        *[far[bit] for bit in late_bits],
    )

    units = w_down.shape[1]
    row_count = dp_size * CAP

    def dispatch(bit):
        rest = [b for b in bits if b != bit]

        def run(kept, sent):
            gate_up_far = hop(gate_up_near, "dp", dp_size, 1)
            down_far = hop(w_down[0], "dp", dp_size, 1)
            rows = gather_rows(kept, sent, bit, rest, dp_size)
            return rows, gate_up_far, down_far

        return run

    def give_back(bit):
        rest = [b for b in bits if b != bit]

        def run(made, masks):
            return scatter_rows(made, bit, rest, dp_size, masks)

        return run

    branch = info[BRANCH]

    def one_pass(step, carried):
        kept, sent, last, _ = carried
        rows, gate_up_far, down_far = lax.switch(
            branch, [dispatch(bit) for bit in bits], kept, sent
        )
        made, masks = pl.pallas_call(
            expert_kernel,
            out_shape=(
                jax.ShapeDtypeStruct((row_count, width), jnp.bfloat16),
                jax.ShapeDtypeStruct((PASS_COUNT, 1, width), jnp.float32),
            ),
            in_specs=smem(2) + vmem(1) + [pl.BlockSpec(memory_space=pltpu.HBM)] * 4,
            out_specs=tuple(vmem(2)),
            scratch_shapes=[
                pltpu.VMEM((2, units, width), jnp.bfloat16),
                pltpu.VMEM((units, width), jnp.bfloat16),
                pltpu.VMEM((2 * units, row_count), jnp.float32),
                pltpu.VMEM((row_count, units), jnp.bfloat16),
                pltpu.SemaphoreType.DMA((width // 512 + 1,)),
            ],
            cost_estimate=pl.CostEstimate(
                flops=6 * row_count * units * width,
                bytes_accessed=6 * units * width,
                transcendentals=row_count * units,
            ),
            compiler_params=pltpu.CompilerParams(vmem_limit_bytes=26 * 2**20),
        )(info, step[None], rows, gate_up_near, gate_up_far, w_down[0], down_far)
        own, other = lax.switch(branch, [give_back(bit) for bit in bits], made, masks)
        expert_sum, last, kept, sent = pl.pallas_call(
            combine_kernel,
            out_shape=(all_rows, some_rows, some_rows, some_rows),
            in_specs=smem(2) + vmem(6),
            out_specs=tuple(vmem(4)),
            compiler_params=pltpu.CompilerParams(vmem_limit_bytes=8 * 2**20),
        )(info, step[None], own, other, last, second, select, gate_values)
        return kept, sent, last, expert_sum

    carried = (kept, sent, last, expert_sum)
    expert_sum = lax.fori_loop(0, info[PASSES], one_pass, carried)[3]
    return (attn_proj[None], expert_sum[None])


def solution(mesh):
    placed = (
        P("dp", "ctx", None),
        P("dp", "ctx", None),
        P("dp", "ctx", None),
        P("dp", "ctx", None),
        P("dp", None),
        P(),
        P("dp", None, None, "ctx"),
        P("dp", "ctx", None),
        P("dp", "ctx", None),
        P("dp", "ctx", None),
        P("dp", "ctx", None),
        P(),
    )
    dp_size, ctx_size = mesh.shape["dp"], mesh.shape["ctx"]
    small = ctx_size == 2 and dp_size == 2 * HEADS
    return jax.shard_map(
        body_move_rows if small else body_move_weights,
        mesh=mesh,
        in_specs=placed,
        out_specs=(P("dp", "ctx", None), P("dp", "ctx", None)),
        check_vma=False,
    )
```
